256 devices in a mesh: dp: 4 (over x), expert: 16 (over z, core), etp: 4 (over y).
Axes of the slice: x: 4, y: 4, z: 8, core: 2. Of those that a mesh axis runs over, the one named last changes fastest.
Arguments:
- tokens: bfloat16 [2048, 3072], P(('dp', 'expert')), may hold values from -6 to 6
- out_grad: bfloat16 [2048, 3072], P(('dp', 'expert')), may hold values from -6 to 6
- gates: bfloat16 [2048, 4], P(('dp', 'expert')), may hold values from 0.099609375 to 1
- expert_ids: int32 [2048, 4], P(('dp', 'expert')), may hold values from 0 to 15, all different within a row; in each aligned block of 32 rows (0 to 31, 32 to 63, ...) at most 12 rows name the same one
- w_gate: bfloat16 [16, 5376, 3072], P('expert', ('dp', 'etp')), may hold values from -0.109375 to 0.109375
- w_up: bfloat16 [16, 5376, 3072], P('expert', ('dp', 'etp')), may hold values from -0.109375 to 0.109375
- w_down: bfloat16 [16, 5376, 3072], P('expert', ('dp', 'etp')), may hold values from -0.078125 to 0.078125
Outputs:
- input_grad: bfloat16 [2048, 3072], P(('dp', 'expert'), 'etp')
- gate_grad: float32 [2048, 4], P(('dp', 'expert', 'etp'))
- grad_gate: bfloat16 [16, 5376, 3072], P('expert', ('dp', 'etp'))
- grad_up: bfloat16 [16, 5376, 3072], P('expert', ('dp', 'etp'))
- grad_down: bfloat16 [16, 5376, 3072], P('expert', ('dp', 'etp'))
The draws below stay inside these ranges and needn't reach their ends.
Inputs may be any that keep to these rules, and one draw needn't show every extreme that they name: `expert_ids`: in each aligned block of 32 rows (the tokens of one device along dp and expert) no expert is named by more than 12 rows, a bound that some block reaches. A row names 4 different experts.
All inputs are finite; a program needn't handle non-finite values.
Results may differ from the reference program's by a relative error of at most 0.0049.
Values may be sent and summed in bfloat16 or wider, within the bound.
A program may use at most 128 MiB of HBM per device.

```python
import math
import jax
import jax.numpy as jnp
import numpy as np
from jax import lax

D = 3072
FF = 5376
EXPERTS = 16
TOP = 4
TOK_DEV = 32
CAP = 12
TOKENS = 2048
N_DP = 4
N_EXPERT = 16


def level_of(own_key, extent, shards, low, top_value):
    def one(dim, blocks):
        draws = jax.random.uniform(jax.random.fold_in(jax.random.fold_in(own_key, 6), dim), (blocks,), jnp.float32, low / len(shards), top_value / len(shards))
        return jnp.repeat(jnp.exp(draws), extent[dim] // blocks).reshape((-1,) + (1,) * (len(extent) - dim - 1))

    level = one(*shards[0])
    for cut in shards[1:]:
        level = level * one(*cut)
    return level


def deal_out(key, own, number, rows, number_of, top, reach, skew):
    sequence = jax.random.permutation(key, number_of)
    packed, ordinary = shares(number_of, rows * top, reach, skew, True), shares(number_of, rows * top, reach, skew, False)
    places = jnp.arange(number_of)

    def named(lengths, offset_by):
        used = int((lengths > 0).sum())
        fixed = max(1, used // 4)
        moved = fixed + (places - fixed + offset_by * (used - fixed)) % max(1, number_of - fixed)
        return jnp.zeros((number_of,), jnp.int32).at[sequence[jnp.where(places < fixed, places, moved)]].set(jnp.asarray(lengths, jnp.int32))

    lengths = jnp.where(number % 4 == 0, named(packed, number // 4), named(ordinary, number - number // 4 - 1))
    mixed = jax.random.permutation(jax.random.fold_in(own, 3), number_of)
    donor, sink = mixed[0:number_of // 2 * 2:2], mixed[1:number_of // 2 * 2:2]
    slack = jnp.minimum(lengths[donor] - 1, reach - lengths[sink]) // 2
    slack = jnp.where((donor == sequence[0]) | (sink == sequence[0]) | (lengths[sink] == 0), 0, jnp.maximum(slack, 0))
    moved = jax.random.randint(jax.random.fold_in(own, 4), (number_of // 2,), 0, 1 << 20) % (slack + 1)
    lengths = lengths.at[donor].add(-moved).at[sink].add(moved)
    items = jnp.searchsorted(jnp.cumsum(lengths), jnp.arange(rows * top), side="right").astype(jnp.int32)
    listing = items.reshape(top, rows).T
    listing = listing[jax.random.permutation(jax.random.fold_in(own, 1), rows)]
    offset_by = jax.random.randint(jax.random.fold_in(own, 2), (rows, 1), 0, top)
    return jnp.take_along_axis(listing, (jnp.arange(top)[None, :] + offset_by) % top, axis=1)


def shares(number_of, total, bound, slope, full):
    weights = [(1 << 20) // math.isqrt(grade ** slope) + 1 for grade in range(1, number_of + 1)]
    largest = bound if full else min(bound, max(-(-total // number_of), total * weights[0] // sum(weights)))
    least = 1 if total - largest >= number_of - 1 else 0
    counts, spare = [largest] + [least] * (number_of - 1), total - largest - least * (number_of - 1)
    while spare > 0:
        movable = [i for i in range(1, number_of) if counts[i] < largest] or [i for i in range(1, number_of) if counts[i] < bound]
        mass, budget = sum([weights[i] for i in movable]), spare
        for i in movable:
            more = min(bound - counts[i], max(1, budget * weights[i] // mass), spare)
            counts[i] = counts[i] + more
            spare = spare - more
    return np.array(counts)


def centred(rng, shape, deviation, reach, pieces=(), held_as=jnp.bfloat16):
    values = jax.random.normal(rng, shape, jnp.float32) * deviation
    if len(pieces) > 0:
        values = level_of(rng, shape, pieces, -0.22, 0.18) * values
    return jnp.clip(values, min=-reach, max=reach).astype(held_as)


def setup_inputs(seed: int = 0) -> dict:
    key_list = jax.random.split(jax.random.key(seed), 8)
    tokens = centred(key_list[0], (TOKENS, D), 1.0, 6.0, ((0, 64),))
    out_grad = centred(key_list[1], (TOKENS, D), 1.0, 6.0, ((0, 64),))
    gates = jnp.clip(0.099609375 + 0.9003906 * jax.random.uniform(key_list[2], (TOKENS, TOP), jnp.float32) ** level_of(key_list[2], (TOKENS, TOP), ((0, 64),), -0.2, 0.2), 0.099609375, 1.0).astype(jnp.bfloat16)
    expert_ids_keys = jax.random.split(jax.random.fold_in(key_list[3], 1), TOKENS // TOK_DEV)
    expert_ids_turns = jax.random.permutation(jax.random.fold_in(key_list[3], 3), TOKENS // TOK_DEV)
    expert_ids = jax.vmap(lambda own, number: deal_out(jax.random.fold_in(key_list[3], 2), own, number, TOK_DEV, EXPERTS, TOP, CAP, 2))(expert_ids_keys, expert_ids_turns).reshape((TOKENS, TOP))
    w_gate = centred(key_list[4], (EXPERTS, FF, D), D ** -0.5, 0.109375, ((0, 16), (1, 16)))
    w_up = centred(key_list[5], (EXPERTS, FF, D), D ** -0.5, 0.109375, ((0, 16), (1, 16)))
    w_down = centred(key_list[6], (EXPERTS, FF, D), FF ** -0.5, 0.078125, ((0, 16), (1, 16)))
    return dict(tokens=tokens, out_grad=out_grad, gates=gates, expert_ids=expert_ids, w_gate=w_gate, w_up=w_up, w_down=w_down)


highest = lax.Precision.HIGHEST


def slot_tables(routes):
    blocks, count, choose = routes.shape
    flat = routes.reshape(blocks, count * choose)
    labels = jnp.arange(EXPERTS, dtype=jnp.int32)
    onehot = (flat[:, :, None] == labels).astype(jnp.int32)
    earlier = jnp.cumsum(onehot, axis=1) - onehot
    position = jnp.sum(earlier * onehot, axis=2)
    places = jnp.arange(CAP, dtype=jnp.int32)
    hits = onehot[:, :, :, None] * (position[:, :, None, None] == places).astype(jnp.int32)
    return hits.astype(jnp.float32).reshape(blocks, count, choose, EXPERTS, CAP)


def expert_pass(operands):
    expert_rows, grad_rows, gate_rows, weight_gate, weight_up, weight_down = operands
    row_count = expert_rows.shape[0] * expert_rows.shape[1]
    inputs = expert_rows.reshape(row_count, D)
    cotangent = grad_rows.reshape(row_count, D)
    scales = gate_rows.reshape(row_count).astype(jnp.float32)[:, None]
    pre_gate = jnp.dot(inputs, weight_gate.T, preferred_element_type=jnp.float32)
    pre_up = jnp.dot(inputs, weight_up.T, preferred_element_type=jnp.float32)
    raw_grad = jnp.dot(cotangent, weight_down.T, preferred_element_type=jnp.float32)
    sigmoid_gate = jax.nn.sigmoid(pre_gate)
    activated = pre_gate * sigmoid_gate
    product = activated * pre_up
    gate_terms = jnp.sum(product * raw_grad, axis=1)
    scaled = (scales * product).astype(jnp.bfloat16)
    grad_down = jnp.dot(scaled.T, cotangent, preferred_element_type=jnp.float32).astype(jnp.bfloat16)
    hidden_grad = scales * raw_grad
    grad_pre_gate = (hidden_grad * pre_up * sigmoid_gate * (1.0 + pre_gate * (1.0 - sigmoid_gate))).astype(jnp.bfloat16)
    grad_pre_up = (hidden_grad * activated).astype(jnp.bfloat16)
    grad_gate = jnp.dot(grad_pre_gate.T, inputs, preferred_element_type=jnp.float32).astype(jnp.bfloat16)
    grad_up = jnp.dot(grad_pre_up.T, inputs, preferred_element_type=jnp.float32).astype(jnp.bfloat16)
    slot_grad = jnp.dot(grad_pre_gate, weight_gate, preferred_element_type=jnp.float32)
    slot_grad = slot_grad + jnp.dot(grad_pre_up, weight_up, preferred_element_type=jnp.float32)
    return grad_gate, grad_up, grad_down, slot_grad.reshape(expert_rows.shape), gate_terms.reshape(gate_rows.shape)


def reference(tokens, out_grad, gates, expert_ids, w_gate, w_up, w_down):
    blocks = N_DP * N_EXPERT
    hits = slot_tables(expert_ids.reshape(blocks, TOK_DEV, TOP))
    table = jnp.sum(hits, axis=2)
    gate_slots = jnp.einsum("btkec,btk->ebc", hits, gates.astype(jnp.float32).reshape(blocks, TOK_DEV, TOP), precision=highest).astype(jnp.bfloat16)
    token_rows = jnp.einsum("btec,btd->ebcd", table, tokens.astype(jnp.float32).reshape(blocks, TOK_DEV, D), precision=highest).astype(jnp.bfloat16)
    grad_slots = jnp.einsum("btec,btd->ebcd", table, out_grad.astype(jnp.float32).reshape(blocks, TOK_DEV, D), precision=highest).astype(jnp.bfloat16)
    grad_gate, grad_up, grad_down, slot_grad, gate_terms = lax.map(expert_pass, (token_rows, grad_slots, gate_slots, w_gate, w_up, w_down))
    input_grad = jnp.einsum("btec,ebcd->btd", table, slot_grad, precision=highest).reshape(TOKENS, D).astype(jnp.bfloat16)
    gate_grad = jnp.einsum("btkec,ebc->btk", hits, gate_terms, precision=highest).reshape(TOKENS, TOP)
    return input_grad, gate_grad, grad_gate, grad_up, grad_down
```

```python
import functools

import jax
import jax.numpy as jnp
from jax import lax
from jax.experimental import pallas as pl
from jax.experimental.pallas import tpu as pltpu
from jax.sharding import PartitionSpec as P

EXPERTS = 16
TOP = 4
CAP = 12
PAD = 16
N_DP = 4
N_ETP = 4
ROWS = EXPERTS * CAP
PADDED = EXPERTS * PAD
D = 3072
COLS = D // N_ETP
LANES = 128
MESH = pl.DeviceIdType.MESH
F32 = jnp.float32
BF16 = jnp.bfloat16


def iota(shape, dim):
    return lax.broadcasted_iota(jnp.int32, shape, dim)


def compact_matrix(rows):
    r, k = iota((rows, PADDED), 0), iota((rows, PADDED), 1)
    return jnp.where(((k >> 4) * CAP + (k & 15) == r) & ((k & 15) < CAP), 1.0, 0.0).astype(BF16)


def extra_row(which):
    b, k = iota((EXPERTS, PADDED), 0), iota((EXPERTS, PADDED), 1)
    return jnp.where(k == b * PAD + CAP + which, 1.0, 0.0).astype(BF16)


def lane_spread():
    c, k = iota((LANES, PADDED), 0), iota((LANES, PADDED), 1)
    return jnp.where((k & 15) == c, 1.0, 0.0).astype(BF16)


def block_mask():
    b, k = iota((EXPERTS, PADDED), 0), iota((EXPERTS, PADDED), 1)
    return jnp.where((k >> 4) == b, 1.0, 0.0).astype(F32)


def dot(a, b):
    return jnp.dot(a, b, preferred_element_type=F32)


def dot_t(a, b):
    return lax.dot_general(a, b, (((1,), (1,)), ((), ())), preferred_element_type=F32)


def position():
    return lax.axis_index("dp"), lax.axis_index("expert"), lax.axis_index("etp")


def copy_to(src, dst, send_sem, recv_sem, device):
    return pltpu.make_async_remote_copy(
        src_ref=src, dst_ref=dst, send_sem=send_sem, recv_sem=recv_sem, device_id=device, device_id_type=MESH
    )


def greet(devices):
    barrier = pltpu.get_barrier_semaphore()
    for device in devices:
        pl.semaphore_signal(barrier, inc=1, device_id=device, device_id_type=MESH)
    pl.semaphore_wait(barrier, len(devices))


def piece(ref, i, j):
    return ref.at[i, :, pl.ds(pl.multiple_of(j * COLS, COLS), COLS)]


class PlaneGather:
    COUNT = 22

    def __init__(self, ref, dp_first, send_sems, recv_sems):
        x, e, y = position()
        self.ref, self.dp_first, self.send_sems, self.recv_sems = ref, dp_first, send_sems, recv_sems
        self.e = e
        self.a, self.b = (x, y) if dp_first else (y, x)
        self.sent = []

    def at(self, i, j, half=None):
        i, j = i % 4, j % 4
        view = piece(self.ref, i, j) if self.dp_first else piece(self.ref, j, i)
        if half is not None:
            view = view.at[pl.ds(half * (ROWS // 2), ROWS // 2), :]
        return view

    def device(self, i, j):
        i, j = i % 4, j % 4
        return (i, self.e, j) if self.dp_first else (j, self.e, i)

    def copy(self, view, index, device):
        return copy_to(view, view, self.send_sems.at[index], self.recv_sems.at[index], device)

    def send(self, view, index, device):
        c = self.copy(view, index, device)
        c.start()
        self.sent.append(c)

    def wait(self, view, index):
        self.copy(view, index, self.device(self.a, self.b)).wait_recv()

    def both_second(self, i, slot, half=None):
        view = self.at(i, self.b, half)
        self.send(view, 4 + 2 * slot, self.device(self.a, self.b + 1))
        self.send(view, 5 + 2 * slot, self.device(self.a, self.b - 1))

    def forward_second(self, i, slot):
        self.wait(self.at(i, self.b - 1), 4 + 2 * slot)
        self.send(self.at(i, self.b - 1, 0), 14 + 2 * slot, self.device(self.a, self.b + 1))
        self.wait(self.at(i, self.b + 1), 5 + 2 * slot)
        self.send(self.at(i, self.b + 1, 1), 15 + 2 * slot, self.device(self.a, self.b - 1))

    def steps(self):
        a, b = self.a, self.b

        def own():
            self.send(self.at(a, b), 0, self.device(a + 1, b))
            self.send(self.at(a, b), 1, self.device(a - 1, b))
            self.both_second(a, 0)

        def lower():
            self.wait(self.at(a - 1, b), 0)
            self.send(self.at(a - 1, b, 0), 2, self.device(a + 1, b))
            self.both_second(a - 1, 1)

        def upper():
            self.wait(self.at(a + 1, b), 1)
            self.send(self.at(a + 1, b, 1), 3, self.device(a - 1, b))
            self.both_second(a + 1, 2)

        def opposite():
            self.wait(self.at(a + 2, b, 0), 2)
            self.both_second(a + 2, 3, 0)
            self.wait(self.at(a + 2, b, 1), 3)
            self.both_second(a + 2, 4, 1)

        def opposite_second():
            self.wait(self.at(a + 2, b - 1, 0), 10)
            self.send(self.at(a + 2, b - 1, 0), 20, self.device(a, b + 1))
            self.wait(self.at(a + 2, b + 1, 1), 13)
            self.send(self.at(a + 2, b + 1, 1), 21, self.device(a, b - 1))

        def last():
            self.wait(self.at(a + 2, b + 1, 0), 11)
            self.wait(self.at(a + 2, b - 1, 1), 12)
            for slot, i in enumerate((a, a - 1, a + 1, a + 2)):
                self.wait(self.at(i, b + 2, 0), 14 + 2 * slot)
                self.wait(self.at(i, b + 2, 1), 15 + 2 * slot)

        return [
            own,
            lower,
            upper,
            lambda: self.forward_second(a, 0),
            opposite,
            lambda: self.forward_second(a - 1, 1),
            lambda: self.forward_second(a + 1, 2),
            opposite_second,
            last,
        ]


def gather_kernel(sx, sd, rows, grads, scales, rx, rd, slot_send, slot_recv, x_send, x_recv, d_send, d_recv, g_send, g_recv):
    x, e, y = position()
    peers = [(x, (e + j) % EXPERTS, y) for j in range(1, EXPERTS)]
    peers += [((x + j) % N_DP, e, y) for j in range(1, N_DP)]
    peers += [(x, e, (y + 1) % N_ETP), (x, e, (y + 3) % N_ETP)]
    greet(peers)

    slots = []
    for which, (source, landed) in enumerate(((sx, rx), (sd, rd))):
        for j in range(1, EXPERTS):
            to = (e + j) % EXPERTS
            c = copy_to(source.at[to], landed.at[e], slot_send.at[which, j], slot_recv.at[which, j], (x, to, y))
            c.start()
            slots.append(c)
        landed[e] = source[e]

    def arrive(which):
        source, landed = ((sx, rx), (sd, rd))[which]
        for j in range(1, EXPERTS):
            frm = (e + EXPERTS - j) % EXPERTS
            copy_to(source.at[frm], landed.at[frm], slot_send.at[which, j], slot_recv.at[which, j], (x, e, y)).wait_recv()

    compact = compact_matrix(ROWS)
    columns = pl.ds(pl.multiple_of(y * COLS, COLS), COLS)
    gather_x = PlaneGather(rows, True, x_send, x_recv)
    gather_d = PlaneGather(grads, False, d_send, d_recv)
    steps_x, steps_d = gather_x.steps(), gather_d.steps()

    arrive(0)
    block = rx[...].reshape(PADDED, COLS)
    rows[x, :, columns] = dot(compact, block).astype(BF16)
    steps_x[0]()
    gate = dot(extra_row(0), block[:, :LANES]).astype(BF16)
    gate = jnp.sum(dot(gate, lane_spread()) * block_mask(), axis=0, keepdims=True).astype(BF16)
    gate = dot_t(gate, compact_matrix(PADDED))
    scales[x] = jnp.broadcast_to(gate, (8, PADDED))
    sent = []
    for j in range(1, N_DP):
        c = copy_to(scales.at[x], scales.at[x], g_send.at[j], g_recv.at[j], ((x + j) % N_DP, e, y))
        c.start()
        sent.append(c)

    arrive(1)
    grads[x, :, columns] = dot(compact, rd[...].reshape(PADDED, COLS)).astype(BF16)
    steps_d[0]()
    for one, two in zip(steps_x[1:], steps_d[1:]):
        one()
        two()
    for j in range(1, N_DP):
        frm = (x + N_DP - j) % N_DP
        copy_to(scales.at[frm], scales.at[frm], g_send.at[j], g_recv.at[j], (x, e, y)).wait_recv()
    for c in slots + sent + gather_x.sent + gather_d.sent:
        c.wait_send()


class PlaneReduce:
    def __init__(self, ref, low, dp_first, opp, full, opp2, full2, sems):
        x, e, y = position()
        self.ref, self.low, self.dp_first = ref, low, dp_first
        self.opp, self.full, self.opp2, self.full2 = opp, full, opp2, full2
        self.send_sems, self.recv_sems = sems
        self.e = e
        self.a, self.b = (x, y) if dp_first else (y, x)
        self.sent = []

    def device(self, i, j):
        i, j = i % 4, j % 4
        return (i, self.e, j) if self.dp_first else (j, self.e, i)

    def at(self, i, j, start, size):
        i, j = i % 4, j % 4
        view = piece(self.ref, i, j) if self.dp_first else piece(self.ref, j, i)
        return view.at[pl.ds(self.low + start, size), :]

    def send(self, src, dst, index, device):
        c = copy_to(src, dst, self.send_sems.at[index], self.recv_sems.at[index], device)
        c.start()
        self.sent.append(c)

    def wait(self, dst, index):
        copy_to(dst, dst, self.send_sems.at[index], self.recv_sems.at[index], self.device(self.a, self.b)).wait_recv()

    HALF = ROWS // 2
    QUARTER = ROWS // 4

    def send_opposite(self, j, k):
        a, b, q = self.a, self.b, self.QUARTER
        self.send(self.at(a + 2, j, 0, q), self.opp.at[0, k], 4 * k, self.device(a + 1, b))
        self.send(self.at(a + 2, j, q, q), self.opp.at[1, k], 4 * k + 1, self.device(a - 1, b))

    def send_near(self, j, k):
        a, b, q, h = self.a, self.b, self.QUARTER, self.HALF
        for side, to in ((0, a + 1), (1, a - 1)):
            self.wait(self.opp.at[side, k], 4 * k + side)
            view = self.at(to, j, side * q, q)
            view[...] = (view[...].astype(F32) + self.opp[side, k].astype(F32)).astype(BF16)
            self.send(self.at(to, j, 0, h), self.full.at[side, k], 4 * k + 2 + side, self.device(to, b))

    def total(self, j, k):
        for side in range(2):
            self.wait(self.full.at[side, k], 4 * k + 2 + side)
        own = self.at(self.a, j, 0, self.HALF)[...].astype(F32)
        return own + self.full[0, k].astype(F32) + self.full[1, k].astype(F32)

    def steps(self):
        a, b, q, h = self.a, self.b, self.QUARTER, self.HALF
        order = (b + 2, b + 1, b - 1, b)
        second = 16

        def keep(k):
            view = self.at(a, order[k], 0, h)
            view[...] = self.total(order[k], k).astype(BF16)

        def second_opposite():
            keep(0)
            self.send(self.at(a, b + 2, 0, q), self.opp2.at[0], second, self.device(a, b + 1))
            self.send(self.at(a, b + 2, q, q), self.opp2.at[1], second + 1, self.device(a, b - 1))

        def second_near(side):
            to = b + 1 if side == 0 else b - 1
            keep(1 + side)
            self.wait(self.opp2.at[side], second + side)
            view = self.at(a, to, side * q, q)
            view[...] = (view[...].astype(F32) + self.opp2[side].astype(F32)).astype(BF16)
            self.send(self.at(a, to, 0, h), self.full2.at[side], second + 2 + side, self.device(a, to))

        def finish():
            value = self.total(b, 3)
            for side in range(2):
                self.wait(self.full2.at[side], second + 2 + side)
            return value + self.full2[0].astype(F32) + self.full2[1].astype(F32)

        steps = [functools.partial(self.send_opposite, order[k], k) for k in range(4)]
        steps += [functools.partial(self.send_near, order[k], k) for k in range(4)]
        steps += [second_opposite, lambda: second_near(0), lambda: second_near(1), finish]
        return steps


def return_kernel(slots_in, terms_in, table, out, terms_out, slots, terms, landed_x, landed_y,
                  opp_a, full_a, opp2_a, full2_a, opp_b, full_b, opp2_b, full2_b, ready, back,
                  send_a, recv_a, send_b, recv_b, t_send, t_recv, r_send, r_recv, local):
    x, e, y = position()
    load = pltpu.make_async_copy(slots_in, slots, local)
    load.start()
    terms[...] = terms_in[...]
    peers = [(x, (e + j) % EXPERTS, y) for j in range(1, EXPERTS)]
    peers += [((x + j) % N_DP, e, y) for j in range(1, N_DP)]
    peers += [(x, e, (y + j) % N_ETP) for j in range(1, N_ETP)]
    greet(peers)
    load.wait()

    one = PlaneReduce(slots, 0, True, opp_a, full_a, opp2_a, full2_a, (send_a, recv_a))
    two = PlaneReduce(slots, ROWS // 2, False, opp_b, full_b, opp2_b, full2_b, (send_b, recv_b))
    steps = list(zip(one.steps(), two.steps()))
    for first, second in steps[:4]:
        first()
        second()
    sent = []
    for j in range(1, N_DP):
        to = (x + j) % N_DP
        c = copy_to(terms.at[to], landed_x.at[j], t_send.at[j], t_recv.at[j], (to, e, y))
        c.start()
        sent.append(c)
    for first, second in steps[4:8]:
        first()
        second()
    total = terms[x]
    for j in range(1, N_DP):
        copy_to(landed_x.at[j], landed_x.at[j], t_send.at[j], t_recv.at[j], (x, e, y)).wait_recv()
        total = total + landed_x[j]
    landed_y[0] = total
    for j in range(1, N_ETP):
        c = copy_to(landed_y.at[0], landed_y.at[j], t_send.at[3 + j], t_recv.at[3 + j], (x, e, (y + j) % N_ETP))
        c.start()
        sent.append(c)
    for first, second in steps[8:11]:
        first()
        second()
    for j in range(1, N_ETP):
        copy_to(landed_y.at[j], landed_y.at[j], t_send.at[3 + j], t_recv.at[3 + j], (x, e, y)).wait_recv()
        total = total + landed_y[j]

    value = total[:1]
    spread, mask = lane_spread(), block_mask()
    widen = compact_matrix(PADDED)
    spare = jnp.zeros((PADDED, LANES), F32)
    for which in range(3):
        part = value.astype(BF16)
        value = value - part.astype(F32)
        part = (dot(part, widen) * mask).astype(BF16)
        part = dot_t(part, spread).astype(BF16)
        spare = spare + lax.dot_general(
            extra_row(which), part, (((0,), (0,)), ((), ())), preferred_element_type=F32
        )
    summed = jnp.concatenate([steps[11][0](), steps[11][1]()], axis=0).astype(BF16)
    padded = lax.dot_general(compact_matrix(ROWS), summed, (((0,), (0,)), ((), ())), preferred_element_type=F32)
    ready[:, :, :LANES] = (padded[:, :LANES] + spare).astype(BF16).reshape(EXPERTS, PAD, LANES)
    ready[:, :, LANES:] = padded[:, LANES:].astype(BF16).reshape(EXPERTS, PAD, COLS - LANES)

    for j in range(1, EXPERTS):
        to = (e + j) % EXPERTS
        c = copy_to(ready.at[to], back.at[e], r_send.at[j], r_recv.at[j], (x, to, y))
        c.start()
        sent.append(c)
    back[e] = ready[e]
    for j in range(1, EXPERTS):
        frm = (e + EXPERTS - j) % EXPERTS
        copy_to(back.at[frm], back.at[frm], r_send.at[j], r_recv.at[j], (x, e, y)).wait_recv()
    block = back[...].reshape(PADDED, COLS)
    out[...] = dot(table[...], block).astype(BF16)
    lanes = block[:, :LANES]
    terms_out[...] = dot(extra_row(0), lanes) + (dot(extra_row(1), lanes) + dot(extra_row(2), lanes))
    for c in sent + one.sent + two.sent:
        c.wait_send()


def gather_call(sx, sd):
    dma = pltpu.SemaphoreType.DMA
    vmem = pl.BlockSpec(memory_space=pltpu.VMEM)
    whole = jax.ShapeDtypeStruct((N_DP, ROWS, D), BF16)
    return pl.pallas_call(
        gather_kernel,
        out_shape=(whole, whole, jax.ShapeDtypeStruct((N_DP, 8, PADDED), F32)),
        in_specs=[vmem] * 2,
        out_specs=(vmem,) * 3,
        scratch_shapes=[
            pltpu.VMEM((EXPERTS, PAD, COLS), BF16),
            pltpu.VMEM((EXPERTS, PAD, COLS), BF16),
            dma((2, EXPERTS)),
            dma((2, EXPERTS)),
            dma((PlaneGather.COUNT,)),
            dma((PlaneGather.COUNT,)),
            dma((PlaneGather.COUNT,)),
            dma((PlaneGather.COUNT,)),
            dma((N_DP,)),
            dma((N_DP,)),
        ],
        compiler_params=pltpu.CompilerParams(collective_id=0, has_side_effects=True, vmem_limit_bytes=48 << 20),
        name="gather",
    )(sx, sd)


def return_call(slots, terms, table):
    dma = pltpu.SemaphoreType.DMA
    vmem = pl.BlockSpec(memory_space=pltpu.VMEM)
    tok = table.shape[0]
    half, quarter = ROWS // 2, ROWS // 4
    landing = [
        pltpu.VMEM((2, 4, quarter, COLS), BF16),
        pltpu.VMEM((2, 4, half, COLS), BF16),
        pltpu.VMEM((2, quarter, COLS), BF16),
        pltpu.VMEM((2, half, COLS), BF16),
    ]
    return pl.pallas_call(
        return_kernel,
        out_shape=(jax.ShapeDtypeStruct((tok, COLS), BF16), jax.ShapeDtypeStruct((EXPERTS, LANES), F32)),
        in_specs=[pl.BlockSpec(memory_space=pl.ANY), vmem, vmem],
        out_specs=(vmem, vmem),
        scratch_shapes=[
            pltpu.VMEM((N_DP, ROWS, D), BF16),
            pltpu.VMEM((N_DP, 8, PADDED), F32),
            pltpu.VMEM((N_DP, 8, PADDED), F32),
            pltpu.VMEM((N_ETP, 8, PADDED), F32),
            *landing,
            *landing,
            pltpu.VMEM((EXPERTS, PAD, COLS), BF16),
            pltpu.VMEM((EXPERTS, PAD, COLS), BF16),
            dma((20,)),
            dma((20,)),
            dma((20,)),
            dma((20,)),
            dma((8,)),
            dma((8,)),
            dma((EXPERTS,)),
            dma((EXPERTS,)),
            dma,
        ],
        compiler_params=pltpu.CompilerParams(collective_id=1, has_side_effects=True, vmem_limit_bytes=48 << 20),
        name="return",
    )(slots, terms, table)


def route(expert_ids):
    count = expert_ids.shape[0]
    flat = expert_ids.reshape(-1)
    onehot = (flat[:, None] == jnp.arange(EXPERTS, dtype=jnp.int32)).astype(BF16)
    before = jnp.tril(jnp.ones((flat.shape[0], flat.shape[0]), BF16), -1)
    earlier = dot(before, onehot)
    slot = jnp.sum(earlier * onehot.astype(F32), axis=1).astype(jnp.int32)
    hits = (onehot[:, :, None] > 0) & (slot[:, None, None] == jnp.arange(PAD, dtype=jnp.int32))
    return hits.reshape(count, TOP, EXPERTS, PAD)


def per_device(tokens, out_grad, gates, expert_ids, w_gate, w_up, w_down):
    tok = tokens.shape[0]
    y = lax.axis_index("etp")
    w_gate, w_up, w_down = w_gate[0], w_up[0], w_down[0]
    hits = route(expert_ids)
    hits_f = hits.astype(F32)
    table = jnp.sum(hits_f, axis=1).reshape(tok, PADDED).astype(BF16)
    quarter = functools.partial(lax.dynamic_slice_in_dim, start_index=y * COLS, slice_size=COLS, axis=1)
    spread = lambda rows: lax.dot_general(
        table, quarter(rows), (((0,), (0,)), ((), ())), preferred_element_type=F32
    ).reshape(EXPERTS, PAD, COLS)
    gate_rows = jnp.sum(hits_f * gates.astype(F32)[:, :, None, None], axis=(0, 1))
    sx = spread(tokens).at[:, CAP, :PAD].add(gate_rows).astype(BF16)
    sd = spread(out_grad).astype(BF16)

    rows, grads, scales = gather_call(sx, sd)
    rows, grads = rows.reshape(N_DP * ROWS, D), grads.reshape(N_DP * ROWS, D)
    scales = scales[:, 0, :ROWS].reshape(1, N_DP * ROWS)
    pre_gate, pre_up, raw_grad = dot_t(w_gate, rows), dot_t(w_up, rows), dot_t(w_down, grads)
    sigmoid_gate = jax.nn.sigmoid(pre_gate)
    activated = pre_gate * sigmoid_gate
    product = activated * pre_up
    terms = jnp.sum(product * raw_grad, axis=0)
    scaled = (scales * product).astype(BF16)
    hidden_grad = scales * raw_grad
    grad_pre_gate = (hidden_grad * pre_up * sigmoid_gate * (1.0 + pre_gate * (1.0 - sigmoid_gate))).astype(BF16)
    grad_pre_up = (hidden_grad * activated).astype(BF16)
    back = functools.partial(lax.dot_general, dimension_numbers=(((0,), (0,)), ((), ())), preferred_element_type=F32)
    slots = (back(grad_pre_gate, w_gate) + back(grad_pre_up, w_up)).astype(BF16).reshape(N_DP, ROWS, D)
    terms = jnp.pad(terms.reshape(N_DP, 1, ROWS), ((0, 0), (0, 7), (0, PADDED - ROWS)))
    grad_gate = dot(grad_pre_gate, rows).astype(BF16)
    grad_up = dot(grad_pre_up, rows).astype(BF16)
    grad_down = dot(scaled, grads).astype(BF16)

    input_grad, gate_slots = return_call(slots, terms, table)
    share = tok // N_ETP
    own = lax.dynamic_slice_in_dim(hits_f, y * share, share, 0)
    gate_grad = jnp.sum(own * gate_slots[:, :PAD], axis=(2, 3))
    return input_grad, gate_grad, grad_gate[None], grad_up[None], grad_down[None]


def solution(mesh):
    in_specs = (
        P(("dp", "expert"), None),
        P(("dp", "expert"), None),
        P(("dp", "expert"), None),
        P(("dp", "expert"), None),
        P("expert", ("dp", "etp"), None),
        P("expert", ("dp", "etp"), None),
        P("expert", ("dp", "etp"), None),
    )
    out_specs = (
        P(("dp", "expert"), "etp"),
        P(("dp", "expert", "etp"), None),
        P("expert", ("dp", "etp"), None),
        P("expert", ("dp", "etp"), None),
        P("expert", ("dp", "etp"), None),
    )
    return jax.shard_map(
        per_device, mesh=mesh, in_specs=in_specs, out_specs=out_specs, check_vma=False
    )
```

```python
import jax
import jax.numpy as jnp
from jax import lax
from jax.experimental import pallas as pl
from jax.experimental.pallas import tpu as pltpu
from jax.sharding import PartitionSpec as P

EXPERTS = 16
TOP = 4
CAP = 12
PAD = 16
N_DP = 4
N_ETP = 4
ROWS = EXPERTS * CAP
PADDED = EXPERTS * PAD
D = 3072
FF = 336
FPAD = 384
COLS = D // N_ETP
LANES = 128
MESH = pl.DeviceIdType.MESH
F32 = jnp.float32
BF16 = jnp.bfloat16


def iota(shape, dim):
    return lax.broadcasted_iota(jnp.int32, shape, dim)


def compact_matrix(rows):
    r, k = iota((rows, PADDED), 0), iota((rows, PADDED), 1)
    return jnp.where(((k >> 4) * CAP + (k & 15) == r) & ((k & 15) < CAP), 1.0, 0.0).astype(BF16)


def extra_row(which):
    b, k = iota((EXPERTS, PADDED), 0), iota((EXPERTS, PADDED), 1)
    return jnp.where(k == b * PAD + CAP + which, 1.0, 0.0).astype(BF16)


def lane_spread():
    c, k = iota((LANES, PADDED), 0), iota((LANES, PADDED), 1)
    return jnp.where((k & 15) == c, 1.0, 0.0).astype(BF16)


def block_mask():
    b, k = iota((EXPERTS, PADDED), 0), iota((EXPERTS, PADDED), 1)
    return jnp.where((k >> 4) == b, 1.0, 0.0).astype(F32)


def block_of_row():
    r, b = iota((ROWS, EXPERTS), 0), iota((ROWS, EXPERTS), 1)
    return jnp.where((r >= b * CAP) & (r < b * CAP + CAP), 1.0, 0.0).astype(BF16)


def slot_of_row():
    return dot_t(compact_matrix(ROWS), lane_spread())


def parts(value):
    out = []
    for _ in range(3):
        part = value.astype(BF16)
        value = value - part.astype(F32)
        out.append(part)
    return out


def dot(a, b):
    return jnp.dot(a, b, preferred_element_type=F32)


def dot_t(a, b):
    return lax.dot_general(a, b, (((1,), (1,)), ((), ())), preferred_element_type=F32)


def t_dot(a, b):
    return lax.dot_general(a, b, (((0,), (0,)), ((), ())), preferred_element_type=F32)


def position():
    return lax.axis_index("dp"), lax.axis_index("expert"), lax.axis_index("etp")


def copy_to(src, dst, send_sem, recv_sem, device):
    return pltpu.make_async_remote_copy(
        src_ref=src, dst_ref=dst, send_sem=send_sem, recv_sem=recv_sem, device_id=device, device_id_type=MESH
    )


def piece(ref, i, j):
    return ref.at[i, :, pl.ds(pl.multiple_of(j * COLS, COLS), COLS)]


class PlaneGather:
    COUNT = 22

    def __init__(self, ref, dp_first, send_sems, recv_sems):
        x, e, y = position()
        self.ref, self.dp_first, self.send_sems, self.recv_sems = ref, dp_first, send_sems, recv_sems
        self.e = e
        self.a, self.b = (x, y) if dp_first else (y, x)
        self.sent = []

    def at(self, i, j, half=None):
        i, j = i % 4, j % 4
        view = piece(self.ref, i, j) if self.dp_first else piece(self.ref, j, i)
        if half is not None:
            view = view.at[pl.ds(half * (ROWS // 2), ROWS // 2), :]
        return view

    def device(self, i, j):
        i, j = i % 4, j % 4
        return (i, self.e, j) if self.dp_first else (j, self.e, i)

    def copy(self, view, index, device):
        return copy_to(view, view, self.send_sems.at[index], self.recv_sems.at[index], device)

    def send(self, view, index, device):
        c = self.copy(view, index, device)
        c.start()
        self.sent.append(c)

    def wait(self, view, index):
        self.copy(view, index, self.device(self.a, self.b)).wait_recv()

    def both_second(self, i, slot, half=None):
        view = self.at(i, self.b, half)
        self.send(view, 4 + 2 * slot, self.device(self.a, self.b + 1))
        self.send(view, 5 + 2 * slot, self.device(self.a, self.b - 1))

    def forward_second(self, i, slot):
        self.wait(self.at(i, self.b - 1), 4 + 2 * slot)
        self.send(self.at(i, self.b - 1, 0), 14 + 2 * slot, self.device(self.a, self.b + 1))
        self.wait(self.at(i, self.b + 1), 5 + 2 * slot)
        self.send(self.at(i, self.b + 1, 1), 15 + 2 * slot, self.device(self.a, self.b - 1))

    def steps(self):
        a, b = self.a, self.b

        def own():
            self.send(self.at(a, b), 0, self.device(a + 1, b))
            self.send(self.at(a, b), 1, self.device(a - 1, b))
            self.both_second(a, 0)

        def lower():
            self.wait(self.at(a - 1, b), 0)
            self.send(self.at(a - 1, b, 0), 2, self.device(a + 1, b))
            self.both_second(a - 1, 1)

        def upper():
            self.wait(self.at(a + 1, b), 1)
            self.send(self.at(a + 1, b, 1), 3, self.device(a - 1, b))
            self.both_second(a + 1, 2)

        def opposite():
            self.wait(self.at(a + 2, b, 0), 2)
            self.both_second(a + 2, 3, 0)
            self.wait(self.at(a + 2, b, 1), 3)
            self.both_second(a + 2, 4, 1)

        def opposite_second():
            self.wait(self.at(a + 2, b - 1, 0), 10)
            self.send(self.at(a + 2, b - 1, 0), 20, self.device(a, b + 1))
            self.wait(self.at(a + 2, b + 1, 1), 13)
            self.send(self.at(a + 2, b + 1, 1), 21, self.device(a, b - 1))

        return [
            own,
            lower,
            upper,
            lambda: self.forward_second(a, 0),
            opposite,
            lambda: self.forward_second(a - 1, 1),
            lambda: self.forward_second(a + 1, 2),
            opposite_second,
        ]

    def finish_first(self, slot):
        a, b = self.a, self.b
        if slot == 3:
            self.wait(self.at(a + 2, b + 1, 0), 11)
            self.wait(self.at(a + 2, b - 1, 1), 12)
        i = (a, a - 1, a + 1, a + 2)[slot]
        self.wait(self.at(i, b + 2, 0), 14 + 2 * slot)
        self.wait(self.at(i, b + 2, 1), 15 + 2 * slot)

    def finish_second(self, slot):
        a, b = self.a, self.b
        if slot == 1:
            self.wait(self.at(a + 2, b - 1, 1), 12)
        if slot == 2:
            self.wait(self.at(a + 2, b + 1, 0), 11)
        if slot == 3:
            for k, i in enumerate((a, a - 1, a + 1, a + 2)):
                self.wait(self.at(i, b + 2, 0), 14 + 2 * k)
                self.wait(self.at(i, b + 2, 1), 15 + 2 * k)


class PlaneReduce:
    HALF = ROWS // 2
    QUARTER = ROWS // 4
    COUNT = 20

    def __init__(self, ref, out, low, dp_first, order, opp, full, opp2, full2, send_sems, recv_sems):
        x, e, y = position()
        self.ref, self.out, self.low, self.dp_first, self.order = ref, out, low, dp_first, order
        self.opp, self.full, self.opp2, self.full2 = opp, full, opp2, full2
        self.send_sems, self.recv_sems = send_sems, recv_sems
        self.e = e
        self.a, self.b = (x, y) if dp_first else (y, x)
        self.sent = []

    def device(self, i, j):
        i, j = i % 4, j % 4
        return (i, self.e, j) if self.dp_first else (j, self.e, i)

    def at(self, i, j, start, size, ref=None):
        i, j = i % 4, j % 4
        ref = self.out if ref is None else ref
        view = piece(ref, i, j) if self.dp_first else piece(ref, j, i)
        return view.at[pl.ds(self.low + start, size), :]

    def send(self, src, dst, index, device):
        c = copy_to(src, dst, self.send_sems.at[index], self.recv_sems.at[index], device)
        c.start()
        self.sent.append(c)

    def wait(self, dst, index):
        copy_to(dst, dst, self.send_sems.at[index], self.recv_sems.at[index], self.device(self.a, self.b)).wait_recv()

    def opposite(self, k):
        a, b, q = self.a, self.b, self.QUARTER
        j = b + self.order[k]
        self.send(self.at(a + 2, j, 0, q), self.opp.at[0, k], 4 * k, self.device(a + 1, b))
        self.send(self.at(a + 2, j, q, q), self.opp.at[1, k], 4 * k + 1, self.device(a - 1, b))

    def near(self, k):
        a, b, q, h = self.a, self.b, self.QUARTER, self.HALF
        j = b + self.order[k]
        for side, to in ((0, a + 1), (1, a - 1)):
            self.wait(self.opp.at[side, k], 4 * k + side)
            own = self.at(to, j, side * q, q, self.ref)[...]
            self.at(to, j, side * q, q)[...] = (own + self.opp[side, k].astype(F32)).astype(BF16)
            self.send(self.at(to, j, 0, h), self.full.at[side, k], 4 * k + 2 + side, self.device(to, b))

    def total(self, relative):
        k = self.order.index(relative)
        for side in range(2):
            self.wait(self.full.at[side, k], 4 * k + 2 + side)
        own = self.at(self.a, self.b + relative, 0, self.HALF, self.ref)[...]
        return own + self.full[0, k].astype(F32) + self.full[1, k].astype(F32)

    def second_opposite(self):
        a, b, q, h = self.a, self.b, self.QUARTER, self.HALF
        self.at(a, b + 2, 0, h)[...] = self.total(2).astype(BF16)
        self.send(self.at(a, b + 2, 0, q), self.opp2.at[0], 16, self.device(a, b + 1))
        self.send(self.at(a, b + 2, q, q), self.opp2.at[1], 17, self.device(a, b - 1))

    def second_near(self, side):
        a, b, q, h = self.a, self.b, self.QUARTER, self.HALF
        step = 1 if side == 0 else -1
        value = self.total(step)
        self.wait(self.opp2.at[side], 16 + side)
        extra = self.opp2[side].astype(F32)
        if side == 0:
            value = jnp.concatenate([value[:q] + extra, value[q:]], axis=0)
        else:
            value = jnp.concatenate([value[:q], value[q:] + extra], axis=0)
        self.at(a, b + step, 0, h)[...] = value.astype(BF16)
        self.send(self.at(a, b + step, 0, h), self.full2.at[side], 18 + side, self.device(a, b + step))

    def finish(self):
        value = self.total(0)
        for side in range(2):
            self.wait(self.full2.at[side], 18 + side)
        return value + self.full2[0].astype(F32) + self.full2[1].astype(F32)


def kernel(
    tokens, out_grad, gates, expert_ids, w_gate, w_up, w_down,
    input_grad, gate_grad, grad_gate, grad_up, grad_down,
    tok, cot, sx, sd, rx, rd, rows, grads, scales, w_in, w_out, pre, raw, deltas, scaled, turned, turned_scaled,
    sums, wire, made, terms, landed_x, landed_y,
    opp_a, full_a, opp2_a, full2_a, opp_b, full_b, opp2_b, full2_b, back, pairs,
    slot_send, slot_recv, x_send, x_recv, d_send, d_recv, g_send, g_recv,
    send_a, recv_a, send_b, recv_b, t_send, t_recv, r_send, r_recv, local,
):
    x, e, y = position()
    columns = pl.ds(pl.multiple_of(y * COLS, COLS), COLS)
    loads = [
        pltpu.make_async_copy(tokens.at[:, columns], tok, local.at[0]),
        pltpu.make_async_copy(out_grad.at[:, columns], cot, local.at[1]),
        pltpu.make_async_copy(w_gate.at[0], w_in.at[pl.ds(0, FF), :], local.at[2]),
        pltpu.make_async_copy(w_up.at[0], w_in.at[pl.ds(FPAD, FF), :], local.at[3]),
        pltpu.make_async_copy(w_down.at[0], w_out.at[pl.ds(0, FF), :], local.at[4]),
    ]
    for c in loads:
        c.start()
    peers = [(x, (e + j) % EXPERTS, y) for j in range(1, EXPERTS)]
    peers += [((x + j) % N_DP, e, y) for j in range(1, N_DP)]
    peers += [(x, e, (y + j) % N_ETP) for j in range(1, N_ETP)]
    barrier = pltpu.get_barrier_semaphore()
    for device in peers:
        pl.semaphore_signal(barrier, inc=1, device_id=device, device_id_type=MESH)

    count = tok.shape[0]
    lane = iota((count, PADDED), 1)
    ids, weight = expert_ids[...], gates[...].astype(F32)
    chosen = [jnp.where(ids[:, k : k + 1] == (lane >> 4), 1.0, 0.0) for k in range(TOP)]
    member = chosen[0] + chosen[1] + chosen[2] + chosen[3]
    before = jnp.where(iota((count, count), 0) > iota((count, count), 1), 1.0, 0.0).astype(BF16)
    earlier = dot(before, member.astype(BF16))
    table = jnp.where(earlier == (lane & 15).astype(F32), member, 0.0)
    gate_slots = sum(chosen[k] * weight[:, k : k + 1] for k in range(TOP)) * table
    gate_slots = jnp.sum(gate_slots, axis=0, keepdims=True)
    gate_rows = dot_t((block_mask() * gate_slots).astype(BF16), lane_spread()).astype(BF16)
    gate_rows = t_dot(extra_row(0), gate_rows)
    table = table.astype(BF16)

    loads[0].wait()
    slots = t_dot(table, tok[...])
    sx[:, :, :LANES] = (slots[:, :LANES] + gate_rows).astype(BF16).reshape(EXPERTS, PAD, LANES)
    sx[:, :, LANES:] = slots[:, LANES:].astype(BF16).reshape(EXPERTS, PAD, COLS - LANES)
    pl.semaphore_wait(barrier, len(peers))
    sent = []

    def exchange(which):
        source, landed = ((sx, rx), (sd, rd))[which]
        for j in range(1, EXPERTS):
            to = (e + j) % EXPERTS
            c = copy_to(source.at[to], landed.at[e], slot_send.at[which, j], slot_recv.at[which, j], (x, to, y))
            c.start()
            sent.append(c)
        landed[e] = source[e]

    def arrive(which):
        source, landed = ((sx, rx), (sd, rd))[which]
        for j in range(1, EXPERTS):
            frm = (e + EXPERTS - j) % EXPERTS
            copy_to(source.at[frm], landed.at[frm], slot_send.at[which, j], slot_recv.at[which, j], (x, e, y)).wait_recv()

    exchange(0)
    loads[1].wait()
    sd[...] = t_dot(table, cot[...]).astype(BF16).reshape(EXPERTS, PAD, COLS)
    exchange(1)
    for ref, low in ((w_in, FF), (w_in, FPAD + FF), (w_out, FF)):
        ref[pl.ds(low, FPAD - FF), :] = jnp.zeros((FPAD - FF, D), BF16)

    gather_x = PlaneGather(rows, True, x_send, x_recv)
    gather_d = PlaneGather(grads, False, d_send, d_recv)
    steps_x, steps_d = gather_x.steps(), gather_d.steps()
    compact = compact_matrix(ROWS)
    arrive(0)
    block = rx[...].reshape(PADDED, COLS)
    rows[x, :, columns] = dot(compact, block).astype(BF16)
    steps_x[0]()
    scales[x] = dot(extra_row(0), block[:, :LANES]).astype(BF16)
    for j in range(1, N_DP):
        c = copy_to(scales.at[x], scales.at[x], g_send.at[j], g_recv.at[j], ((x + j) % N_DP, e, y))
        c.start()
        sent.append(c)
    arrive(1)
    grads[x, :, columns] = dot(compact, rd[...].reshape(PADDED, COLS)).astype(BF16)
    steps_d[0]()

    reduce_a = PlaneReduce(
        sums, wire, 0, True, (2, 1, -1, 0), opp_a, full_a, opp2_a, full2_a, send_a, recv_a
    )
    reduce_b = PlaneReduce(
        sums, wire, ROWS // 2, False, (0, -1, 1, 2), opp_b, full_b, opp2_b, full2_b, send_b, recv_b
    )

    def group(slot):
        g = (x + (0, 3, 1, 2)[slot]) % N_DP
        gather_x.finish_first(slot)
        gather_d.finish_second(slot)
        if slot == 0:
            for c in loads[2:]:
                c.wait()
        else:
            j = (0, 3, 1, 2)[slot]
            copy_to(scales.at[g], scales.at[g], g_send.at[4 - j], g_recv.at[4 - j], (x, e, y)).wait_recv()
        pre[...] = jnp.zeros_like(pre)
        raw[...] = jnp.zeros_like(raw)

        @pl.loop(0, N_ETP)
        def _(k):
            part = pl.ds(pl.multiple_of(k * COLS, COLS), COLS)
            pre[...] += dot_t(rows[g, :, part], w_in[:, part])
            raw[...] += dot_t(grads[g, :, part], w_out[:, part])

        a, u, r = pre[:, :FPAD], pre[:, FPAD:], raw[...]
        which = slot_of_row()
        scale = jnp.sum(dot(block_of_row(), scales[g]) * which, axis=1, keepdims=True)
        sigmoid = jax.nn.sigmoid(a)
        activated = a * sigmoid
        product = activated * u
        q = jnp.sum(product * r, axis=1, keepdims=True) * which
        terms[g] = sum(t_dot(block_of_row(), part) for part in parts(q))
        own = pl.ds(pl.multiple_of(g * ROWS, ROWS), ROWS)
        scaled[own, :] = (scale * product).astype(BF16)
        hidden = scale * r
        deltas[own, :FPAD] = (hidden * u * sigmoid * (1.0 + a * (1.0 - sigmoid))).astype(BF16)
        deltas[own, FPAD:] = (hidden * activated).astype(BF16)

        @pl.loop(0, N_ETP)
        def _(k):
            part = pl.ds(pl.multiple_of(k * COLS, COLS), COLS)
            value = dot(deltas[own, :], w_in[:, part])
            sums[g, :, part] = value
            wire[g, :, part] = value.astype(BF16)

    def weight_grad(which):
        source = (rows, rows, grads)[which]

        @pl.loop(0, N_ETP)
        def _(k):
            part = pl.ds(pl.multiple_of(k * COLS, COLS), COLS)
            left = turned_scaled[:FF, :] if which == 2 else turned[pl.ds(which * FPAD, FF), :]
            made[which, :, part] = dot(left, source[:, :, part].reshape(N_DP * ROWS, COLS)).astype(BF16)

        c = pltpu.make_async_copy(made.at[which], (grad_gate, grad_up, grad_down)[which].at[0], local.at[5 + which])
        c.start()
        loads.append(c)

    for one, two in zip(steps_x[1:6], steps_d[1:6]):
        one()
        two()
    group(0)
    for one, two in zip(steps_x[6:], steps_d[6:]):
        one()
        two()
    reduce_b.opposite(0)
    group(1)
    reduce_b.opposite(1)
    reduce_b.near(0)
    group(2)
    reduce_b.opposite(2)
    reduce_b.near(1)
    group(3)
    for k in range(4):
        reduce_a.opposite(k)
    reduce_b.opposite(3)
    reduce_b.near(2)
    for j in range(1, N_DP):
        to = (x + j) % N_DP
        c = copy_to(terms.at[to], landed_x.at[j], t_send.at[j], t_recv.at[j], (to, e, y))
        c.start()
        sent.append(c)
    turned[...] = deltas[...].T
    turned_scaled[...] = scaled[...].T
    reduce_a.near(0)
    reduce_b.near(3)
    for k in range(1, 4):
        reduce_a.near(k)
    weight_grad(0)
    total = terms[x]
    for j in range(1, N_DP):
        copy_to(landed_x.at[j], landed_x.at[j], t_send.at[j], t_recv.at[j], (x, e, y)).wait_recv()
        total = total + landed_x[j]
    landed_y[0] = total
    for j in range(1, N_ETP):
        c = copy_to(landed_y.at[0], landed_y.at[j], t_send.at[3 + j], t_recv.at[3 + j], (x, e, (y + j) % N_ETP))
        c.start()
        sent.append(c)
    reduce_a.second_opposite()
    reduce_b.second_opposite()
    weight_grad(1)
    for side in range(2):
        reduce_a.second_near(side)
        reduce_b.second_near(side)
    weight_grad(2)
    for j in range(1, N_ETP):
        copy_to(landed_y.at[j], landed_y.at[j], t_send.at[3 + j], t_recv.at[3 + j], (x, e, y)).wait_recv()
        total = total + landed_y[j]
    spare = sum(t_dot(extra_row(which), part) for which, part in enumerate(parts(total)))
    summed = jnp.concatenate([reduce_a.finish(), reduce_b.finish()], axis=0).astype(BF16)
    padded = t_dot(compact, summed)
    for c in sent[: 2 * (EXPERTS - 1)]:
        c.wait_send()
    sx[:, :, :LANES] = (padded[:, :LANES] + spare).astype(BF16).reshape(EXPERTS, PAD, LANES)
    sx[:, :, LANES:] = padded[:, LANES:].astype(BF16).reshape(EXPERTS, PAD, COLS - LANES)
    for j in range(1, EXPERTS):
        to = (e + j) % EXPERTS
        c = copy_to(sx.at[to], back.at[e], r_send.at[j], r_recv.at[j], (x, to, y))
        c.start()
        sent.append(c)
    back[e] = sx[e]
    for j in range(1, EXPERTS):
        frm = (e + EXPERTS - j) % EXPERTS
        copy_to(back.at[frm], back.at[frm], r_send.at[j], r_recv.at[j], (x, e, y)).wait_recv()
    block = back[...].reshape(PADDED, COLS)
    input_grad[...] = dot(table, block).astype(BF16)
    lanes = block[:, :LANES]
    value = jnp.zeros((EXPERTS, PADDED), F32)
    for which in range(3):
        part = dot(extra_row(which), lanes).astype(BF16)
        value = value + dot(part, lane_spread())
    value = jnp.sum(value * block_mask(), axis=0, keepdims=True) * table.astype(F32)
    for k in range(TOP):
        pairs[:, k : k + 1] = jnp.sum(chosen[k] * value, axis=1, keepdims=True)
    share = gate_grad.shape[0]
    gate_grad[...] = pairs[pl.ds(pl.multiple_of(y * share, share), share), :]
    for c in loads[5:]:
        c.wait()
    for c in sent[2 * (EXPERTS - 1) :] + gather_x.sent + gather_d.sent + reduce_a.sent + reduce_b.sent:
        c.wait_send()


def per_device(tokens, out_grad, gates, expert_ids, w_gate, w_up, w_down):
    dma = pltpu.SemaphoreType.DMA
    vmem = pl.BlockSpec(memory_space=pltpu.VMEM)
    hbm = pl.BlockSpec(memory_space=pl.ANY)
    count = tokens.shape[0]
    half, quarter = ROWS // 2, ROWS // 4
    landing = [
        pltpu.VMEM((2, 4, quarter, COLS), BF16),
        pltpu.VMEM((2, 4, half, COLS), BF16),
        pltpu.VMEM((2, quarter, COLS), BF16),
        pltpu.VMEM((2, half, COLS), BF16),
    ]
    all_rows = N_DP * ROWS
    weight = jax.ShapeDtypeStruct(w_gate.shape, BF16)
    return pl.pallas_call(
        kernel,
        out_shape=(
            jax.ShapeDtypeStruct((count, COLS), BF16),
            jax.ShapeDtypeStruct((count // N_ETP, TOP), F32),
            weight,
            weight,
            weight,
        ),
        in_specs=[hbm, hbm, vmem, vmem, hbm, hbm, hbm],
        out_specs=(vmem, vmem, hbm, hbm, hbm),
        scratch_shapes=[
            pltpu.VMEM((count, COLS), BF16),
            pltpu.VMEM((count, COLS), BF16),
            *[pltpu.VMEM((EXPERTS, PAD, COLS), BF16)] * 4,
            pltpu.VMEM((N_DP, ROWS, D), BF16),
            pltpu.VMEM((N_DP, ROWS, D), BF16),
            pltpu.VMEM((N_DP, EXPERTS, LANES), BF16),
            pltpu.VMEM((2 * FPAD, D), BF16),
            pltpu.VMEM((FPAD, D), BF16),
            pltpu.VMEM((ROWS, 2 * FPAD), F32),
            pltpu.VMEM((ROWS, FPAD), F32),
            pltpu.VMEM((all_rows, 2 * FPAD), BF16),
            pltpu.VMEM((all_rows, FPAD), BF16),
            pltpu.VMEM((2 * FPAD, all_rows), BF16),
            pltpu.VMEM((FPAD, all_rows), BF16),
            pltpu.VMEM((N_DP, ROWS, D), F32),
            pltpu.VMEM((N_DP, ROWS, D), BF16),
            pltpu.VMEM((3, FF, D), BF16),
            pltpu.VMEM((N_DP, EXPERTS, LANES), F32),
            pltpu.VMEM((N_DP, EXPERTS, LANES), F32),
            pltpu.VMEM((N_ETP, EXPERTS, LANES), F32),
            *landing,
            *landing,
            pltpu.VMEM((EXPERTS, PAD, COLS), BF16),
            pltpu.VMEM((count, TOP), F32),
            dma((2, EXPERTS)),
            dma((2, EXPERTS)),
            *[dma((PlaneGather.COUNT,))] * 4,
            dma((N_DP,)),
            dma((N_DP,)),
            *[dma((PlaneReduce.COUNT,))] * 4,
            dma((8,)),
            dma((8,)),
            dma((EXPERTS,)),
            dma((EXPERTS,)),
            dma((8,)),
        ],
        compiler_params=pltpu.CompilerParams(collective_id=0, has_side_effects=True, vmem_limit_bytes=58 << 20),
        name="backward",
    )(tokens, out_grad, gates, expert_ids, w_gate, w_up, w_down)


def solution(mesh):
    in_specs = (
        P(("dp", "expert"), None),
        P(("dp", "expert"), None),
        P(("dp", "expert"), None),
        P(("dp", "expert"), None),
        P("expert", ("dp", "etp"), None),
        P("expert", ("dp", "etp"), None),
        P("expert", ("dp", "etp"), None),
    )
    out_specs = (
        P(("dp", "expert"), "etp"),
        P(("dp", "expert", "etp"), None),
        P("expert", ("dp", "etp"), None),
        P("expert", ("dp", "etp"), None),
        P("expert", ("dp", "etp"), None),
    )
    return jax.shard_map(
        per_device, mesh=mesh, in_specs=in_specs, out_specs=out_specs, check_vma=False
    )
```

```python
import jax
import jax.numpy as jnp
from jax import lax
from jax.experimental import pallas as pl
from jax.experimental.pallas import tpu as pltpu
from jax.sharding import PartitionSpec as P

EXPERTS = 16
TOP = 4
CAP = 12
PAD = 16
N_DP = 4
N_ETP = 4
ROWS = EXPERTS * CAP
PADDED = EXPERTS * PAD
D = 3072
FF = 336
FPAD = 384
COLS = D // N_ETP
WHOLE = 512
SLOTTED = D - WHOLE
PART = SLOTTED // N_ETP
EARLY = 256
TOK = 32
CHUNK = 512
LANES = 128
MESH = pl.DeviceIdType.MESH
F32 = jnp.float32
BF16 = jnp.bfloat16


def iota(shape, dim):
    return lax.broadcasted_iota(jnp.int32, shape, dim)


def compact_matrix(rows):
    r, k = iota((rows, PADDED), 0), iota((rows, PADDED), 1)
    return jnp.where(((k >> 4) * CAP + (k & 15) == r) & ((k & 15) < CAP), 1.0, 0.0).astype(BF16)


def same_row(which):
    k, m = iota((PADDED, PADDED), 0), iota((PADDED, PADDED), 1)
    return jnp.where(m == (k >> 4) * PAD + CAP + which, 1.0, 0.0).astype(BF16)


def extra_row(which):
    b, k = iota((EXPERTS, PADDED), 0), iota((EXPERTS, PADDED), 1)
    return jnp.where(k == b * PAD + CAP + which, 1.0, 0.0).astype(BF16)


def lane_spread():
    c, k = iota((LANES, PADDED), 0), iota((LANES, PADDED), 1)
    return jnp.where((k & 15) == c, 1.0, 0.0).astype(BF16)


def block_of_row():
    r, b = iota((ROWS, EXPERTS), 0), iota((ROWS, EXPERTS), 1)
    return jnp.where((r >= b * CAP) & (r < b * CAP + CAP), 1.0, 0.0).astype(BF16)


def slot_of_row():
    return dot_t(compact_matrix(ROWS), lane_spread())


def parts(value):
    out = []
    for _ in range(3):
        part = value.astype(BF16)
        value = value - part.astype(F32)
        out.append(part)
    return out


def dot(a, b):
    return jnp.dot(a, b, preferred_element_type=F32)


def dot_t(a, b):
    return lax.dot_general(a, b, (((1,), (1,)), ((), ())), preferred_element_type=F32)


def t_dot(a, b):
    return lax.dot_general(a, b, (((0,), (0,)), ((), ())), preferred_element_type=F32)


def position():
    return lax.axis_index("dp"), lax.axis_index("expert"), lax.axis_index("etp")


def copy_to(src, dst, send_sem, recv_sem, device):
    return pltpu.make_async_remote_copy(
        src_ref=src, dst_ref=dst, send_sem=send_sem, recv_sem=recv_sem, device_id=device, device_id_type=MESH
    )


def piece(ref, i, j):
    return ref.at[i, :, pl.ds(pl.multiple_of(j * COLS, COLS), COLS)]


class PlaneGather:
    COUNT = 22

    def __init__(self, ref, start, width, dp_first, send_sems, recv_sems):
        x, e, y = position()
        self.ref, self.dp_first, self.send_sems, self.recv_sems = ref, dp_first, send_sems, recv_sems
        self.start, self.width = start, width
        self.e = e
        self.a, self.b = (x, y) if dp_first else (y, x)
        self.sent = []

    def at(self, i, j, half=None):
        i, j = i % 4, j % 4
        if not self.dp_first:
            i, j = j, i
        columns = pl.ds(pl.multiple_of(j * PART + self.start, LANES), self.width)
        if half is None:
            return self.ref.at[i, :, columns]
        return self.ref.at[i, pl.ds(half * (ROWS // 2), ROWS // 2), columns]

    def device(self, i, j):
        i, j = i % 4, j % 4
        return (i, self.e, j) if self.dp_first else (j, self.e, i)

    def copy(self, view, index, device):
        return copy_to(view, view, self.send_sems.at[index], self.recv_sems.at[index], device)

    def send(self, view, index, device):
        c = self.copy(view, index, device)
        c.start()
        self.sent.append(c)

    def wait(self, view, index):
        self.copy(view, index, self.device(self.a, self.b)).wait_recv()

    def both_second(self, i, slot, half=None):
        view = self.at(i, self.b, half)
        self.send(view, 4 + 2 * slot, self.device(self.a, self.b + 1))
        self.send(view, 5 + 2 * slot, self.device(self.a, self.b - 1))

    def forward_second(self, i, slot):
        self.wait(self.at(i, self.b - 1), 4 + 2 * slot)
        self.send(self.at(i, self.b - 1, 0), 14 + 2 * slot, self.device(self.a, self.b + 1))
        self.wait(self.at(i, self.b + 1), 5 + 2 * slot)
        self.send(self.at(i, self.b + 1, 1), 15 + 2 * slot, self.device(self.a, self.b - 1))

    def steps(self):
        a, b = self.a, self.b

        def own():
            self.send(self.at(a, b), 0, self.device(a + 1, b))
            self.send(self.at(a, b), 1, self.device(a - 1, b))
            self.both_second(a, 0)

        def lower():
            self.wait(self.at(a - 1, b), 0)
            self.send(self.at(a - 1, b, 0), 2, self.device(a + 1, b))
            self.both_second(a - 1, 1)

        def upper():
            self.wait(self.at(a + 1, b), 1)
            self.send(self.at(a + 1, b, 1), 3, self.device(a - 1, b))
            self.both_second(a + 1, 2)

        def opposite():
            self.wait(self.at(a + 2, b, 0), 2)
            self.both_second(a + 2, 3, 0)
            self.wait(self.at(a + 2, b, 1), 3)
            self.both_second(a + 2, 4, 1)

        def opposite_second():
            self.wait(self.at(a + 2, b - 1, 0), 10)
            self.send(self.at(a + 2, b - 1, 0), 20, self.device(a, b + 1))
            self.wait(self.at(a + 2, b + 1, 1), 13)
            self.send(self.at(a + 2, b + 1, 1), 21, self.device(a, b - 1))

        return [
            own,
            lower,
            upper,
            lambda: self.forward_second(a, 0),
            opposite,
            lambda: self.forward_second(a - 1, 1),
            lambda: self.forward_second(a + 1, 2),
            opposite_second,
        ]

    def finish_first(self, slot):
        a, b = self.a, self.b
        if slot == 3:
            self.wait(self.at(a + 2, b + 1, 0), 11)
            self.wait(self.at(a + 2, b - 1, 1), 12)
        i = (a, a - 1, a + 1, a + 2)[slot]
        self.wait(self.at(i, b + 2, 0), 14 + 2 * slot)
        self.wait(self.at(i, b + 2, 1), 15 + 2 * slot)

    def finish_second(self, slot):
        a, b = self.a, self.b
        if slot == 1:
            self.wait(self.at(a + 2, b - 1, 1), 12)
        if slot == 2:
            self.wait(self.at(a + 2, b + 1, 0), 11)
        if slot == 3:
            for k, i in enumerate((a, a - 1, a + 1, a + 2)):
                self.wait(self.at(i, b + 2, 0), 14 + 2 * k)
                self.wait(self.at(i, b + 2, 1), 15 + 2 * k)


class PlaneReduce:
    HALF = ROWS // 2
    QUARTER = ROWS // 4
    COUNT = 20

    def __init__(self, ref, out, low, dp_first, order, opp, full, opp2, full2, send_sems, recv_sems):
        x, e, y = position()
        self.ref, self.out, self.low, self.dp_first, self.order = ref, out, low, dp_first, order
        self.opp, self.full, self.opp2, self.full2 = opp, full, opp2, full2
        self.send_sems, self.recv_sems = send_sems, recv_sems
        self.e = e
        self.a, self.b = (x, y) if dp_first else (y, x)
        self.sent = []

    def device(self, i, j):
        i, j = i % 4, j % 4
        return (i, self.e, j) if self.dp_first else (j, self.e, i)

    def at(self, i, j, start, size, ref=None):
        i, j = i % 4, j % 4
        ref = self.out if ref is None else ref
        view = piece(ref, i, j) if self.dp_first else piece(ref, j, i)
        return view.at[pl.ds(self.low + start, size), :]

    def send(self, src, dst, index, device):
        c = copy_to(src, dst, self.send_sems.at[index], self.recv_sems.at[index], device)
        c.start()
        self.sent.append(c)

    def wait(self, dst, index):
        copy_to(dst, dst, self.send_sems.at[index], self.recv_sems.at[index], self.device(self.a, self.b)).wait_recv()

    def opposite(self, k):
        a, b, q = self.a, self.b, self.QUARTER
        j = b + self.order[k]
        self.send(self.at(a + 2, j, 0, q), self.opp.at[0, k], 4 * k, self.device(a + 1, b))
        self.send(self.at(a + 2, j, q, q), self.opp.at[1, k], 4 * k + 1, self.device(a - 1, b))

    def near(self, k):
        a, b, q, h = self.a, self.b, self.QUARTER, self.HALF
        j = b + self.order[k]
        for side, to in ((0, a + 1), (1, a - 1)):
            self.wait(self.opp.at[side, k], 4 * k + side)
            own = self.at(to, j, side * q, q, self.ref)[...]
            self.at(to, j, side * q, q)[...] = (own + self.opp[side, k].astype(F32)).astype(BF16)
            self.send(self.at(to, j, 0, h), self.full.at[side, k], 4 * k + 2 + side, self.device(to, b))

    def total(self, relative):
        k = self.order.index(relative)
        for side in range(2):
            self.wait(self.full.at[side, k], 4 * k + 2 + side)
        own = self.at(self.a, self.b + relative, 0, self.HALF, self.ref)[...]
        return own + self.full[0, k].astype(F32) + self.full[1, k].astype(F32)

    def second_opposite(self):
        a, b, q, h = self.a, self.b, self.QUARTER, self.HALF
        self.at(a, b + 2, 0, h)[...] = self.total(2).astype(BF16)
        self.send(self.at(a, b + 2, 0, q), self.opp2.at[0], 16, self.device(a, b + 1))
        self.send(self.at(a, b + 2, q, q), self.opp2.at[1], 17, self.device(a, b - 1))

    def second_near(self, side):
        a, b, q, h = self.a, self.b, self.QUARTER, self.HALF
        step = 1 if side == 0 else -1
        value = self.total(step)
        self.wait(self.opp2.at[side], 16 + side)
        extra = self.opp2[side].astype(F32)
        if side == 0:
            value = jnp.concatenate([value[:q] + extra, value[q:]], axis=0)
        else:
            value = jnp.concatenate([value[:q], value[q:] + extra], axis=0)
        self.at(a, b + step, 0, h)[...] = value.astype(BF16)
        self.send(self.at(a, b + step, 0, h), self.full2.at[side], 18 + side, self.device(a, b + step))

    def finish(self):
        value = self.total(0)
        for side in range(2):
            self.wait(self.full2.at[side], 18 + side)
        return value + self.full2[0].astype(F32) + self.full2[1].astype(F32)


class TokenGather:
    def __init__(self, ref, sources, dp_send, dp_recv, z_send, z_recv, core_send, core_recv, local):
        self.x, self.e, self.y = position()
        self.ref, self.sources = ref, sources
        self.dp_send, self.dp_recv = dp_send, dp_recv
        self.z_send, self.z_recv, self.core_send, self.core_recv = z_send, z_recv, core_send, core_recv
        self.other = self.e + 1 - 2 * (self.e % 2)
        self.sent = []
        own = [
            pltpu.make_async_copy(s.at[:, pl.ds(SLOTTED, WHOLE)], self.landing(self.x, which), local.at[which])
            for which, s in enumerate(sources)
        ]
        self.own = own

    def landing(self, i, which):
        rows = pl.ds(pl.multiple_of(self.e * TOK, TOK), TOK)
        return self.ref.at[i, rows, pl.ds(which * WHOLE, WHOLE)]

    def block(self, e, half=None):
        rows = pl.ds(pl.multiple_of((e % EXPERTS) * TOK, TOK), TOK)
        if half is None:
            return self.ref.at[:, rows, :]
        return self.ref.at[pl.ds(2 * half, 2), rows, :]

    def copy(self, src, dst, send, recv, device):
        c = copy_to(src, dst, send, recv, device)
        c.start()
        self.sent.append(c)

    def along_dp(self):
        for c in self.own:
            c.start()
        for j in range(1, N_DP):
            for which, source in enumerate(self.sources):
                self.copy(
                    source.at[:, pl.ds(SLOTTED, WHOLE)], self.landing(self.x, which),
                    self.dp_send.at[which, j], self.dp_recv.at[which, j], ((self.x + j) % N_DP, self.e, self.y),
                )

    def arrived_dp(self):
        for c in self.own:
            c.wait()
        for j in range(1, N_DP):
            for which in range(2):
                view = self.landing((self.x + N_DP - j) % N_DP, which)
                copy_to(
                    view, view, self.dp_send.at[which, j], self.dp_recv.at[which, j], (self.x, self.e, self.y)
                ).wait_recv()

    def view(self, e, side, distance):
        away = 2 * distance
        return self.block(e + (EXPERTS - away if side == 0 else away), side if distance == 4 else None)

    def onward(self, side, distance):
        e = self.e
        view = self.view(e, side, distance)
        if distance > 0:
            copy_to(
                view, view, self.z_send.at[side, distance], self.z_recv.at[side, distance], (self.x, e, self.y)
            ).wait_recv()
        if distance < 4:
            to = (e + (2 if side == 0 else EXPERTS - 2)) % EXPERTS
            next_view = self.view(to, side, distance + 1)
            self.copy(
                next_view, next_view,
                self.z_send.at[side, distance + 1], self.z_recv.at[side, distance + 1], (self.x, to, self.y),
            )
        if distance > 0 or side == 0:
            self.copy(
                view, view, self.core_send.at[side, distance], self.core_recv.at[side, distance],
                (self.x, self.other, self.y),
            )

    def round(self, distance):
        for side in range(2):
            self.onward(side, distance)

    def finish(self):
        for distance in range(5):
            for side in range(2):
                if distance > 0 or side == 0:
                    view = self.view(self.other, side, distance)
                    copy_to(
                        view, view, self.core_send.at[side, distance], self.core_recv.at[side, distance],
                        (self.x, self.e, self.y),
                    ).wait_recv()


def kernel(
    tokens, out_grad, gates, expert_ids, w_gate, w_up, w_down,
    input_grad, gate_grad, grad_gate, grad_up, grad_down,
    tok, cot, sx, sd, rx, rd, rows, grads, tables, whole, w_in, w_out, pre, raw, deltas, scaled, turned, turned_scaled,
    sums, wire, made, terms, landed_x, landed_y,
    opp_a, full_a, opp2_a, full2_a, opp_b, full_b, opp2_b, full2_b, back, ready,
    slot_send, slot_recv, x_send, x_recv, late_send, late_recv, d_send, d_recv, g_send, g_recv,
    dp_send, dp_recv, z_send, z_recv, core_send, core_recv,
    send_a, recv_a, send_b, recv_b, t_send, t_recv, r_send, r_recv, local,
):
    x, e, y = position()
    columns = pl.ds(pl.multiple_of(y * PART, LANES), PART)
    loads = [
        pltpu.make_async_copy(tokens.at[:, columns], tok, local.at[0]),
        pltpu.make_async_copy(out_grad.at[:, columns], cot, local.at[1]),
        pltpu.make_async_copy(w_gate.at[0], w_in.at[pl.ds(0, FF), :], local.at[2]),
        pltpu.make_async_copy(w_up.at[0], w_in.at[pl.ds(FPAD, FF), :], local.at[3]),
        pltpu.make_async_copy(w_down.at[0], w_out.at[pl.ds(0, FF), :], local.at[4]),
    ]
    for c in loads:
        c.start()
    peers = [(x, (e + j) % EXPERTS, y) for j in range(1, EXPERTS)]
    peers += [((x + j) % N_DP, e, y) for j in range(1, N_DP)]
    peers += [(x, e, (y + j) % N_ETP) for j in range(1, N_ETP)]
    barrier = pltpu.get_barrier_semaphore()
    for device in peers:
        pl.semaphore_signal(barrier, inc=1, device_id=device, device_id_type=MESH)

    expert, place = iota((PADDED, TOK), 0) >> 4, iota((PADDED, TOK), 0) & 15
    ids, weight = expert_ids[...], gates[...].astype(F32)
    chosen = [jnp.where(ids[k : k + 1, :] == expert, 1.0, 0.0) for k in range(TOP)]
    member = chosen[0] + chosen[1] + chosen[2] + chosen[3]
    before = jnp.where(iota((TOK, TOK), 0) < iota((TOK, TOK), 1), 1.0, 0.0).astype(BF16)
    earlier = dot(member.astype(BF16), before)
    table = jnp.where((earlier == place.astype(F32)) & (place < CAP), member, 0.0)
    gate_slots = sum(chosen[k] * weight[k : k + 1, :] for k in range(TOP)) * table
    gate_slots = jnp.sum(gate_slots, axis=1, keepdims=True)
    table = table.astype(BF16)
    widen = jnp.where(iota((TOK, LANES), 0) == iota((TOK, LANES), 1), 1.0, 0.0).astype(BF16)
    sent = []

    loads[0].wait()
    sx[:, :, :PART] = dot(table, tok[...]).astype(BF16).reshape(EXPERTS, PAD, PART)
    wide = jnp.where(iota((PADDED, LANES), 1) == TOK, gate_slots, dot(table, widen))
    sx[:, :, PART:] = wide.astype(BF16).reshape(EXPERTS, PAD, LANES)
    pl.semaphore_wait(barrier, len(peers))
    cuts = ((sx, rx, 0, EARLY), (sx, rx, EARLY, PART + LANES - EARLY), (sd, rd, 0, PART))

    def exchange(which):
        source, landed, start, width = cuts[which]
        for j in range(1, EXPERTS):
            to = (e + j) % EXPERTS
            c = copy_to(
                source.at[to, :, pl.ds(start, width)], landed.at[e, :, pl.ds(start, width)],
                slot_send.at[which, j], slot_recv.at[which, j], (x, to, y),
            )
            c.start()
            sent.append(c)

    def arrive(which):
        source, landed, start, width = cuts[which]
        for j in range(1, EXPERTS):
            frm = (e + EXPERTS - j) % EXPERTS
            view = landed.at[frm, :, pl.ds(start, width)]
            copy_to(view, view, slot_send.at[which, j], slot_recv.at[which, j], (x, e, y)).wait_recv()

    token_gather = TokenGather(
        whole, (tokens, out_grad), dp_send, dp_recv, z_send, z_recv, core_send, core_recv, local.at[pl.ds(8, 2)]
    )
    exchange(0)
    token_gather.along_dp()
    exchange(1)
    rx[e] = sx[e]
    loads[1].wait()
    sd[...] = dot(table, cot[...]).astype(BF16).reshape(EXPERTS, PAD, PART)
    exchange(2)
    rd[e] = sd[e]
    for ref, low in ((w_in, FF), (w_in, FPAD + FF), (w_out, FF)):
        ref[pl.ds(low, FPAD - FF), :] = jnp.zeros((FPAD - FF, D), BF16)

    first = PlaneGather(rows, 0, EARLY, True, x_send, x_recv)
    late = PlaneGather(rows, EARLY, PART - EARLY, True, late_send, late_recv)
    second = PlaneGather(grads, 0, PART, False, d_send, d_recv)
    steps_0, steps_1, steps_2 = first.steps(), late.steps(), second.steps()
    compact = compact_matrix(ROWS)

    def pack(landed, ref, start, width):
        value = dot(compact, landed[:, :, start : start + width].reshape(PADDED, width)).astype(BF16)
        ref[x, :, pl.ds(pl.multiple_of(y * PART + start, LANES), width)] = value

    def run(steps, *which):
        for k in which:
            steps[k]()

    arrive(0)
    pack(rx, rows, 0, EARLY)
    run(steps_0, 0)
    token_gather.arrived_dp()
    token_gather.round(0)
    arrive(1)
    pack(rx, rows, EARLY, PART - EARLY)
    run(steps_1, 0)
    tables[x] = dot(compact, rx[:, :, PART:].reshape(PADDED, LANES)).astype(BF16)
    for j in range(1, N_DP):
        c = copy_to(tables.at[x], tables.at[x], g_send.at[j], g_recv.at[j], ((x + j) % N_DP, e, y))
        c.start()
        sent.append(c)
    run(steps_0, 1, 2)
    arrive(2)
    pack(rd, grads, 0, PART)
    run(steps_2, 0)
    run(steps_0, 3, 4)
    run(steps_1, 1, 2)
    token_gather.round(1)
    run(steps_2, 1, 2)
    run(steps_1, 3, 4)
    run(steps_0, 5, 6, 7)
    token_gather.round(2)
    run(steps_2, 3, 4)
    run(steps_1, 5, 6, 7)
    token_gather.round(3)
    run(steps_2, 5, 6, 7)

    reduce_a = PlaneReduce(
        sums, wire, 0, True, (2, 1, -1, 0), opp_a, full_a, opp2_a, full2_a, send_a, recv_a
    )
    reduce_b = PlaneReduce(
        sums, wire, ROWS // 2, False, (0, -1, 1, 2), opp_b, full_b, opp2_b, full2_b, send_b, recv_b
    )

    def forward(g, k):
        part = pl.ds(pl.multiple_of(k * CHUNK, CHUNK), CHUNK)
        pre[g] += dot_t(rows[g, :, part], w_in[:, part])
        raw[g] += dot_t(grads[g, :, part], w_out[:, part])

    def begin(slot):
        j = (0, 3, 1, 2)[slot]
        g = (x + j) % N_DP
        first.finish_first(slot)
        late.finish_first(slot)
        second.finish_second(slot)
        if slot == 0:
            for c in loads[2:]:
                c.wait()
        pre[g] = jnp.zeros((ROWS, 2 * FPAD), F32)
        raw[g] = jnp.zeros((ROWS, FPAD), F32)

        @pl.loop(0, SLOTTED // CHUNK)
        def _(k):
            forward(g, k)

    def complete(slot):
        j = (0, 3, 1, 2)[slot]
        g = (x + j) % N_DP
        if slot > 0:
            copy_to(tables.at[g], tables.at[g], g_send.at[4 - j], g_recv.at[4 - j], (x, e, y)).wait_recv()
        repeat = jnp.where(iota((LANES, EXPERTS * TOK), 0) == (iota((LANES, EXPERTS * TOK), 1) & 31), 1.0, 0.0)
        within = jnp.where(iota((EXPERTS, EXPERTS * TOK), 0) == (iota((EXPERTS, EXPERTS * TOK), 1) >> 5), 1.0, 0.0)
        pick = dot(tables[g], repeat.astype(BF16)) * dot(block_of_row(), within.astype(BF16))
        picked = dot(pick.astype(BF16), whole[g]).astype(BF16)
        rows[g, :, SLOTTED:] = picked[:, :WHOLE]
        grads[g, :, SLOTTED:] = picked[:, WHOLE:]
        forward(g, SLOTTED // CHUNK)
        a, u, r = pre[g, :, :FPAD], pre[g, :, FPAD:], raw[g]
        which = slot_of_row()
        scale = tables[g, :, TOK : TOK + 1].astype(F32)
        sigmoid = jax.nn.sigmoid(a)
        activated = a * sigmoid
        product = activated * u
        q = jnp.sum(product * r, axis=1, keepdims=True) * which
        terms[g] = sum(t_dot(block_of_row(), part) for part in parts(q))
        own = pl.ds(pl.multiple_of(g * ROWS, ROWS), ROWS)
        scaled[own, :] = (scale * product).astype(BF16)
        hidden = scale * r
        deltas[own, :FPAD] = (hidden * u * sigmoid * (1.0 + a * (1.0 - sigmoid))).astype(BF16)
        deltas[own, FPAD:] = (hidden * activated).astype(BF16)

        @pl.loop(0, N_ETP)
        def _(k):
            part = pl.ds(pl.multiple_of(k * COLS, COLS), COLS)
            value = dot(deltas[own, :], w_in[:, part])
            sums[g, :, part] = value
            wire[g, :, part] = value.astype(BF16)

    def weight_grad(which):
        source = (rows, rows, grads)[which]

        @pl.loop(0, N_ETP)
        def _(k):
            part = pl.ds(pl.multiple_of(k * COLS, COLS), COLS)
            left = turned_scaled[:FF, :] if which == 2 else turned[pl.ds(which * FPAD, FF), :]
            made[which, :, part] = dot(left, source[:, :, part].reshape(N_DP * ROWS, COLS)).astype(BF16)

        c = pltpu.make_async_copy(made.at[which], (grad_gate, grad_up, grad_down)[which].at[0], local.at[5 + which])
        c.start()
        loads.append(c)

    begin(0)
    token_gather.round(4)
    begin(1)
    token_gather.finish()
    complete(0)
    reduce_b.opposite(0)
    complete(1)
    reduce_b.opposite(1)
    reduce_b.near(0)
    begin(2)
    complete(2)
    reduce_b.opposite(2)
    reduce_b.near(1)
    begin(3)
    complete(3)
    for k in range(4):
        reduce_a.opposite(k)
    reduce_b.opposite(3)
    reduce_b.near(2)
    for j in range(1, N_DP):
        to = (x + j) % N_DP
        c = copy_to(terms.at[to], landed_x.at[j], t_send.at[j], t_recv.at[j], (to, e, y))
        c.start()
        sent.append(c)
    turned[...] = deltas[...].T
    turned_scaled[...] = scaled[...].T
    reduce_a.near(0)
    reduce_b.near(3)
    for k in range(1, 4):
        reduce_a.near(k)
    weight_grad(0)
    total = terms[x]
    for j in range(1, N_DP):
        copy_to(landed_x.at[j], landed_x.at[j], t_send.at[j], t_recv.at[j], (x, e, y)).wait_recv()
        total = total + landed_x[j]
    landed_y[0] = total
    for j in range(1, N_ETP):
        c = copy_to(landed_y.at[0], landed_y.at[j], t_send.at[3 + j], t_recv.at[3 + j], (x, e, (y + j) % N_ETP))
        c.start()
        sent.append(c)
    reduce_a.second_opposite()
    reduce_b.second_opposite()
    weight_grad(1)
    for side in range(2):
        reduce_a.second_near(side)
        reduce_b.second_near(side)
    weight_grad(2)
    for j in range(1, N_ETP):
        copy_to(landed_y.at[j], landed_y.at[j], t_send.at[3 + j], t_recv.at[3 + j], (x, e, y)).wait_recv()
        total = total + landed_y[j]
    spare = sum(t_dot(extra_row(which), part) for which, part in enumerate(parts(total)))
    summed = jnp.concatenate([reduce_a.finish(), reduce_b.finish()], axis=0).astype(BF16)
    padded = t_dot(compact, summed)
    ready[:, :, :LANES] = (padded[:, :LANES] + spare).astype(BF16).reshape(EXPERTS, PAD, LANES)
    ready[:, :, LANES:] = padded[:, LANES:].astype(BF16).reshape(EXPERTS, PAD, COLS - LANES)
    for j in range(1, EXPERTS):
        to = (e + j) % EXPERTS
        c = copy_to(ready.at[to], back.at[e], r_send.at[j], r_recv.at[j], (x, to, y))
        c.start()
        sent.append(c)
    back[e] = ready[e]
    for j in range(1, EXPERTS):
        frm = (e + EXPERTS - j) % EXPERTS
        copy_to(back.at[frm], back.at[frm], r_send.at[j], r_recv.at[j], (x, e, y)).wait_recv()
    block = back[...].reshape(PADDED, COLS)
    input_grad[...] = t_dot(table, block).astype(BF16)
    lanes = block[:, :LANES]
    mine = jnp.where(iota((PADDED, LANES), 1) == (iota((PADDED, LANES), 0) & 15), 1.0, 0.0)
    value = sum(dot(same_row(which), lanes) for which in range(3))
    value = jnp.sum(value * mine, axis=1, keepdims=True) * table.astype(F32)
    pairs = jnp.concatenate([jnp.sum(chosen[k] * value, axis=0, keepdims=True) for k in range(TOP)], axis=0)
    share = TOK // N_ETP
    take = jnp.where(iota((TOK, share), 0) == iota((TOK, share), 1) + y * share, 1.0, 0.0).astype(BF16)
    gate_grad[...] = sum(dot(part, take) for part in parts(pairs))
    for c in loads[5:]:
        c.wait()
    for c in sent + first.sent + late.sent + second.sent + token_gather.sent + reduce_a.sent + reduce_b.sent:
        c.wait_send()


def per_device(tokens, out_grad, gates, expert_ids, w_gate, w_up, w_down):
    dma = pltpu.SemaphoreType.DMA
    vmem = pl.BlockSpec(memory_space=pltpu.VMEM)
    hbm = pl.BlockSpec(memory_space=pl.ANY)
    count = tokens.shape[0]
    half, quarter = ROWS // 2, ROWS // 4
    landing = [
        pltpu.VMEM((2, 4, quarter, COLS), BF16),
        pltpu.VMEM((2, 4, half, COLS), BF16),
        pltpu.VMEM((2, quarter, COLS), BF16),
        pltpu.VMEM((2, half, COLS), BF16),
    ]
    all_rows = N_DP * ROWS
    weight = jax.ShapeDtypeStruct(w_gate.shape, BF16)
    input_grad, gate_grad, *weight_grads = pl.pallas_call(
        kernel,
        out_shape=(
            jax.ShapeDtypeStruct((count, COLS), BF16),
            jax.ShapeDtypeStruct((TOP, count // N_ETP), F32),
            weight,
            weight,
            weight,
        ),
        in_specs=[hbm, hbm, vmem, vmem, hbm, hbm, hbm],
        out_specs=(vmem, vmem, hbm, hbm, hbm),
        scratch_shapes=[
            pltpu.VMEM((count, PART), BF16),
            pltpu.VMEM((count, PART), BF16),
            pltpu.VMEM((EXPERTS, PAD, PART + LANES), BF16),
            pltpu.VMEM((EXPERTS, PAD, PART), BF16),
            pltpu.VMEM((EXPERTS, PAD, PART + LANES), BF16),
            pltpu.VMEM((EXPERTS, PAD, PART), BF16),
            pltpu.VMEM((N_DP, ROWS, D), BF16),
            pltpu.VMEM((N_DP, ROWS, D), BF16),
            pltpu.VMEM((N_DP, ROWS, LANES), BF16),
            pltpu.VMEM((N_DP, EXPERTS * TOK, 2 * WHOLE), BF16),
            pltpu.VMEM((2 * FPAD, D), BF16),
            pltpu.VMEM((FPAD, D), BF16),
            pltpu.VMEM((N_DP, ROWS, 2 * FPAD), F32),
            pltpu.VMEM((N_DP, ROWS, FPAD), F32),
            pltpu.VMEM((all_rows, 2 * FPAD), BF16),
            pltpu.VMEM((all_rows, FPAD), BF16),
            pltpu.VMEM((2 * FPAD, all_rows), BF16),
            pltpu.VMEM((FPAD, all_rows), BF16),
            pltpu.VMEM((N_DP, ROWS, D), F32),
            pltpu.VMEM((N_DP, ROWS, D), BF16),
            pltpu.VMEM((3, FF, D), BF16),
            pltpu.VMEM((N_DP, EXPERTS, LANES), F32),
            pltpu.VMEM((N_DP, EXPERTS, LANES), F32),
            pltpu.VMEM((N_ETP, EXPERTS, LANES), F32),
            *landing,
            *landing,
            pltpu.VMEM((EXPERTS, PAD, COLS), BF16),
            pltpu.VMEM((EXPERTS, PAD, COLS), BF16),
            dma((3, EXPERTS)),
            dma((3, EXPERTS)),
            *[dma((PlaneGather.COUNT,))] * 6,
            dma((N_DP,)),
            dma((N_DP,)),
            *[dma((2, N_DP))] * 2,
            *[dma((2, 5))] * 4,
            *[dma((PlaneReduce.COUNT,))] * 4,
            dma((8,)),
            dma((8,)),
            dma((EXPERTS,)),
            dma((EXPERTS,)),
            dma((10,)),
        ],
        compiler_params=pltpu.CompilerParams(collective_id=0, has_side_effects=True, vmem_limit_bytes=58 << 20),
        name="backward",
    )(tokens, out_grad, gates.T, expert_ids.T, w_gate, w_up, w_down)
    return input_grad, gate_grad.T, *weight_grads


def solution(mesh):
    in_specs = (
        P(("dp", "expert"), None),
        P(("dp", "expert"), None),
        P(("dp", "expert"), None),
        P(("dp", "expert"), None),
        P("expert", ("dp", "etp"), None),
        P("expert", ("dp", "etp"), None),
        P("expert", ("dp", "etp"), None),
    )
    out_specs = (
        P(("dp", "expert"), "etp"),
        P(("dp", "expert", "etp"), None),
        P("expert", ("dp", "etp"), None),
        P("expert", ("dp", "etp"), None),
        P("expert", ("dp", "etp"), None),
    )
    return jax.shard_map(
        per_device, mesh=mesh, in_specs=in_specs, out_specs=out_specs, check_vma=False
    )
```

```python
import jax
import jax.numpy as jnp
from jax import lax
from jax.experimental import pallas as pl
from jax.experimental.pallas import tpu as pltpu
from jax.sharding import PartitionSpec as P

EXPERTS = 16
TOP = 4
CAP = 12
PAD = 16
N_DP = 4
N_ETP = 4
ROWS = EXPERTS * CAP
PADDED = EXPERTS * PAD
D = 3072
FF = 336
FPAD = 384
COLS = D // N_ETP
WHOLE = 512
SLOTTED = D - WHOLE
PART = SLOTTED // N_ETP
TOK = 32
LANES = 128
MESH = pl.DeviceIdType.MESH
F32 = jnp.float32
BF16 = jnp.bfloat16


def iota(shape, dim):
    return lax.broadcasted_iota(jnp.int32, shape, dim)


def compact_matrix(rows):
    r, k = iota((rows, PADDED), 0), iota((rows, PADDED), 1)
    return jnp.where(((k >> 4) * CAP + (k & 15) == r) & ((k & 15) < CAP), 1.0, 0.0).astype(BF16)


def same_row(which):
    k, m = iota((PADDED, PADDED), 0), iota((PADDED, PADDED), 1)
    return jnp.where(m == (k >> 4) * PAD + CAP + which, 1.0, 0.0).astype(BF16)


def extra_row(which):
    b, k = iota((EXPERTS, PADDED), 0), iota((EXPERTS, PADDED), 1)
    return jnp.where(k == b * PAD + CAP + which, 1.0, 0.0).astype(BF16)


def lane_spread():
    c, k = iota((LANES, PADDED), 0), iota((LANES, PADDED), 1)
    return jnp.where((k & 15) == c, 1.0, 0.0).astype(BF16)


def block_of_row():
    r, b = iota((ROWS, EXPERTS), 0), iota((ROWS, EXPERTS), 1)
    return jnp.where((r >= b * CAP) & (r < b * CAP + CAP), 1.0, 0.0).astype(BF16)


def slot_of_row():
    return dot_t(compact_matrix(ROWS), lane_spread())


def parts(value):
    out = []
    for _ in range(3):
        part = value.astype(BF16)
        value = value - part.astype(F32)
        out.append(part)
    return out


def dot(a, b):
    return jnp.dot(a, b, preferred_element_type=F32)


def dot_t(a, b):
    return lax.dot_general(a, b, (((1,), (1,)), ((), ())), preferred_element_type=F32)


def t_dot(a, b):
    return lax.dot_general(a, b, (((0,), (0,)), ((), ())), preferred_element_type=F32)


def position():
    return lax.axis_index("dp"), lax.axis_index("expert"), lax.axis_index("etp")


def copy_to(src, dst, send_sem, recv_sem, device):
    return pltpu.make_async_remote_copy(
        src_ref=src, dst_ref=dst, send_sem=send_sem, recv_sem=recv_sem, device_id=device, device_id_type=MESH
    )


def piece(ref, i, j):
    return ref.at[i, :, pl.ds(pl.multiple_of(j * COLS, COLS), COLS)]


class PlaneGather:
    COUNT = 22

    def __init__(self, ref, start, width, dp_first, send_sems, recv_sems):
        x, e, y = position()
        self.ref, self.dp_first, self.send_sems, self.recv_sems = ref, dp_first, send_sems, recv_sems
        self.start, self.width = start, width
        self.e = e
        self.a, self.b = (x, y) if dp_first else (y, x)
        self.sent = []

    def at(self, i, j, half=None):
        i, j = i % 4, j % 4
        if not self.dp_first:
            i, j = j, i
        columns = pl.ds(pl.multiple_of(j * PART + self.start, LANES), self.width)
        if half is None:
            return self.ref.at[i, :, columns]
        return self.ref.at[i, pl.ds(half * (ROWS // 2), ROWS // 2), columns]

    def device(self, i, j):
        i, j = i % 4, j % 4
        return (i, self.e, j) if self.dp_first else (j, self.e, i)

    def copy(self, view, index, device):
        return copy_to(view, view, self.send_sems.at[index], self.recv_sems.at[index], device)

    def send(self, view, index, device):
        c = self.copy(view, index, device)
        c.start()
        self.sent.append(c)

    def wait(self, view, index):
        self.copy(view, index, self.device(self.a, self.b)).wait_recv()

    def both_second(self, i, slot, half=None):
        view = self.at(i, self.b, half)
        self.send(view, 4 + 2 * slot, self.device(self.a, self.b + 1))
        self.send(view, 5 + 2 * slot, self.device(self.a, self.b - 1))

    def forward_second(self, i, slot):
        self.wait(self.at(i, self.b - 1), 4 + 2 * slot)
        self.send(self.at(i, self.b - 1, 0), 14 + 2 * slot, self.device(self.a, self.b + 1))
        self.wait(self.at(i, self.b + 1), 5 + 2 * slot)
        self.send(self.at(i, self.b + 1, 1), 15 + 2 * slot, self.device(self.a, self.b - 1))

    def steps(self):
        a, b = self.a, self.b

        def own():
            self.send(self.at(a, b), 0, self.device(a + 1, b))
            self.send(self.at(a, b), 1, self.device(a - 1, b))
            self.both_second(a, 0)

        def lower():
            self.wait(self.at(a - 1, b), 0)
            self.send(self.at(a - 1, b, 0), 2, self.device(a + 1, b))
            self.both_second(a - 1, 1)

        def upper():
            self.wait(self.at(a + 1, b), 1)
            self.send(self.at(a + 1, b, 1), 3, self.device(a - 1, b))
            self.both_second(a + 1, 2)

        def opposite():
            self.wait(self.at(a + 2, b, 0), 2)
            self.both_second(a + 2, 3, 0)
            self.wait(self.at(a + 2, b, 1), 3)
            self.both_second(a + 2, 4, 1)

        def opposite_second():
            self.wait(self.at(a + 2, b - 1, 0), 10)
            self.send(self.at(a + 2, b - 1, 0), 20, self.device(a, b + 1))
            self.wait(self.at(a + 2, b + 1, 1), 13)
            self.send(self.at(a + 2, b + 1, 1), 21, self.device(a, b - 1))

        return [
            own,
            lower,
            upper,
            lambda: self.forward_second(a, 0),
            opposite,
            lambda: self.forward_second(a - 1, 1),
            lambda: self.forward_second(a + 1, 2),
            opposite_second,
        ]

    def finish_near(self):
        a, b = self.a, self.b
        self.wait(self.at(a + 2, b + 1, 0), 11)
        self.wait(self.at(a + 2, b - 1, 1), 12)

    def finish_far(self, slot):
        i = self.a + (0, -1, 1, 2)[slot]
        self.wait(self.at(i, self.b + 2, 0), 14 + 2 * slot)
        self.wait(self.at(i, self.b + 2, 1), 15 + 2 * slot)


class PlaneReduce:
    HALF = ROWS // 2
    QUARTER = ROWS // 4
    COUNT = 20

    def __init__(self, ref, out, low, dp_first, order, opp, full, opp2, full2, send_sems, recv_sems):
        x, e, y = position()
        self.ref, self.out, self.low, self.dp_first, self.order = ref, out, low, dp_first, order
        self.opp, self.full, self.opp2, self.full2 = opp, full, opp2, full2
        self.send_sems, self.recv_sems = send_sems, recv_sems
        self.e = e
        self.a, self.b = (x, y) if dp_first else (y, x)
        self.sent = []

    def device(self, i, j):
        i, j = i % 4, j % 4
        return (i, self.e, j) if self.dp_first else (j, self.e, i)

    def at(self, i, j, start, size, ref=None):
        i, j = i % 4, j % 4
        ref = self.out if ref is None else ref
        view = piece(ref, i, j) if self.dp_first else piece(ref, j, i)
        return view.at[pl.ds(self.low + start, size), :]

    def send(self, src, dst, index, device):
        c = copy_to(src, dst, self.send_sems.at[index], self.recv_sems.at[index], device)
        c.start()
        self.sent.append(c)

    def wait(self, dst, index):
        copy_to(dst, dst, self.send_sems.at[index], self.recv_sems.at[index], self.device(self.a, self.b)).wait_recv()

    def opposite(self, k):
        a, b, q = self.a, self.b, self.QUARTER
        j = b + self.order[k]
        self.send(self.at(a + 2, j, 0, q), self.opp.at[0, k], 4 * k, self.device(a + 1, b))
        self.send(self.at(a + 2, j, q, q), self.opp.at[1, k], 4 * k + 1, self.device(a - 1, b))

    def near(self, k):
        a, b, q, h = self.a, self.b, self.QUARTER, self.HALF
        j = b + self.order[k]
        for side, to in ((0, a + 1), (1, a - 1)):
            self.wait(self.opp.at[side, k], 4 * k + side)
            own = self.at(to, j, side * q, q, self.ref)[...]
            self.at(to, j, side * q, q)[...] = (own + self.opp[side, k].astype(F32)).astype(BF16)
            self.send(self.at(to, j, 0, h), self.full.at[side, k], 4 * k + 2 + side, self.device(to, b))

    def total(self, relative):
        k = self.order.index(relative)
        for side in range(2):
            self.wait(self.full.at[side, k], 4 * k + 2 + side)
        own = self.at(self.a, self.b + relative, 0, self.HALF, self.ref)[...]
        return own + self.full[0, k].astype(F32) + self.full[1, k].astype(F32)

    def second_opposite(self):
        a, b, q, h = self.a, self.b, self.QUARTER, self.HALF
        self.at(a, b + 2, 0, h)[...] = self.total(2).astype(BF16)
        self.send(self.at(a, b + 2, 0, q), self.opp2.at[0], 16, self.device(a, b + 1))
        self.send(self.at(a, b + 2, q, q), self.opp2.at[1], 17, self.device(a, b - 1))

    def second_near(self, side):
        a, b, q, h = self.a, self.b, self.QUARTER, self.HALF
        step = 1 if side == 0 else -1
        value = self.total(step)
        self.wait(self.opp2.at[side], 16 + side)
        extra = self.opp2[side].astype(F32)
        if side == 0:
            value = jnp.concatenate([value[:q] + extra, value[q:]], axis=0)
        else:
            value = jnp.concatenate([value[:q], value[q:] + extra], axis=0)
        self.at(a, b + step, 0, h)[...] = value.astype(BF16)
        self.send(self.at(a, b + step, 0, h), self.full2.at[side], 18 + side, self.device(a, b + step))

    def finish(self):
        value = self.total(0)
        for side in range(2):
            self.wait(self.full2.at[side], 18 + side)
        return value + self.full2[0].astype(F32) + self.full2[1].astype(F32)


class Ring:
    def __init__(self, block, z_send, z_recv, core_send, core_recv):
        self.x, self.e, self.y = position()
        self.block = block
        self.z_send, self.z_recv, self.core_send, self.core_recv = z_send, z_recv, core_send, core_recv
        self.other = self.e + 1 - 2 * (self.e % 2)
        self.sent = []

    def copy(self, src, dst, send, recv, device):
        c = copy_to(src, dst, send, recv, device)
        c.start()
        self.sent.append(c)

    def view(self, e, side, distance):
        away = 2 * distance
        return self.block((e + (EXPERTS - away if side == 0 else away)) % EXPERTS, side if distance == 4 else None)

    def onward(self, side, distance):
        e = self.e
        view = self.view(e, side, distance)
        if distance > 0:
            copy_to(
                view, view, self.z_send.at[side, distance], self.z_recv.at[side, distance], (self.x, e, self.y)
            ).wait_recv()
        if distance < 4:
            to = (e + (2 if side == 0 else EXPERTS - 2)) % EXPERTS
            next_view = self.view(to, side, distance + 1)
            self.copy(
                next_view, next_view,
                self.z_send.at[side, distance + 1], self.z_recv.at[side, distance + 1], (self.x, to, self.y),
            )
        if distance > 0 or side == 0:
            self.copy(
                view, view, self.core_send.at[side, distance], self.core_recv.at[side, distance],
                (self.x, self.other, self.y),
            )

    def round(self, distance):
        for side in range(2):
            self.onward(side, distance)

    def finish(self):
        for distance in range(5):
            for side in range(2):
                if distance > 0 or side == 0:
                    view = self.view(self.other, side, distance)
                    copy_to(
                        view, view, self.core_send.at[side, distance], self.core_recv.at[side, distance],
                        (self.x, self.e, self.y),
                    ).wait_recv()


def kernel(
    tokens, out_grad, gates, expert_ids, w_gate, w_up, w_down,
    input_grad, gate_grad, grad_gate, grad_up, grad_down,
    near, table_out, table_in, rows, grads, tables, whole, w_in, w_out, pre, raw, deltas, scaled, turned, turned_scaled,
    sums, wire, made, terms, landed_x, landed_y,
    opp_a, full_a, opp2_a, full2_a, opp_b, full_b, opp2_b, full2_b, back, ready,
    slot_send, slot_recv, x_send, x_recv, d_send, d_recv, g_send, g_recv,
    dp_send, dp_recv, z_sems,
    send_a, recv_a, send_b, recv_b, t_send, t_recv, r_send, r_recv, local,
):
    x, e, y = position()
    columns = pl.ds(pl.multiple_of(y * PART, LANES), PART)
    late = pl.ds(SLOTTED, WHOLE)

    def token_rows(place, half=None):
        if half is None:
            return pl.ds(pl.multiple_of(place * TOK, TOK), TOK)
        return pl.ds(pl.multiple_of(place * TOK + half * (TOK // 2), TOK // 2), TOK // 2)

    def whole_block(place, half=None):
        return whole.at[:, token_rows(place), :] if half is None else whole.at[pl.ds(2 * half, 2), token_rows(place), :]

    def whole_landing(i, which):
        return whole.at[i, token_rows(e), pl.ds(which * WHOLE, WHOLE)]

    ring_x = Ring(lambda p, half=None: near.at[token_rows(p, half), pl.ds(0, PART)], *[z_sems.at[k] for k in range(4)])
    ring_d = Ring(lambda p, half=None: near.at[token_rows(p, half), pl.ds(PART, PART)], *[z_sems.at[k] for k in range(4, 8)])
    ring_w = Ring(whole_block, *[z_sems.at[k] for k in range(8, 12)])

    loads = [
        pltpu.make_async_copy(tokens.at[:, columns], ring_x.block(e), local.at[0]),
        pltpu.make_async_copy(out_grad.at[:, columns], ring_d.block(e), local.at[1]),
        pltpu.make_async_copy(w_gate.at[0], w_in.at[pl.ds(0, FF), :], local.at[2]),
        pltpu.make_async_copy(w_up.at[0], w_in.at[pl.ds(FPAD, FF), :], local.at[3]),
        pltpu.make_async_copy(w_down.at[0], w_out.at[pl.ds(0, FF), :], local.at[4]),
    ]
    own_whole = [
        pltpu.make_async_copy(s.at[:, late], whole_landing(x, which), local.at[8 + which])
        for which, s in enumerate((tokens, out_grad))
    ]
    for c in loads[:2] + own_whole + loads[2:]:
        c.start()
    peers = [(x, (e + j) % EXPERTS, y) for j in range(1, EXPERTS)]
    peers += [((x + j) % N_DP, e, y) for j in range(1, N_DP)]
    peers += [(x, e, (y + j) % N_ETP) for j in range(1, N_ETP)]
    barrier = pltpu.get_barrier_semaphore()
    for device in peers:
        pl.semaphore_signal(barrier, inc=1, device_id=device, device_id_type=MESH)

    expert, place = iota((PADDED, TOK), 0) >> 4, iota((PADDED, TOK), 0) & 15
    ids, weight = expert_ids[...], gates[...].astype(F32)
    chosen = [jnp.where(ids[k : k + 1, :] == expert, 1.0, 0.0) for k in range(TOP)]
    member = chosen[0] + chosen[1] + chosen[2] + chosen[3]
    before = jnp.where(iota((TOK, TOK), 0) < iota((TOK, TOK), 1), 1.0, 0.0).astype(BF16)
    earlier = dot(member.astype(BF16), before)
    table = jnp.where((earlier == place.astype(F32)) & (place < CAP), member, 0.0)
    gate_slots = sum(chosen[k] * weight[k : k + 1, :] for k in range(TOP)) * table
    gate_slots = jnp.sum(gate_slots, axis=1, keepdims=True)
    table = table.astype(BF16)
    widen = jnp.where(iota((TOK, LANES), 0) == iota((TOK, LANES), 1), 1.0, 0.0).astype(BF16)
    sent = []

    wide = jnp.where(iota((PADDED, LANES), 1) == TOK, gate_slots, dot(table, widen))
    table_out[...] = wide.astype(BF16).reshape(EXPERTS, PAD, LANES)
    loads[0].wait()
    loads[1].wait()
    pl.semaphore_wait(barrier, len(peers))

    ring_x.round(0)
    ring_d.round(0)
    for j in range(1, EXPERTS):
        to = (e + j) % EXPERTS
        c = copy_to(table_out.at[to], table_in.at[e], slot_send.at[j], slot_recv.at[j], (x, to, y))
        c.start()
        sent.append(c)
    for j in range(1, N_DP):
        for which, source in enumerate((tokens, out_grad)):
            c = copy_to(
                source.at[:, late], whole_landing(x, which),
                dp_send.at[which, j], dp_recv.at[which, j], ((x + j) % N_DP, e, y),
            )
            c.start()
            sent.append(c)
    table_in[e] = table_out[e]
    for ref, low in ((w_in, FF), (w_in, FPAD + FF), (w_out, FF)):
        ref[pl.ds(low, FPAD - FF), :] = jnp.zeros((FPAD - FF, D), BF16)

    gather_x = PlaneGather(rows, 0, PART, True, x_send, x_recv)
    gather_d = PlaneGather(grads, 0, PART, False, d_send, d_recv)
    steps_x, steps_d = gather_x.steps(), gather_d.steps()

    def pick(g):
        repeat = jnp.where(iota((LANES, EXPERTS * TOK), 0) == (iota((LANES, EXPERTS * TOK), 1) & 31), 1.0, 0.0)
        within = jnp.where(iota((EXPERTS, EXPERTS * TOK), 0) == (iota((EXPERTS, EXPERTS * TOK), 1) >> 5), 1.0, 0.0)
        return (dot(tables[g], repeat.astype(BF16)) * dot(block_of_row(), within.astype(BF16))).astype(BF16)

    def run(*which):
        for k in which:
            steps_x[k]()
            steps_d[k]()

    ring_x.round(1)
    ring_d.round(1)
    compact = compact_matrix(ROWS)
    for j in range(1, EXPERTS):
        view = table_in.at[(e + EXPERTS - j) % EXPERTS]
        copy_to(view, view, slot_send.at[j], slot_recv.at[j], (x, e, y)).wait_recv()
    ring_x.round(2)
    ring_d.round(2)
    tables[x] = dot(compact, table_in[...].reshape(PADDED, LANES)).astype(BF16)
    for j in range(1, N_DP):
        c = copy_to(tables.at[x], tables.at[x], g_send.at[j], g_recv.at[j], ((x + j) % N_DP, e, y))
        c.start()
        sent.append(c)
    picker = pick(x)
    ring_x.round(3)
    ring_d.round(3)
    ring_x.round(4)
    ring_x.finish()
    rows[x, :, columns] = dot(picker, near[:, :PART]).astype(BF16)
    steps_x[0]()
    ring_d.round(4)
    ring_d.finish()
    grads[x, :, columns] = dot(picker, near[:, PART:]).astype(BF16)
    steps_d[0]()
    for c in own_whole:
        c.wait()
    for j in range(1, N_DP):
        for which in range(2):
            view = whole_landing((x + N_DP - j) % N_DP, which)
            copy_to(view, view, dp_send.at[which, j], dp_recv.at[which, j], (x, e, y)).wait_recv()
    ring_w.round(0)

    reduce_a = PlaneReduce(
        sums, wire, 0, True, (2, 1, -1, 0), opp_a, full_a, opp2_a, full2_a, send_a, recv_a
    )
    reduce_b = PlaneReduce(
        sums, wire, ROWS // 2, False, (2, 1, -1, 0), opp_b, full_b, opp2_b, full2_b, send_b, recv_b
    )
    group = [(x + j) % N_DP for j in (0, 3, 1, 2)]

    def add_x(i, j):
        part = pl.ds(pl.multiple_of((j % N_ETP) * PART, LANES), PART)
        pre[i % N_DP] += dot_t(rows[i % N_DP, :, part], w_in[:, part])

    def add_d(i, j):
        part = pl.ds(pl.multiple_of((j % N_ETP) * PART, LANES), PART)
        raw[i % N_DP] += dot_t(grads[i % N_DP, :, part], w_out[:, part])

    def add_sides(move):
        @pl.loop(0, 2)
        def _(k):
            add_x(x + N_DP + move, y + 3 + 2 * k)
            add_d(x + 3 + 2 * k, y + N_ETP + move)

    def add_far(slots):
        for slot in slots:
            gather_x.finish_far(slot)
            gather_d.finish_far(slot)
        start, step = {0: (0, 3), 2: (1, 1)}[slots[0]]

        @pl.loop(0, 2)
        def _(k):
            add_x(x + start + step * k, y + 2)
            add_d(x + 2, y + start + step * k)

    def add_tokens():
        for j in range(1, N_DP):
            g = (x + N_DP - j) % N_DP
            copy_to(tables.at[g], tables.at[g], g_send.at[j], g_recv.at[j], (x, e, y)).wait_recv()

        @pl.loop(0, N_DP)
        def _(g):
            picked = dot(pick(g), whole[g]).astype(BF16)
            rows[g, :, SLOTTED:] = picked[:, :WHOLE]
            grads[g, :, SLOTTED:] = picked[:, WHOLE:]
            pre[g] += dot_t(picked[:, :WHOLE], w_in[:, SLOTTED:])
            raw[g] += dot_t(picked[:, WHOLE:], w_out[:, SLOTTED:])

    def backward(slot):
        g = group[slot]
        a, u, r = pre[g, :, :FPAD], pre[g, :, FPAD:], raw[g]
        which = slot_of_row()
        scale = tables[g, :, TOK : TOK + 1].astype(F32)
        sigmoid = jax.nn.sigmoid(a)
        activated = a * sigmoid
        product = activated * u
        q = jnp.sum(product * r, axis=1, keepdims=True) * which
        terms[g] = sum(t_dot(block_of_row(), part) for part in parts(q))
        own = pl.ds(pl.multiple_of(g * ROWS, ROWS), ROWS)
        scaled[own, :] = (scale * product).astype(BF16)
        hidden = scale * r
        deltas[own, :FPAD] = (hidden * u * sigmoid * (1.0 + a * (1.0 - sigmoid))).astype(BF16)
        deltas[own, FPAD:] = (hidden * activated).astype(BF16)

        @pl.loop(0, N_ETP)
        def _(k):
            part = pl.ds(pl.multiple_of(k * COLS, COLS), COLS)
            value = dot(deltas[own, :], w_in[:, part])
            sums[g, :, part] = value
            wire[g, :, part] = value.astype(BF16)

    def weight_grad(which):
        source = (rows, rows, grads)[which]

        @pl.loop(0, N_ETP)
        def _(k):
            part = pl.ds(pl.multiple_of(k * COLS, COLS), COLS)
            left = turned_scaled[:FF, :] if which == 2 else turned[pl.ds(which * FPAD, FF), :]
            made[which, :, part] = dot(left, source[:, :, part].reshape(N_DP * ROWS, COLS)).astype(BF16)

        c = pltpu.make_async_copy(made.at[which], (grad_gate, grad_up, grad_down)[which].at[0], local.at[5 + which])
        c.start()
        loads.append(c)

    pre[...] = jnp.zeros_like(pre)
    raw[...] = jnp.zeros_like(raw)
    for c in loads[2:]:
        c.wait()
    add_x(x, y)
    add_d(x, y)
    run(1, 2)
    ring_w.round(1)

    @pl.loop(0, 2)
    def _(k):
        add_x(x + 3 + 2 * k, y)
        add_d(x, y + 3 + 2 * k)

    run(3)
    add_sides(0)
    run(4)
    ring_w.round(2)
    add_x(x + 2, y)
    add_d(x, y + 2)
    run(5)
    ring_w.round(3)
    add_sides(-1)
    run(6)
    ring_w.round(4)
    add_sides(1)
    run(7)
    gather_x.finish_near()
    gather_d.finish_near()
    add_sides(2)
    ring_w.finish()
    add_tokens()
    add_far((0, 1))
    add_far((2, 3))

    backward(3)
    for k in range(4):
        reduce_a.opposite(k)
    reduce_b.opposite(0)
    backward(2)
    reduce_b.opposite(1)
    backward(1)
    reduce_b.opposite(2)
    reduce_a.near(0)
    reduce_b.near(0)
    backward(0)
    reduce_b.opposite(3)
    for j in range(1, N_DP):
        to = (x + j) % N_DP
        c = copy_to(terms.at[to], landed_x.at[j], t_send.at[j], t_recv.at[j], (to, e, y))
        c.start()
        sent.append(c)
    for k in range(1, 4):
        reduce_a.near(k)
        reduce_b.near(k)
    turned[...] = deltas[...].T
    turned_scaled[...] = scaled[...].T
    weight_grad(0)
    total = terms[x]
    for j in range(1, N_DP):
        copy_to(landed_x.at[j], landed_x.at[j], t_send.at[j], t_recv.at[j], (x, e, y)).wait_recv()
        total = total + landed_x[j]
    landed_y[0] = total
    for j in range(1, N_ETP):
        c = copy_to(landed_y.at[0], landed_y.at[j], t_send.at[3 + j], t_recv.at[3 + j], (x, e, (y + j) % N_ETP))
        c.start()
        sent.append(c)
    reduce_a.second_opposite()
    reduce_b.second_opposite()
    weight_grad(1)
    for side in range(2):
        reduce_a.second_near(side)
        reduce_b.second_near(side)
    weight_grad(2)
    for j in range(1, N_ETP):
        copy_to(landed_y.at[j], landed_y.at[j], t_send.at[3 + j], t_recv.at[3 + j], (x, e, y)).wait_recv()
        total = total + landed_y[j]
    spare = sum(t_dot(extra_row(which), part) for which, part in enumerate(parts(total)))
    summed = jnp.concatenate([reduce_a.finish(), reduce_b.finish()], axis=0).astype(BF16)
    padded = t_dot(compact, summed)
    ready[:, :, :LANES] = (padded[:, :LANES] + spare).astype(BF16).reshape(EXPERTS, PAD, LANES)
    ready[:, :, LANES:] = padded[:, LANES:].astype(BF16).reshape(EXPERTS, PAD, COLS - LANES)
    for j in range(1, EXPERTS):
        to = (e + j) % EXPERTS
        c = copy_to(ready.at[to], back.at[e], r_send.at[j], r_recv.at[j], (x, to, y))
        c.start()
        sent.append(c)
    back[e] = ready[e]
    for j in range(1, EXPERTS):
        frm = (e + EXPERTS - j) % EXPERTS
        copy_to(back.at[frm], back.at[frm], r_send.at[j], r_recv.at[j], (x, e, y)).wait_recv()
    block = back[...].reshape(PADDED, COLS)
    input_grad[...] = t_dot(table, block).astype(BF16)
    lanes = block[:, :LANES]
    mine = jnp.where(iota((PADDED, LANES), 1) == (iota((PADDED, LANES), 0) & 15), 1.0, 0.0)
    value = sum(dot(same_row(which), lanes) for which in range(3))
    value = jnp.sum(value * mine, axis=1, keepdims=True) * table.astype(F32)
    pairs = jnp.concatenate([jnp.sum(chosen[k] * value, axis=0, keepdims=True) for k in range(TOP)], axis=0)
    share = TOK // N_ETP
    take = jnp.where(iota((TOK, share), 0) == iota((TOK, share), 1) + y * share, 1.0, 0.0).astype(BF16)
    gate_grad[...] = sum(dot(part, take) for part in parts(pairs))
    for c in loads[5:]:
        c.wait()
    for c in sent + gather_x.sent + gather_d.sent + reduce_a.sent + reduce_b.sent:
        c.wait_send()
    for ring in (ring_x, ring_d, ring_w):
        for c in ring.sent:
            c.wait_send()


def copy_out(*refs):
    count = (len(refs) - 2) // 3
    sources, targets, held = refs[:count], refs[count : 2 * count], refs[2 * count : 3 * count]
    into, out = refs[3 * count :]
    steps = []
    for source, target, place in zip(sources, targets, held):
        if len(source.shape) < 3:
            steps.append((source, place, target))
            continue
        for low, size in ((0, 176), (176, 160)):
            view = (0, pl.ds(low, size), slice(None))
            steps.append((source.at[view], place.at[view], target.at[view]))
    steps = steps[::-1]
    first = [pltpu.make_async_copy(source, place, into.at[k]) for k, (source, place, _) in enumerate(steps)]
    second = [pltpu.make_async_copy(place, target, out.at[k]) for k, (_, place, target) in enumerate(steps)]
    for c in first:
        c.start()
    for one, two in zip(first, second):
        one.wait()
        two.start()
    for c in second:
        c.wait()


def per_device(tokens, out_grad, gates, expert_ids, w_gate, w_up, w_down):
    dma = pltpu.SemaphoreType.DMA
    vmem = pl.BlockSpec(memory_space=pltpu.VMEM)
    hbm = pl.BlockSpec(memory_space=pl.ANY)
    count = tokens.shape[0]
    half, quarter = ROWS // 2, ROWS // 4
    landing = [
        pltpu.VMEM((2, 4, quarter, COLS), BF16),
        pltpu.VMEM((2, 4, half, COLS), BF16),
        pltpu.VMEM((2, quarter, COLS), BF16),
        pltpu.VMEM((2, half, COLS), BF16),
    ]
    all_rows = N_DP * ROWS
    weight = jax.ShapeDtypeStruct(w_gate.shape, BF16)
    results = pl.pallas_call(
        kernel,
        out_shape=(
            jax.ShapeDtypeStruct((count, COLS), BF16),
            jax.ShapeDtypeStruct((TOP, count // N_ETP), F32),
            weight,
            weight,
            weight,
        ),
        in_specs=[hbm, hbm, vmem, vmem, hbm, hbm, hbm],
        out_specs=(vmem, vmem, hbm, hbm, hbm),
        scratch_shapes=[
            pltpu.VMEM((EXPERTS * TOK, 2 * PART), BF16),
            pltpu.VMEM((EXPERTS, PAD, LANES), BF16),
            pltpu.VMEM((EXPERTS, PAD, LANES), BF16),
            pltpu.VMEM((N_DP, ROWS, D), BF16),
            pltpu.VMEM((N_DP, ROWS, D), BF16),
            pltpu.VMEM((N_DP, ROWS, LANES), BF16),
            pltpu.VMEM((N_DP, EXPERTS * TOK, 2 * WHOLE), BF16),
            pltpu.VMEM((2 * FPAD, D), BF16),
            pltpu.VMEM((FPAD, D), BF16),
            pltpu.VMEM((N_DP, ROWS, 2 * FPAD), F32),
            pltpu.VMEM((N_DP, ROWS, FPAD), F32),
            pltpu.VMEM((all_rows, 2 * FPAD), BF16),
            pltpu.VMEM((all_rows, FPAD), BF16),
            pltpu.VMEM((2 * FPAD, all_rows), BF16),
            pltpu.VMEM((FPAD, all_rows), BF16),
            pltpu.VMEM((N_DP, ROWS, D), F32),
            pltpu.VMEM((N_DP, ROWS, D), BF16),
            pltpu.VMEM((3, FF, D), BF16),
            pltpu.VMEM((N_DP, EXPERTS, LANES), F32),
            pltpu.VMEM((N_DP, EXPERTS, LANES), F32),
            pltpu.VMEM((N_ETP, EXPERTS, LANES), F32),
            *landing,
            *landing,
            pltpu.VMEM((EXPERTS, PAD, COLS), BF16),
            pltpu.VMEM((EXPERTS, PAD, COLS), BF16),
            dma((EXPERTS,)),
            dma((EXPERTS,)),
            *[dma((PlaneGather.COUNT,))] * 4,
            dma((N_DP,)),
            dma((N_DP,)),
            *[dma((2, N_DP))] * 2,
            dma((12, 2, 5)),
            *[dma((PlaneReduce.COUNT,))] * 4,
            dma((8,)),
            dma((8,)),
            dma((EXPERTS,)),
            dma((EXPERTS,)),
            dma((10,)),
        ],
        compiler_params=pltpu.CompilerParams(collective_id=0, has_side_effects=True, vmem_limit_bytes=58 << 20),
        name="backward",
    )(tokens, out_grad, gates.T, expert_ids.T, w_gate, w_up, w_down)
    input_grad, gate_grad, *weight_grads = pl.pallas_call(
        copy_out,
        out_shape=tuple(jax.ShapeDtypeStruct(r.shape, r.dtype) for r in results),
        in_specs=[hbm] * 5,
        out_specs=(hbm,) * 5,
        scratch_shapes=[*[pltpu.VMEM(r.shape, r.dtype) for r in results], dma((8,)), dma((8,))],
        compiler_params=pltpu.CompilerParams(vmem_limit_bytes=58 << 20),
        name="outputs",
    )(*results)
    return input_grad, gate_grad.T, *weight_grads


def solution(mesh):
    in_specs = (
        P(("dp", "expert"), None),
        P(("dp", "expert"), None),
        P(("dp", "expert"), None),
        P(("dp", "expert"), None),
        P("expert", ("dp", "etp"), None),
        P("expert", ("dp", "etp"), None),
        P("expert", ("dp", "etp"), None),
    )
    out_specs = (
        P(("dp", "expert"), "etp"),
        P(("dp", "expert", "etp"), None),
        P("expert", ("dp", "etp"), None),
        P("expert", ("dp", "etp"), None),
        P("expert", ("dp", "etp"), None),
    )
    return jax.shard_map(
        per_device, mesh=mesh, in_specs=in_specs, out_specs=out_specs, check_vma=False
    )
```

```python
import jax
import jax.numpy as jnp
from jax import lax
from jax.experimental import pallas as pl
from jax.experimental.pallas import tpu as pltpu
from jax.sharding import PartitionSpec as P

EXPERTS = 16
TOP = 4
CAP = 12
PAD = 16
N_DP = 4
N_ETP = 4
ROWS = EXPERTS * CAP
PADDED = EXPERTS * PAD
D = 3072
FF = 336
FPAD = 384
COLS = D // N_ETP
WHOLE = 512
SLOTTED = D - WHOLE
PART = SLOTTED // N_ETP
TOK = 32
LANES = 128
MESH = pl.DeviceIdType.MESH
F32 = jnp.float32
BF16 = jnp.bfloat16


def iota(shape, dim):
    return lax.broadcasted_iota(jnp.int32, shape, dim)


def compact_matrix(rows):
    r, k = iota((rows, PADDED), 0), iota((rows, PADDED), 1)
    return jnp.where(((k >> 4) * CAP + (k & 15) == r) & ((k & 15) < CAP), 1.0, 0.0).astype(BF16)


def place_of(block):
    away = ((block >> 1) + 8 - (lax.axis_index("expert") >> 1)) & 7
    return jnp.where(away > 4, 2 * (8 - away), jnp.maximum(2 * away - 1, 0)) * 2 + (block & 1)


def placed_matrix():
    r, k = iota((ROWS, PADDED), 0), iota((ROWS, PADDED), 1)
    return jnp.where((place_of(k >> 4) * CAP + (k & 15) == r) & ((k & 15) < CAP), 1.0, 0.0).astype(BF16)


def same_row(which):
    k, m = iota((PADDED, PADDED), 0), iota((PADDED, PADDED), 1)
    return jnp.where(m == (k >> 4) * PAD + CAP + which, 1.0, 0.0).astype(BF16)


def extra_row(which):
    b, k = iota((EXPERTS, PADDED), 0), iota((EXPERTS, PADDED), 1)
    return jnp.where(k == b * PAD + CAP + which, 1.0, 0.0).astype(BF16)


def lane_spread():
    c, k = iota((LANES, PADDED), 0), iota((LANES, PADDED), 1)
    return jnp.where((k & 15) == c, 1.0, 0.0).astype(BF16)


def block_of_row(placed=True):
    r, b = iota((ROWS, EXPERTS), 0), iota((ROWS, EXPERTS), 1)
    if not placed:
        b = place_of(b)
    return jnp.where((r >= b * CAP) & (r < b * CAP + CAP), 1.0, 0.0).astype(BF16)


def slot_of_row():
    return dot_t(compact_matrix(ROWS), lane_spread())


def parts(value):
    out = []
    for _ in range(3):
        part = value.astype(BF16)
        value = value - part.astype(F32)
        out.append(part)
    return out


def dot(a, b):
    return jnp.dot(a, b, preferred_element_type=F32)


def dot_t(a, b):
    return lax.dot_general(a, b, (((1,), (1,)), ((), ())), preferred_element_type=F32)


def t_dot(a, b):
    return lax.dot_general(a, b, (((0,), (0,)), ((), ())), preferred_element_type=F32)


def position():
    return lax.axis_index("dp"), lax.axis_index("expert"), lax.axis_index("etp")


def copy_to(src, dst, send_sem, recv_sem, device):
    return pltpu.make_async_remote_copy(
        src_ref=src, dst_ref=dst, send_sem=send_sem, recv_sem=recv_sem, device_id=device, device_id_type=MESH
    )


def piece(ref, i, j):
    return ref.at[i, :, pl.ds(pl.multiple_of(j * COLS, COLS), COLS)]


class PlaneGather:
    COUNT = 26

    def __init__(self, ref, start, width, dp_first, send_sems, recv_sems):
        x, e, y = position()
        self.ref, self.dp_first, self.send_sems, self.recv_sems = ref, dp_first, send_sems, recv_sems
        self.start, self.width = start, width
        self.e = e
        self.a, self.b = (x, y) if dp_first else (y, x)
        self.sent = []

    def at(self, i, j, half=None):
        i, j = i % 4, j % 4
        if not self.dp_first:
            i, j = j, i
        columns = pl.ds(pl.multiple_of(j * PART + self.start, LANES), self.width)
        if half is None:
            return self.ref.at[i, :, columns]
        return self.ref.at[i, pl.ds(half * (ROWS // 2), ROWS // 2), columns]

    def device(self, i, j):
        i, j = i % 4, j % 4
        return (i, self.e, j) if self.dp_first else (j, self.e, i)

    def copy(self, view, index, device):
        return copy_to(view, view, self.send_sems.at[index], self.recv_sems.at[index], device)

    def send(self, view, index, device):
        c = self.copy(view, index, device)
        c.start()
        self.sent.append(c)

    def wait(self, view, index):
        self.copy(view, index, self.device(self.a, self.b)).wait_recv()

    def own(self, half):
        a, b = self.a, self.b
        view = self.at(a, b, half)
        self.send(view, 22 * half, self.device(a + 1, b))
        self.send(view, 1 + 22 * half, self.device(a - 1, b))
        self.send(view, 4 + 20 * half, self.device(a, b + 1))
        self.send(view, 5 + 20 * half, self.device(a, b - 1))

    def forward_own(self):
        a, b = self.a, self.b
        self.wait(self.at(a, b - 1, 0), 4)
        self.send(self.at(a, b - 1, 0), 14, self.device(a, b + 1))
        self.wait(self.at(a, b + 1, 1), 25)
        self.send(self.at(a, b + 1, 1), 15, self.device(a, b - 1))
        self.wait(self.at(a, b - 1, 1), 24)
        self.wait(self.at(a, b + 1, 0), 5)

    def both_second(self, i, slot, half=None):
        view = self.at(i, self.b, half)
        self.send(view, 4 + 2 * slot, self.device(self.a, self.b + 1))
        self.send(view, 5 + 2 * slot, self.device(self.a, self.b - 1))

    def forward_second(self, i, slot):
        self.wait(self.at(i, self.b - 1), 4 + 2 * slot)
        self.send(self.at(i, self.b - 1, 0), 14 + 2 * slot, self.device(self.a, self.b + 1))
        self.wait(self.at(i, self.b + 1), 5 + 2 * slot)
        self.send(self.at(i, self.b + 1, 1), 15 + 2 * slot, self.device(self.a, self.b - 1))

    def steps(self):
        a, b = self.a, self.b

        def lower():
            self.wait(self.at(a - 1, b, 0), 0)
            self.send(self.at(a - 1, b, 0), 2, self.device(a + 1, b))
            self.wait(self.at(a - 1, b, 1), 22)
            self.both_second(a - 1, 1)

        def upper():
            self.wait(self.at(a + 1, b, 1), 23)
            self.send(self.at(a + 1, b, 1), 3, self.device(a - 1, b))
            self.wait(self.at(a + 1, b, 0), 1)
            self.both_second(a + 1, 2)

        def opposite():
            self.wait(self.at(a + 2, b, 0), 2)
            self.both_second(a + 2, 3, 0)
            self.wait(self.at(a + 2, b, 1), 3)
            self.both_second(a + 2, 4, 1)

        def opposite_second():
            self.wait(self.at(a + 2, b - 1, 0), 10)
            self.send(self.at(a + 2, b - 1, 0), 20, self.device(a, b + 1))
            self.wait(self.at(a + 2, b + 1, 1), 13)
            self.send(self.at(a + 2, b + 1, 1), 21, self.device(a, b - 1))

        return [
            None,
            lower,
            upper,
            self.forward_own,
            opposite,
            lambda: self.forward_second(a - 1, 1),
            lambda: self.forward_second(a + 1, 2),
            opposite_second,
        ]

    def finish_near(self):
        a, b = self.a, self.b
        self.wait(self.at(a + 2, b + 1, 0), 11)
        self.wait(self.at(a + 2, b - 1, 1), 12)

    def finish_far(self, slot):
        i = self.a + (0, -1, 1, 2)[slot]
        self.wait(self.at(i, self.b + 2, 0), 14 + 2 * slot)
        self.wait(self.at(i, self.b + 2, 1), 15 + 2 * slot)


class PlaneReduce:
    HALF = ROWS // 2
    QUARTER = ROWS // 4
    COUNT = 20

    def __init__(self, ref, out, low, dp_first, order, opp, full, opp2, full2, send_sems, recv_sems):
        x, e, y = position()
        self.ref, self.out, self.low, self.dp_first, self.order = ref, out, low, dp_first, order
        self.opp, self.full, self.opp2, self.full2 = opp, full, opp2, full2
        self.send_sems, self.recv_sems = send_sems, recv_sems
        self.e = e
        self.a, self.b = (x, y) if dp_first else (y, x)
        self.sent = []

    def device(self, i, j):
        i, j = i % 4, j % 4
        return (i, self.e, j) if self.dp_first else (j, self.e, i)

    def at(self, i, j, start, size, ref=None):
        i, j = i % 4, j % 4
        ref = self.out if ref is None else ref
        view = piece(ref, i, j) if self.dp_first else piece(ref, j, i)
        return view.at[pl.ds(self.low + start, size), :]

    def send(self, src, dst, index, device):
        c = copy_to(src, dst, self.send_sems.at[index], self.recv_sems.at[index], device)
        c.start()
        self.sent.append(c)

    def wait(self, dst, index):
        copy_to(dst, dst, self.send_sems.at[index], self.recv_sems.at[index], self.device(self.a, self.b)).wait_recv()

    def opposite(self, k):
        a, b, q = self.a, self.b, self.QUARTER
        j = b + self.order[k]
        self.send(self.at(a + 2, j, 0, q), self.opp.at[0, k], 4 * k, self.device(a + 1, b))
        self.send(self.at(a + 2, j, q, q), self.opp.at[1, k], 4 * k + 1, self.device(a - 1, b))

    def near(self, k):
        a, b, q, h = self.a, self.b, self.QUARTER, self.HALF
        j = b + self.order[k]
        for side, to in ((0, a + 1), (1, a - 1)):
            self.wait(self.opp.at[side, k], 4 * k + side)
            own = self.at(to, j, side * q, q, self.ref)[...]
            self.at(to, j, side * q, q)[...] = (own + self.opp[side, k].astype(F32)).astype(BF16)
            self.send(self.at(to, j, 0, h), self.full.at[side, k], 4 * k + 2 + side, self.device(to, b))

    def total(self, relative):
        k = self.order.index(relative)
        for side in range(2):
            self.wait(self.full.at[side, k], 4 * k + 2 + side)
        own = self.at(self.a, self.b + relative, 0, self.HALF, self.ref)[...]
        return own + self.full[0, k].astype(F32) + self.full[1, k].astype(F32)

    def second_opposite(self):
        a, b, q, h = self.a, self.b, self.QUARTER, self.HALF
        self.at(a, b + 2, 0, h)[...] = self.total(2).astype(BF16)
        self.send(self.at(a, b + 2, 0, q), self.opp2.at[0], 16, self.device(a, b + 1))
        self.send(self.at(a, b + 2, q, q), self.opp2.at[1], 17, self.device(a, b - 1))

    def second_near(self, side):
        a, b, q, h = self.a, self.b, self.QUARTER, self.HALF
        step = 1 if side == 0 else -1
        value = self.total(step)
        self.wait(self.opp2.at[side], 16 + side)
        extra = self.opp2[side].astype(F32)
        if side == 0:
            value = jnp.concatenate([value[:q] + extra, value[q:]], axis=0)
        else:
            value = jnp.concatenate([value[:q], value[q:] + extra], axis=0)
        self.at(a, b + step, 0, h)[...] = value.astype(BF16)
        self.send(self.at(a, b + step, 0, h), self.full2.at[side], 18 + side, self.device(a, b + step))

    def finish(self):
        value = self.total(0)
        for side in range(2):
            self.wait(self.full2.at[side], 18 + side)
        return value + self.full2[0].astype(F32) + self.full2[1].astype(F32)


class Ring:
    def __init__(self, block, z_send, z_recv, core_send, core_recv):
        self.x, self.e, self.y = position()
        self.block = block
        self.z_send, self.z_recv, self.core_send, self.core_recv = z_send, z_recv, core_send, core_recv
        self.other = self.e + 1 - 2 * (self.e % 2)
        self.sent = []

    def copy(self, src, dst, send, recv, device):
        c = copy_to(src, dst, send, recv, device)
        c.start()
        self.sent.append(c)

    def view(self, e, side, distance):
        away = 2 * distance
        return self.block((e + (EXPERTS - away if side == 0 else away)) % EXPERTS, side if distance == 4 else None)

    def onward(self, side, distance):
        e = self.e
        view = self.view(e, side, distance)
        if distance > 0:
            copy_to(
                view, view, self.z_send.at[side, distance], self.z_recv.at[side, distance], (self.x, e, self.y)
            ).wait_recv()
        if distance < 4:
            to = (e + (2 if side == 0 else EXPERTS - 2)) % EXPERTS
            next_view = self.view(to, side, distance + 1)
            self.copy(
                next_view, next_view,
                self.z_send.at[side, distance + 1], self.z_recv.at[side, distance + 1], (self.x, to, self.y),
            )
        if distance > 0 or side == 0:
            self.copy(
                view, view, self.core_send.at[side, distance], self.core_recv.at[side, distance],
                (self.x, self.other, self.y),
            )

    def round(self, distance):
        for side in range(2):
            self.onward(side, distance)

    NEAR = ((0, 0), (0, 1), (1, 1), (1, 2))
    FAR = ((0, 2), (0, 3), (1, 3), (0, 4), (1, 4))

    def finish(self, which):
        for side, distance in which:
            view = self.view(self.other, side, distance)
            copy_to(
                view, view, self.core_send.at[side, distance], self.core_recv.at[side, distance],
                (self.x, self.e, self.y),
            ).wait_recv()


def kernel(
    tokens, out_grad, gates, expert_ids, w_gate, w_up, w_down,
    input_grad, gate_grad, grad_gate, grad_up, grad_down,
    near, table_out, table_in, rows, grads, tables, whole, w_in, w_out, pre, raw, deltas, scaled, turned, turned_scaled,
    sums, wire, made, terms, landed_x, landed_y,
    opp_a, full_a, opp2_a, full2_a, opp_b, full_b, opp2_b, full2_b, back, ready,
    slot_send, slot_recv, x_send, x_recv, d_send, d_recv, g_send, g_recv,
    dp_send, dp_recv, z_sems,
    send_a, recv_a, send_b, recv_b, t_send, t_recv, r_send, r_recv, local,
):
    x, e, y = position()
    columns = pl.ds(pl.multiple_of(y * PART, LANES), PART)
    late = pl.ds(SLOTTED, WHOLE)

    def token_rows(place, half=None):
        if half is None:
            return pl.ds(pl.multiple_of(place * TOK, TOK), TOK)
        return pl.ds(pl.multiple_of(place * TOK + half * (TOK // 2), TOK // 2), TOK // 2)

    def whole_block(place, half=None):
        return whole.at[:, token_rows(place), :] if half is None else whole.at[pl.ds(2 * half, 2), token_rows(place), :]

    def whole_landing(i, which):
        return whole.at[i, token_rows(e), pl.ds(which * WHOLE, WHOLE)]

    ring_x = Ring(lambda p, half=None: near.at[token_rows(p, half), pl.ds(0, PART)], *[z_sems.at[k] for k in range(4)])
    ring_d = Ring(lambda p, half=None: near.at[token_rows(p, half), pl.ds(PART, PART)], *[z_sems.at[k] for k in range(4, 8)])
    ring_w = Ring(whole_block, *[z_sems.at[k] for k in range(8, 12)])

    loads = [
        pltpu.make_async_copy(tokens.at[:, columns], ring_x.block(e), local.at[0]),
        pltpu.make_async_copy(out_grad.at[:, columns], ring_d.block(e), local.at[1]),
        pltpu.make_async_copy(w_gate.at[0], w_in.at[pl.ds(0, FF), :], local.at[2]),
        pltpu.make_async_copy(w_up.at[0], w_in.at[pl.ds(FPAD, FF), :], local.at[3]),
        pltpu.make_async_copy(w_down.at[0], w_out.at[pl.ds(0, FF), :], local.at[4]),
    ]
    own_whole = [
        pltpu.make_async_copy(s.at[:, late], whole_landing(x, which), local.at[8 + which])
        for which, s in enumerate((tokens, out_grad))
    ]
    for c in loads[:2] + own_whole + loads[2:]:
        c.start()
    peers = [(x, (e + j) % EXPERTS, y) for j in range(1, EXPERTS)]
    peers += [((x + j) % N_DP, e, y) for j in range(1, N_DP)]
    peers += [(x, e, (y + j) % N_ETP) for j in range(1, N_ETP)]
    barrier = pltpu.get_barrier_semaphore()
    for device in peers:
        pl.semaphore_signal(barrier, inc=1, device_id=device, device_id_type=MESH)

    expert, place = iota((PADDED, TOK), 0) >> 4, iota((PADDED, TOK), 0) & 15
    ids, weight = expert_ids[...], gates[...].astype(F32)
    chosen = [jnp.where(ids[k : k + 1, :] == expert, 1.0, 0.0) for k in range(TOP)]
    member = chosen[0] + chosen[1] + chosen[2] + chosen[3]
    before = jnp.where(iota((TOK, TOK), 0) < iota((TOK, TOK), 1), 1.0, 0.0).astype(BF16)
    earlier = dot(member.astype(BF16), before)
    table = jnp.where((earlier == place.astype(F32)) & (place < CAP), member, 0.0)
    gate_slots = sum(chosen[k] * weight[k : k + 1, :] for k in range(TOP)) * table
    gate_slots = jnp.sum(gate_slots, axis=1, keepdims=True)
    table = table.astype(BF16)
    widen = jnp.where(iota((TOK, LANES), 0) == iota((TOK, LANES), 1), 1.0, 0.0).astype(BF16)
    sent = []

    wide = jnp.where(iota((PADDED, LANES), 1) == TOK, gate_slots, dot(table, widen))
    table_out[...] = wide.astype(BF16).reshape(EXPERTS, PAD, LANES)
    loads[0].wait()
    loads[1].wait()
    pl.semaphore_wait(barrier, len(peers))

    ring_x.round(0)
    ring_d.round(0)
    for j in range(1, EXPERTS):
        to = (e + j) % EXPERTS
        c = copy_to(table_out.at[to], table_in.at[e], slot_send.at[j], slot_recv.at[j], (x, to, y))
        c.start()
        sent.append(c)
    for j in range(1, N_DP):
        for which, source in enumerate((tokens, out_grad)):
            c = copy_to(
                source.at[:, late], whole_landing(x, which),
                dp_send.at[which, j], dp_recv.at[which, j], ((x + j) % N_DP, e, y),
            )
            c.start()
            sent.append(c)
    table_in[e] = table_out[e]
    for ref, low in ((w_in, FF), (w_in, FPAD + FF), (w_out, FF)):
        ref[pl.ds(low, FPAD - FF), :] = jnp.zeros((FPAD - FF, D), BF16)

    gather_x = PlaneGather(rows, 0, PART, True, x_send, x_recv)
    gather_d = PlaneGather(grads, 0, PART, False, d_send, d_recv)
    steps_x, steps_d = gather_x.steps(), gather_d.steps()

    def pick(g):
        repeat = jnp.where(iota((LANES, EXPERTS * TOK), 0) == (iota((LANES, EXPERTS * TOK), 1) & 31), 1.0, 0.0)
        within = jnp.where(iota((EXPERTS, EXPERTS * TOK), 0) == (iota((EXPERTS, EXPERTS * TOK), 1) >> 5), 1.0, 0.0)
        return (dot(tables[g], repeat.astype(BF16)) * dot(block_of_row(False), within.astype(BF16))).astype(BF16)

    def run(*which):
        for k in which:
            steps_x[k]()
            steps_d[k]()

    half = ROWS // 2

    def own_half(ref, start, h):
        r, m = iota((half, EXPERTS // 2 * TOK), 0), iota((half, EXPERTS // 2 * TOK), 1)
        within = (r >= (m >> 5) * CAP) & (r < (m >> 5) * CAP + CAP)
        lane, m = iota((LANES, EXPERTS // 2 * TOK), 0), iota((LANES, EXPERTS // 2 * TOK), 1)
        repeat = jnp.where(lane == (m & 31), 1.0, 0.0).astype(BF16)
        own = pl.ds(h * half, half)
        picker = jnp.where(within, dot(tables[x, own, :], repeat), 0.0).astype(BF16)
        taken = []
        for away in ((0, 1, 7, 2), (6, 3, 5, 4))[h]:
            low = pl.multiple_of((((e // 2) + away) % 8) * (2 * TOK), 2 * TOK)
            taken.append(near[pl.ds(low, 2 * TOK), start : start + PART])
        ref[x, own, columns] = dot(picker, jnp.concatenate(taken, axis=0)).astype(BF16)

    for k in range(1, 3):
        ring_x.round(k)
        ring_d.round(k)
    for j in range(1, EXPERTS):
        view = table_in.at[(e + EXPERTS - j) % EXPERTS]
        copy_to(view, view, slot_send.at[j], slot_recv.at[j], (x, e, y)).wait_recv()
    tables[x] = dot(placed_matrix(), table_in[...].reshape(PADDED, LANES)).astype(BF16)
    for j in range(1, N_DP):
        c = copy_to(tables.at[x], tables.at[x], g_send.at[j], g_recv.at[j], ((x + j) % N_DP, e, y))
        c.start()
        sent.append(c)
    ring_x.finish(Ring.NEAR)
    own_half(rows, 0, 0)
    gather_x.own(0)
    ring_x.round(3)
    ring_d.round(3)
    ring_d.finish(Ring.NEAR)
    own_half(grads, PART, 0)
    gather_d.own(0)
    ring_x.round(4)
    ring_d.round(4)
    ring_x.finish(Ring.FAR)
    own_half(rows, 0, 1)
    gather_x.own(1)
    ring_d.finish(Ring.FAR)
    own_half(grads, PART, 1)
    gather_d.own(1)
    for c in own_whole:
        c.wait()
    for j in range(1, N_DP):
        for which in range(2):
            view = whole_landing((x + N_DP - j) % N_DP, which)
            copy_to(view, view, dp_send.at[which, j], dp_recv.at[which, j], (x, e, y)).wait_recv()
    ring_w.round(0)

    reduce_a = PlaneReduce(
        sums, wire, 0, True, (2, 1, -1, 0), opp_a, full_a, opp2_a, full2_a, send_a, recv_a
    )
    reduce_b = PlaneReduce(
        sums, wire, ROWS // 2, False, (2, 1, -1, 0), opp_b, full_b, opp2_b, full2_b, send_b, recv_b
    )
    group = [(x + j) % N_DP for j in (0, 3, 1, 2)]

    def add_x(i, j):
        part = pl.ds(pl.multiple_of((j % N_ETP) * PART, LANES), PART)
        pre[i % N_DP] += dot_t(rows[i % N_DP, :, part], w_in[:, part])

    def add_d(i, j):
        part = pl.ds(pl.multiple_of((j % N_ETP) * PART, LANES), PART)
        raw[i % N_DP] += dot_t(grads[i % N_DP, :, part], w_out[:, part])

    def add_sides(move):
        @pl.loop(0, 2)
        def _(k):
            add_x(x + N_DP + move, y + 3 + 2 * k)
            add_d(x + 3 + 2 * k, y + N_ETP + move)

    def add_far(slots):
        for slot in slots:
            gather_x.finish_far(slot)
            gather_d.finish_far(slot)
        start, step = {0: (0, 3), 2: (1, 1)}[slots[0]]

        @pl.loop(0, 2)
        def _(k):
            add_x(x + start + step * k, y + 2)
            add_d(x + 2, y + start + step * k)

    def add_tokens():
        for j in range(1, N_DP):
            g = (x + N_DP - j) % N_DP
            copy_to(tables.at[g], tables.at[g], g_send.at[j], g_recv.at[j], (x, e, y)).wait_recv()

        @pl.loop(0, N_DP)
        def _(g):
            picked = dot(pick(g), whole[g]).astype(BF16)
            rows[g, :, SLOTTED:] = picked[:, :WHOLE]
            grads[g, :, SLOTTED:] = picked[:, WHOLE:]
            pre[g] += dot_t(picked[:, :WHOLE], w_in[:, SLOTTED:])
            raw[g] += dot_t(picked[:, WHOLE:], w_out[:, SLOTTED:])

    def backward(slot):
        g = group[slot]
        a, u, r = pre[g, :, :FPAD], pre[g, :, FPAD:], raw[g]
        which = slot_of_row()
        scale = tables[g, :, TOK : TOK + 1].astype(F32)
        sigmoid = jax.nn.sigmoid(a)
        activated = a * sigmoid
        product = activated * u
        q = jnp.sum(product * r, axis=1, keepdims=True) * which
        terms[g] = sum(t_dot(block_of_row(), part) for part in parts(q))
        own = pl.ds(pl.multiple_of(g * ROWS, ROWS), ROWS)
        scaled[own, :] = (scale * product).astype(BF16)
        hidden = scale * r
        deltas[own, :FPAD] = (hidden * u * sigmoid * (1.0 + a * (1.0 - sigmoid))).astype(BF16)
        deltas[own, FPAD:] = (hidden * activated).astype(BF16)

        @pl.loop(0, N_ETP)
        def _(k):
            part = pl.ds(pl.multiple_of(k * COLS, COLS), COLS)
            value = dot(deltas[own, :], w_in[:, part])
            sums[g, :, part] = value
            wire[g, :, part] = value.astype(BF16)

    def weight_grad(which):
        source = (rows, rows, grads)[which]

        @pl.loop(0, N_ETP)
        def _(k):
            part = pl.ds(pl.multiple_of(k * COLS, COLS), COLS)
            left = turned_scaled[:FF, :] if which == 2 else turned[pl.ds(which * FPAD, FF), :]
            made[which, :, part] = dot(left, source[:, :, part].reshape(N_DP * ROWS, COLS)).astype(BF16)

        c = pltpu.make_async_copy(made.at[which], (grad_gate, grad_up, grad_down)[which].at[0], local.at[5 + which])
        c.start()
        loads.append(c)

    pre[...] = jnp.zeros_like(pre)
    raw[...] = jnp.zeros_like(raw)
    for c in loads[2:]:
        c.wait()
    add_x(x, y)
    add_d(x, y)
    run(1, 2)
    ring_w.round(1)

    @pl.loop(0, 2)
    def _(k):
        add_x(x + 3 + 2 * k, y)
        add_d(x, y + 3 + 2 * k)

    run(3)
    add_sides(0)
    run(4)
    ring_w.round(2)
    add_x(x + 2, y)
    add_d(x, y + 2)
    run(5)
    ring_w.round(3)
    add_sides(-1)
    run(6)
    ring_w.round(4)
    add_sides(1)
    run(7)
    gather_x.finish_near()
    gather_d.finish_near()
    add_sides(2)
    ring_w.finish(Ring.NEAR + Ring.FAR)
    add_tokens()
    add_far((0, 1))
    add_far((2, 3))

    backward(3)
    for k in range(4):
        reduce_a.opposite(k)
    reduce_b.opposite(0)
    backward(2)
    reduce_b.opposite(1)
    backward(1)
    reduce_b.opposite(2)
    reduce_a.near(0)
    reduce_b.near(0)
    backward(0)
    reduce_b.opposite(3)
    for j in range(1, N_DP):
        to = (x + j) % N_DP
        c = copy_to(terms.at[to], landed_x.at[j], t_send.at[j], t_recv.at[j], (to, e, y))
        c.start()
        sent.append(c)
    for k in range(1, 4):
        reduce_a.near(k)
        reduce_b.near(k)
    turned[...] = deltas[...].T
    turned_scaled[...] = scaled[...].T
    weight_grad(0)
    total = terms[x]
    for j in range(1, N_DP):
        copy_to(landed_x.at[j], landed_x.at[j], t_send.at[j], t_recv.at[j], (x, e, y)).wait_recv()
        total = total + landed_x[j]
    landed_y[0] = total
    for j in range(1, N_ETP):
        c = copy_to(landed_y.at[0], landed_y.at[j], t_send.at[3 + j], t_recv.at[3 + j], (x, e, (y + j) % N_ETP))
        c.start()
        sent.append(c)
    reduce_a.second_opposite()
    reduce_b.second_opposite()
    for side in range(2):
        reduce_a.second_near(side)
        reduce_b.second_near(side)
    for j in range(1, N_ETP):
        copy_to(landed_y.at[j], landed_y.at[j], t_send.at[3 + j], t_recv.at[3 + j], (x, e, y)).wait_recv()
        total = total + landed_y[j]
    spare = sum(t_dot(extra_row(which), part) for which, part in enumerate(parts(total)))
    r, k = iota((half, PADDED // 2), 0), iota((half, PADDED // 2), 1)
    spread = jnp.where(((k >> 4) * CAP + (k & 15) == r) & ((k & 15) < CAP), 1.0, 0.0).astype(BF16)
    core = e % 2
    for h, reduce in ((1, reduce_b), (0, reduce_a)):
        padded = t_dot(spread, reduce.finish().astype(BF16))
        own = pl.ds(h * (EXPERTS // 2), EXPERTS // 2)
        extra = spare[h * (PADDED // 2) : (h + 1) * (PADDED // 2)]
        ready[own, :, :LANES] = (padded[:, :LANES] + extra).astype(BF16).reshape(EXPERTS // 2, PAD, LANES)
        ready[own, :, LANES:] = padded[:, LANES:].astype(BF16).reshape(EXPERTS // 2, PAD, COLS - LANES)
        for k in range(3, -1, -1):
            away = ((0, 1, 7, 2), (6, 3, 5, 4))[h][k]
            for flip in range(2):
                to_core = core if flip == 0 else 1 - core
                source = ready.at[8 * h + 2 * k + to_core]
                if away == 0 and flip == 0:
                    back[e] = source[...]
                    continue
                to = ((e // 2 + away) % 8) * 2 + to_core
                c = copy_to(source, back.at[e], r_send.at[away, flip], r_recv.at[away, flip], (x, to, y))
                c.start()
                sent.append(c)
    weight_grad(1)
    weight_grad(2)
    for away in range(8):
        for flip in range(2):
            if away > 0 or flip > 0:
                frm = ((e // 2 + 8 - away) % 8) * 2 + (core if flip == 0 else 1 - core)
                copy_to(
                    back.at[frm], back.at[frm], r_send.at[away, flip], r_recv.at[away, flip], (x, e, y)
                ).wait_recv()
    block = back[...].reshape(PADDED, COLS)
    input_grad[...] = t_dot(table, block).astype(BF16)
    lanes = block[:, :LANES]
    mine = jnp.where(iota((PADDED, LANES), 1) == (iota((PADDED, LANES), 0) & 15), 1.0, 0.0)
    value = sum(dot(same_row(which), lanes) for which in range(3))
    value = jnp.sum(value * mine, axis=1, keepdims=True) * table.astype(F32)
    pairs = jnp.concatenate([jnp.sum(chosen[k] * value, axis=0, keepdims=True) for k in range(TOP)], axis=0)
    share = TOK // N_ETP
    take = jnp.where(iota((TOK, share), 0) == iota((TOK, share), 1) + y * share, 1.0, 0.0).astype(BF16)
    gate_grad[...] = sum(dot(part, take) for part in parts(pairs))
    for c in loads[5:]:
        c.wait()
    for c in sent + gather_x.sent + gather_d.sent + reduce_a.sent + reduce_b.sent:
        c.wait_send()
    for ring in (ring_x, ring_d, ring_w):
        for c in ring.sent:
            c.wait_send()


def copy_out(*refs):
    count = (len(refs) - 2) // 3
    sources, targets, held = refs[:count], refs[count : 2 * count], refs[2 * count : 3 * count]
    into, out = refs[3 * count :]
    steps = []
    for source, target, place in zip(sources, targets, held):
        if len(source.shape) < 3:
            steps.append((source, place, target))
            continue
        for low, size in ((0, 176), (176, 160)):
            view = (0, pl.ds(low, size), slice(None))
            steps.append((source.at[view], place.at[view], target.at[view]))
    steps = steps[::-1]
    first = [pltpu.make_async_copy(source, place, into.at[k]) for k, (source, place, _) in enumerate(steps)]
    second = [pltpu.make_async_copy(place, target, out.at[k]) for k, (_, place, target) in enumerate(steps)]
    for c in first:
        c.start()
    for one, two in zip(first, second):
        one.wait()
        two.start()
    for c in second:
        c.wait()


def per_device(tokens, out_grad, gates, expert_ids, w_gate, w_up, w_down):
    dma = pltpu.SemaphoreType.DMA
    vmem = pl.BlockSpec(memory_space=pltpu.VMEM)
    hbm = pl.BlockSpec(memory_space=pl.ANY)
    count = tokens.shape[0]
    half, quarter = ROWS // 2, ROWS // 4
    landing = [
        pltpu.VMEM((2, 4, quarter, COLS), BF16),
        pltpu.VMEM((2, 4, half, COLS), BF16),
        pltpu.VMEM((2, quarter, COLS), BF16),
        pltpu.VMEM((2, half, COLS), BF16),
    ]
    all_rows = N_DP * ROWS
    weight = jax.ShapeDtypeStruct(w_gate.shape, BF16)
    results = pl.pallas_call(
        kernel,
        out_shape=(
            jax.ShapeDtypeStruct((count, COLS), BF16),
            jax.ShapeDtypeStruct((TOP, count // N_ETP), F32),
            weight,
            weight,
            weight,
        ),
        in_specs=[hbm, hbm, vmem, vmem, hbm, hbm, hbm],
        out_specs=(vmem, vmem, hbm, hbm, hbm),
        scratch_shapes=[
            pltpu.VMEM((EXPERTS * TOK, 2 * PART), BF16),
            pltpu.VMEM((EXPERTS, PAD, LANES), BF16),
            pltpu.VMEM((EXPERTS, PAD, LANES), BF16),
            pltpu.VMEM((N_DP, ROWS, D), BF16),
            pltpu.VMEM((N_DP, ROWS, D), BF16),
            pltpu.VMEM((N_DP, ROWS, LANES), BF16),
            pltpu.VMEM((N_DP, EXPERTS * TOK, 2 * WHOLE), BF16),
            pltpu.VMEM((2 * FPAD, D), BF16),
            pltpu.VMEM((FPAD, D), BF16),
            pltpu.VMEM((N_DP, ROWS, 2 * FPAD), F32),
            pltpu.VMEM((N_DP, ROWS, FPAD), F32),
            pltpu.VMEM((all_rows, 2 * FPAD), BF16),
            pltpu.VMEM((all_rows, FPAD), BF16),
            pltpu.VMEM((2 * FPAD, all_rows), BF16),
            pltpu.VMEM((FPAD, all_rows), BF16),
            pltpu.VMEM((N_DP, ROWS, D), F32),
            pltpu.VMEM((N_DP, ROWS, D), BF16),
            pltpu.VMEM((3, FF, D), BF16),
            pltpu.VMEM((N_DP, EXPERTS, LANES), F32),
            pltpu.VMEM((N_DP, EXPERTS, LANES), F32),
            pltpu.VMEM((N_ETP, EXPERTS, LANES), F32),
            *landing,
            *landing,
            pltpu.VMEM((EXPERTS, PAD, COLS), BF16),
            pltpu.VMEM((EXPERTS, PAD, COLS), BF16),
            dma((EXPERTS,)),
            dma((EXPERTS,)),
            *[dma((PlaneGather.COUNT,))] * 4,
            dma((N_DP,)),
            dma((N_DP,)),
            *[dma((2, N_DP))] * 2,
            dma((12, 2, 5)),
            *[dma((PlaneReduce.COUNT,))] * 4,
            dma((8,)),
            dma((8,)),
            dma((8, 2)),
            dma((8, 2)),
            dma((10,)),
        ],
        compiler_params=pltpu.CompilerParams(collective_id=0, has_side_effects=True, vmem_limit_bytes=58 << 20),
        name="backward",
    )(tokens, out_grad, gates.T, expert_ids.T, w_gate, w_up, w_down)
    input_grad, gate_grad, *weight_grads = pl.pallas_call(
        copy_out,
        out_shape=tuple(jax.ShapeDtypeStruct(r.shape, r.dtype) for r in results),
        in_specs=[hbm] * 5,
        out_specs=(hbm,) * 5,
        scratch_shapes=[*[pltpu.VMEM(r.shape, r.dtype) for r in results], dma((8,)), dma((8,))],
        compiler_params=pltpu.CompilerParams(vmem_limit_bytes=58 << 20),
        name="outputs",
    )(*results)
    return input_grad, gate_grad.T, *weight_grads


def solution(mesh):
    in_specs = (
        P(("dp", "expert"), None),
        P(("dp", "expert"), None),
        P(("dp", "expert"), None),
        P(("dp", "expert"), None),
        P("expert", ("dp", "etp"), None),
        P("expert", ("dp", "etp"), None),
        P("expert", ("dp", "etp"), None),
    )
    out_specs = (
        P(("dp", "expert"), "etp"),
        P(("dp", "expert", "etp"), None),
        P("expert", ("dp", "etp"), None),
        P("expert", ("dp", "etp"), None),
        P("expert", ("dp", "etp"), None),
    )
    return jax.shard_map(
        per_device, mesh=mesh, in_specs=in_specs, out_specs=out_specs, check_vma=False
    )
```

```python
import jax
import jax.numpy as jnp
from jax import lax
from jax.experimental import pallas as pl
from jax.experimental.pallas import tpu as pltpu
from jax.sharding import PartitionSpec as P

EXPERTS = 16
TOP = 4
CAP = 12
PAD = 16
N_DP = 4
N_ETP = 4
ROWS = EXPERTS * CAP
PADDED = EXPERTS * PAD
D = 3072
FF = 336
FPAD = 384
COLS = D // N_ETP
WHOLE = 512
SLOTTED = D - WHOLE
PART = SLOTTED // N_ETP
TOK = 32
LANES = 128
MESH = pl.DeviceIdType.MESH
F32 = jnp.float32
BF16 = jnp.bfloat16


def iota(shape, dim):
    return lax.broadcasted_iota(jnp.int32, shape, dim)


def compact_matrix(rows):
    r, k = iota((rows, PADDED), 0), iota((rows, PADDED), 1)
    return jnp.where(((k >> 4) * CAP + (k & 15) == r) & ((k & 15) < CAP), 1.0, 0.0).astype(BF16)


def place_of(block):
    away = ((block >> 1) + 8 - (lax.axis_index("expert") >> 1)) & 7
    return jnp.where(away > 4, 2 * (8 - away), jnp.maximum(2 * away - 1, 0)) * 2 + (block & 1)


def placed_matrix():
    r, k = iota((ROWS, PADDED), 0), iota((ROWS, PADDED), 1)
    return jnp.where((place_of(k >> 4) * CAP + (k & 15) == r) & ((k & 15) < CAP), 1.0, 0.0).astype(BF16)


def same_row(which):
    k, m = iota((PADDED, PADDED), 0), iota((PADDED, PADDED), 1)
    return jnp.where(m == (k >> 4) * PAD + CAP + which, 1.0, 0.0).astype(BF16)


def extra_row(which):
    b, k = iota((EXPERTS, PADDED), 0), iota((EXPERTS, PADDED), 1)
    return jnp.where(k == b * PAD + CAP + which, 1.0, 0.0).astype(BF16)


def lane_spread():
    c, k = iota((LANES, PADDED), 0), iota((LANES, PADDED), 1)
    return jnp.where((k & 15) == c, 1.0, 0.0).astype(BF16)


def block_of_row(placed=True):
    r, b = iota((ROWS, EXPERTS), 0), iota((ROWS, EXPERTS), 1)
    if not placed:
        b = place_of(b)
    return jnp.where((r >= b * CAP) & (r < b * CAP + CAP), 1.0, 0.0).astype(BF16)


def slot_of_row():
    return dot_t(compact_matrix(ROWS), lane_spread())


def parts(value):
    out = []
    for _ in range(3):
        part = value.astype(BF16)
        value = value - part.astype(F32)
        out.append(part)
    return out


def dot(a, b):
    return jnp.dot(a, b, preferred_element_type=F32)


def dot_t(a, b):
    return lax.dot_general(a, b, (((1,), (1,)), ((), ())), preferred_element_type=F32)


def t_dot(a, b):
    return lax.dot_general(a, b, (((0,), (0,)), ((), ())), preferred_element_type=F32)


def position():
    return lax.axis_index("dp"), lax.axis_index("expert"), lax.axis_index("etp")


def copy_to(src, dst, send_sem, recv_sem, device):
    return pltpu.make_async_remote_copy(
        src_ref=src, dst_ref=dst, send_sem=send_sem, recv_sem=recv_sem, device_id=device, device_id_type=MESH
    )


def piece(ref, i, j):
    return ref.at[i, :, pl.ds(pl.multiple_of(j * COLS, COLS), COLS)]


class PlaneGather:
    COUNT = 26

    def __init__(self, ref, start, width, dp_first, send_sems, recv_sems):
        x, e, y = position()
        self.ref, self.dp_first, self.send_sems, self.recv_sems = ref, dp_first, send_sems, recv_sems
        self.start, self.width = start, width
        self.e = e
        self.a, self.b = (x, y) if dp_first else (y, x)
        self.sent = []

    def at(self, i, j, half=None):
        i, j = i % 4, j % 4
        if not self.dp_first:
            i, j = j, i
        columns = pl.ds(pl.multiple_of(j * PART + self.start, LANES), self.width)
        if half is None:
            return self.ref.at[i, :, columns]
        return self.ref.at[i, pl.ds(half * (ROWS // 2), ROWS // 2), columns]

    def device(self, i, j):
        i, j = i % 4, j % 4
        return (i, self.e, j) if self.dp_first else (j, self.e, i)

    def copy(self, view, index, device):
        return copy_to(view, view, self.send_sems.at[index], self.recv_sems.at[index], device)

    def send(self, view, index, device):
        c = self.copy(view, index, device)
        c.start()
        self.sent.append(c)

    def wait(self, view, index):
        self.copy(view, index, self.device(self.a, self.b)).wait_recv()

    def own(self, half):
        a, b = self.a, self.b
        view = self.at(a, b, half)
        self.send(view, 22 * half, self.device(a + 1, b))
        self.send(view, 1 + 22 * half, self.device(a - 1, b))
        self.send(view, 4 + 20 * half, self.device(a, b + 1))
        self.send(view, 5 + 20 * half, self.device(a, b - 1))

    def forward_own(self):
        a, b = self.a, self.b
        self.wait(self.at(a, b - 1, 0), 4)
        self.send(self.at(a, b - 1, 0), 14, self.device(a, b + 1))
        self.wait(self.at(a, b + 1, 1), 25)
        self.send(self.at(a, b + 1, 1), 15, self.device(a, b - 1))
        self.wait(self.at(a, b - 1, 1), 24)
        self.wait(self.at(a, b + 1, 0), 5)

    def both_second(self, i, slot, half=None):
        view = self.at(i, self.b, half)
        self.send(view, 4 + 2 * slot, self.device(self.a, self.b + 1))
        self.send(view, 5 + 2 * slot, self.device(self.a, self.b - 1))

    def forward_second(self, i, slot):
        self.wait(self.at(i, self.b - 1), 4 + 2 * slot)
        self.send(self.at(i, self.b - 1, 0), 14 + 2 * slot, self.device(self.a, self.b + 1))
        self.wait(self.at(i, self.b + 1), 5 + 2 * slot)
        self.send(self.at(i, self.b + 1, 1), 15 + 2 * slot, self.device(self.a, self.b - 1))

    def steps(self):
        a, b = self.a, self.b

        def lower():
            self.wait(self.at(a - 1, b, 0), 0)
            self.send(self.at(a - 1, b, 0), 2, self.device(a + 1, b))
            self.wait(self.at(a - 1, b, 1), 22)
            self.both_second(a - 1, 1)

        def upper():
            self.wait(self.at(a + 1, b, 1), 23)
            self.send(self.at(a + 1, b, 1), 3, self.device(a - 1, b))
            self.wait(self.at(a + 1, b, 0), 1)
            self.both_second(a + 1, 2)

        def opposite():
            self.wait(self.at(a + 2, b, 0), 2)
            self.both_second(a + 2, 3, 0)
            self.wait(self.at(a + 2, b, 1), 3)
            self.both_second(a + 2, 4, 1)

        def opposite_second():
            self.wait(self.at(a + 2, b - 1, 0), 10)
            self.send(self.at(a + 2, b - 1, 0), 20, self.device(a, b + 1))
            self.wait(self.at(a + 2, b + 1, 1), 13)
            self.send(self.at(a + 2, b + 1, 1), 21, self.device(a, b - 1))

        return [
            None,
            lower,
            upper,
            self.forward_own,
            opposite,
            lambda: self.forward_second(a - 1, 1),
            lambda: self.forward_second(a + 1, 2),
            opposite_second,
        ]

    def finish_near(self):
        a, b = self.a, self.b
        self.wait(self.at(a + 2, b + 1, 0), 11)
        self.wait(self.at(a + 2, b - 1, 1), 12)

    def finish_far(self, slot):
        i = self.a + (0, -1, 1, 2)[slot]
        self.wait(self.at(i, self.b + 2, 0), 14 + 2 * slot)
        self.wait(self.at(i, self.b + 2, 1), 15 + 2 * slot)


class PlaneReduce:
    HALF = ROWS // 2
    QUARTER = ROWS // 4
    COUNT = 20

    def __init__(self, ref, out, low, dp_first, order, opp, full, opp2, full2, send_sems, recv_sems):
        x, e, y = position()
        self.ref, self.out, self.low, self.dp_first, self.order = ref, out, low, dp_first, order
        self.opp, self.full, self.opp2, self.full2 = opp, full, opp2, full2
        self.send_sems, self.recv_sems = send_sems, recv_sems
        self.e = e
        self.a, self.b = (x, y) if dp_first else (y, x)
        self.sent = []

    def device(self, i, j):
        i, j = i % 4, j % 4
        return (i, self.e, j) if self.dp_first else (j, self.e, i)

    def at(self, i, j, start, size, ref=None):
        i, j = i % 4, j % 4
        ref = self.out if ref is None else ref
        view = piece(ref, i, j) if self.dp_first else piece(ref, j, i)
        return view.at[pl.ds(self.low + start, size), :]

    def send(self, src, dst, index, device):
        c = copy_to(src, dst, self.send_sems.at[index], self.recv_sems.at[index], device)
        c.start()
        self.sent.append(c)

    def wait(self, dst, index):
        copy_to(dst, dst, self.send_sems.at[index], self.recv_sems.at[index], self.device(self.a, self.b)).wait_recv()

    def opposite(self, k):
        a, b, q = self.a, self.b, self.QUARTER
        j = b + self.order[k]
        self.send(self.at(a + 2, j, 0, q), self.opp.at[0, k], 4 * k, self.device(a + 1, b))
        self.send(self.at(a + 2, j, q, q), self.opp.at[1, k], 4 * k + 1, self.device(a - 1, b))

    def near(self, k, sides=(0, 1)):
        a, b, q, h = self.a, self.b, self.QUARTER, self.HALF
        j = b + self.order[k]
        for side in sides:
            to = a + 1 if side == 0 else a - 1
            self.wait(self.opp.at[side, k], 4 * k + side)
            own = self.at(to, j, side * q, q, self.ref)[...]
            self.at(to, j, side * q, q)[...] = (own + self.opp[side, k].astype(F32)).astype(BF16)
            self.send(self.at(to, j, 0, h), self.full.at[side, k], 4 * k + 2 + side, self.device(to, b))

    def total(self, relative):
        k = self.order.index(relative)
        for side in range(2):
            self.wait(self.full.at[side, k], 4 * k + 2 + side)
        own = self.at(self.a, self.b + relative, 0, self.HALF, self.ref)[...]
        return own + self.full[0, k].astype(F32) + self.full[1, k].astype(F32)

    def second_opposite(self):
        a, b, q, h = self.a, self.b, self.QUARTER, self.HALF
        self.at(a, b + 2, 0, h)[...] = self.total(2).astype(BF16)
        self.send(self.at(a, b + 2, 0, q), self.opp2.at[0], 16, self.device(a, b + 1))
        self.send(self.at(a, b + 2, q, q), self.opp2.at[1], 17, self.device(a, b - 1))

    def second_near(self, side):
        a, b, q, h = self.a, self.b, self.QUARTER, self.HALF
        step = 1 if side == 0 else -1
        value = self.total(step)
        self.wait(self.opp2.at[side], 16 + side)
        extra = self.opp2[side].astype(F32)
        if side == 0:
            value = jnp.concatenate([value[:q] + extra, value[q:]], axis=0)
        else:
            value = jnp.concatenate([value[:q], value[q:] + extra], axis=0)
        self.at(a, b + step, 0, h)[...] = value.astype(BF16)
        self.send(self.at(a, b + step, 0, h), self.full2.at[side], 18 + side, self.device(a, b + step))

    def finish(self):
        value = self.total(0)
        for side in range(2):
            self.wait(self.full2.at[side], 18 + side)
        return value + self.full2[0].astype(F32) + self.full2[1].astype(F32)


class Ring:
    def __init__(self, block, z_send, z_recv, core_send, core_recv):
        self.x, self.e, self.y = position()
        self.block = block
        self.z_send, self.z_recv, self.core_send, self.core_recv = z_send, z_recv, core_send, core_recv
        self.other = self.e + 1 - 2 * (self.e % 2)
        self.sent = []

    def copy(self, src, dst, send, recv, device):
        c = copy_to(src, dst, send, recv, device)
        c.start()
        self.sent.append(c)

    def view(self, e, side, distance):
        away = 2 * distance
        return self.block((e + (EXPERTS - away if side == 0 else away)) % EXPERTS, side if distance == 4 else None)

    def onward(self, side, distance):
        e = self.e
        view = self.view(e, side, distance)
        if distance > 0:
            copy_to(
                view, view, self.z_send.at[side, distance], self.z_recv.at[side, distance], (self.x, e, self.y)
            ).wait_recv()
        if distance < 4:
            to = (e + (2 if side == 0 else EXPERTS - 2)) % EXPERTS
            next_view = self.view(to, side, distance + 1)
            self.copy(
                next_view, next_view,
                self.z_send.at[side, distance + 1], self.z_recv.at[side, distance + 1], (self.x, to, self.y),
            )
        if distance > 0 or side == 0:
            self.copy(
                view, view, self.core_send.at[side, distance], self.core_recv.at[side, distance],
                (self.x, self.other, self.y),
            )

    def round(self, distance):
        for side in range(2):
            self.onward(side, distance)

    NEAR = ((0, 0), (0, 1), (1, 1), (1, 2))
    FAR = ((0, 2), (0, 3), (1, 3), (0, 4), (1, 4))

    def finish(self, which):
        for side, distance in which:
            view = self.view(self.other, side, distance)
            copy_to(
                view, view, self.core_send.at[side, distance], self.core_recv.at[side, distance],
                (self.x, self.e, self.y),
            ).wait_recv()


def kernel(
    tokens, out_grad, gates, expert_ids, w_gate, w_up, w_down,
    input_grad, gate_grad, grad_gate, grad_up, grad_down,
    near, table_out, table_in, rows, grads, tables, whole, w_in, w_out, pre, raw, deltas, scaled, turned, turned_scaled,
    sums, wire, made, terms, landed_x, landed_y,
    opp_a, full_a, opp2_a, full2_a, opp_b, full_b, opp2_b, full2_b, back, ready,
    slot_send, slot_recv, x_send, x_recv, d_send, d_recv, g_send, g_recv,
    dp_send, dp_recv, z_sems,
    send_a, recv_a, send_b, recv_b, t_send, t_recv, r_send, r_recv, local,
):
    x, e, y = position()
    peers = [(x, (e + j) % EXPERTS, y) for j in range(1, EXPERTS)]
    peers += [((x + j) % N_DP, e, y) for j in range(1, N_DP)]
    peers += [(x, e, (y + j) % N_ETP) for j in range(1, N_ETP)]
    barrier = pltpu.get_barrier_semaphore()
    for device in peers:
        pl.semaphore_signal(barrier, inc=1, device_id=device, device_id_type=MESH)
    columns = pl.ds(pl.multiple_of(y * PART, LANES), PART)
    late = pl.ds(SLOTTED, WHOLE)

    def token_rows(place, half=None):
        if half is None:
            return pl.ds(pl.multiple_of(place * TOK, TOK), TOK)
        return pl.ds(pl.multiple_of(place * TOK + half * (TOK // 2), TOK // 2), TOK // 2)

    def whole_block(place, half=None):
        return whole.at[:, token_rows(place), :] if half is None else whole.at[pl.ds(2 * half, 2), token_rows(place), :]

    def whole_landing(i, which):
        return whole.at[i, token_rows(e), pl.ds(which * WHOLE, WHOLE)]

    ring_x = Ring(lambda p, half=None: near.at[token_rows(p, half), pl.ds(0, PART)], *[z_sems.at[k] for k in range(4)])
    ring_d = Ring(lambda p, half=None: near.at[token_rows(p, half), pl.ds(PART, PART)], *[z_sems.at[k] for k in range(4, 8)])
    ring_w = Ring(whole_block, *[z_sems.at[k] for k in range(8, 12)])

    loads = [
        pltpu.make_async_copy(tokens.at[:, columns], ring_x.block(e), local.at[0]),
        pltpu.make_async_copy(out_grad.at[:, columns], ring_d.block(e), local.at[1]),
        pltpu.make_async_copy(w_gate.at[0], w_in.at[pl.ds(0, FF), :], local.at[2]),
        pltpu.make_async_copy(w_up.at[0], w_in.at[pl.ds(FPAD, FF), :], local.at[3]),
        pltpu.make_async_copy(w_down.at[0], w_out.at[pl.ds(0, FF), :], local.at[4]),
    ]
    own_whole = [
        pltpu.make_async_copy(s.at[:, late], whole_landing(x, which), local.at[8 + which])
        for which, s in enumerate((tokens, out_grad))
    ]
    for c in loads[:2] + own_whole + loads[2:]:
        c.start()
    expert, place = iota((PADDED, TOK), 0) >> 4, iota((PADDED, TOK), 0) & 15
    ids, weight = expert_ids[...], gates[...].astype(F32)
    chosen = [jnp.where(ids[k : k + 1, :] == expert, 1.0, 0.0) for k in range(TOP)]
    member = chosen[0] + chosen[1] + chosen[2] + chosen[3]
    before = jnp.where(iota((TOK, TOK), 0) < iota((TOK, TOK), 1), 1.0, 0.0).astype(BF16)
    earlier = dot(member.astype(BF16), before)
    table = jnp.where((earlier == place.astype(F32)) & (place < CAP), member, 0.0)
    gate_slots = sum(chosen[k] * weight[k : k + 1, :] for k in range(TOP)) * table
    gate_slots = jnp.sum(gate_slots, axis=1, keepdims=True)
    table = table.astype(BF16)
    widen = jnp.where(iota((TOK, LANES), 0) == iota((TOK, LANES), 1), 1.0, 0.0).astype(BF16)
    sent = []

    wide = jnp.where(iota((PADDED, LANES), 1) == TOK, gate_slots, dot(table, widen))
    table_out[...] = wide.astype(BF16).reshape(EXPERTS, PAD, LANES)
    loads[0].wait()
    loads[1].wait()
    pl.semaphore_wait(barrier, len(peers))

    ring_x.round(0)
    ring_d.round(0)
    for j in range(1, EXPERTS):
        to = (e + j) % EXPERTS
        c = copy_to(table_out.at[to], table_in.at[e], slot_send.at[j], slot_recv.at[j], (x, to, y))
        c.start()
        sent.append(c)
    for j in range(1, N_DP):
        for which, source in enumerate((tokens, out_grad)):
            c = copy_to(
                source.at[:, late], whole_landing(x, which),
                dp_send.at[which, j], dp_recv.at[which, j], ((x + j) % N_DP, e, y),
            )
            c.start()
            sent.append(c)
    table_in[e] = table_out[e]
    for ref, low in ((w_in, FF), (w_in, FPAD + FF), (w_out, FF)):
        ref[pl.ds(low, FPAD - FF), :] = jnp.zeros((FPAD - FF, D), BF16)

    gather_x = PlaneGather(rows, 0, PART, True, x_send, x_recv)
    gather_d = PlaneGather(grads, 0, PART, False, d_send, d_recv)
    steps_x, steps_d = gather_x.steps(), gather_d.steps()

    def pick(g):
        repeat = jnp.where(iota((LANES, EXPERTS * TOK), 0) == (iota((LANES, EXPERTS * TOK), 1) & 31), 1.0, 0.0)
        within = jnp.where(iota((EXPERTS, EXPERTS * TOK), 0) == (iota((EXPERTS, EXPERTS * TOK), 1) >> 5), 1.0, 0.0)
        return (dot(tables[g], repeat.astype(BF16)) * dot(block_of_row(False), within.astype(BF16))).astype(BF16)

    def run(*which):
        for k in which:
            steps_x[k]()
            steps_d[k]()

    half = ROWS // 2

    def own_half(ref, start, h):
        r, m = iota((half, EXPERTS // 2 * TOK), 0), iota((half, EXPERTS // 2 * TOK), 1)
        within = (r >= (m >> 5) * CAP) & (r < (m >> 5) * CAP + CAP)
        lane, m = iota((LANES, EXPERTS // 2 * TOK), 0), iota((LANES, EXPERTS // 2 * TOK), 1)
        repeat = jnp.where(lane == (m & 31), 1.0, 0.0).astype(BF16)
        own = pl.ds(h * half, half)
        picker = jnp.where(within, dot(tables[x, own, :], repeat), 0.0).astype(BF16)
        taken = []
        for away in ((0, 1, 7, 2), (6, 3, 5, 4))[h]:
            low = pl.multiple_of((((e // 2) + away) % 8) * (2 * TOK), 2 * TOK)
            taken.append(near[pl.ds(low, 2 * TOK), start : start + PART])
        ref[x, own, columns] = dot(picker, jnp.concatenate(taken, axis=0)).astype(BF16)

    for k in range(1, 3):
        ring_x.round(k)
        ring_d.round(k)
    for j in range(1, EXPERTS):
        view = table_in.at[(e + EXPERTS - j) % EXPERTS]
        copy_to(view, view, slot_send.at[j], slot_recv.at[j], (x, e, y)).wait_recv()
    tables[x] = dot(placed_matrix(), table_in[...].reshape(PADDED, LANES)).astype(BF16)
    for j in range(1, N_DP):
        c = copy_to(tables.at[x], tables.at[x], g_send.at[j], g_recv.at[j], ((x + j) % N_DP, e, y))
        c.start()
        sent.append(c)
    ring_x.finish(Ring.NEAR)
    own_half(rows, 0, 0)
    gather_x.own(0)
    ring_x.round(3)
    ring_d.round(3)
    ring_d.finish(Ring.NEAR)
    own_half(grads, PART, 0)
    gather_d.own(0)
    ring_x.round(4)
    ring_d.round(4)
    ring_x.finish(Ring.FAR)
    own_half(rows, 0, 1)
    gather_x.own(1)
    ring_d.finish(Ring.FAR)
    own_half(grads, PART, 1)
    gather_d.own(1)
    for c in own_whole:
        c.wait()
    for j in range(1, N_DP):
        for which in range(2):
            view = whole_landing((x + N_DP - j) % N_DP, which)
            copy_to(view, view, dp_send.at[which, j], dp_recv.at[which, j], (x, e, y)).wait_recv()
    ring_w.round(0)

    reduce_a = PlaneReduce(
        sums, wire, 0, True, (2, 1, -1, 0), opp_a, full_a, opp2_a, full2_a, send_a, recv_a
    )
    reduce_b = PlaneReduce(
        sums, wire, ROWS // 2, False, (2, 1, -1, 0), opp_b, full_b, opp2_b, full2_b, send_b, recv_b
    )
    group = [(x + j) % N_DP for j in (0, 3, 1, 2)]

    def add_x(i, j):
        part = pl.ds(pl.multiple_of((j % N_ETP) * PART, LANES), PART)
        pre[i % N_DP] += dot_t(rows[i % N_DP, :, part], w_in[:, part])

    def add_d(i, j):
        part = pl.ds(pl.multiple_of((j % N_ETP) * PART, LANES), PART)
        raw[i % N_DP] += dot_t(grads[i % N_DP, :, part], w_out[:, part])

    def add_sides(move):
        @pl.loop(0, 2)
        def _(k):
            add_x(x + N_DP + move, y + 3 + 2 * k)
            add_d(x + 3 + 2 * k, y + N_ETP + move)

    def add_far(slots):
        for slot in slots:
            gather_x.finish_far(slot)
            gather_d.finish_far(slot)
        start, step = {0: (0, 3), 2: (1, 1)}[slots[0]]

        @pl.loop(0, 2)
        def _(k):
            add_x(x + start + step * k, y + 2)
            add_d(x + 2, y + start + step * k)

    def add_tokens(low, high):
        @pl.loop(low, high)
        def _(k):
            g = (x + k) % N_DP
            picked = dot(pick(g), whole[g]).astype(BF16)
            rows[g, :, SLOTTED:] = picked[:, :WHOLE]
            grads[g, :, SLOTTED:] = picked[:, WHOLE:]
            pre[g] += dot_t(picked[:, :WHOLE], w_in[:, SLOTTED:])
            raw[g] += dot_t(picked[:, WHOLE:], w_out[:, SLOTTED:])

    def backward(slot, send=None):
        g = group[slot]
        a, u, r = pre[g, :, :FPAD], pre[g, :, FPAD:], raw[g]
        which = slot_of_row()
        scale = tables[g, :, TOK : TOK + 1].astype(F32)
        sigmoid = jax.nn.sigmoid(a)
        activated = a * sigmoid
        product = activated * u
        q = jnp.sum(product * r, axis=1, keepdims=True) * which
        terms[g] = sum(t_dot(block_of_row(), part) for part in parts(q))
        own = pl.ds(pl.multiple_of(g * ROWS, ROWS), ROWS)
        scaled[own, :] = (scale * product).astype(BF16)
        hidden = scale * r
        deltas[own, :FPAD] = (hidden * u * sigmoid * (1.0 + a * (1.0 - sigmoid))).astype(BF16)
        deltas[own, FPAD:] = (hidden * activated).astype(BF16)

        def columns_of(k):
            part = pl.ds(pl.multiple_of(k * COLS, COLS), COLS)
            value = dot(deltas[own, :], w_in[:, part])
            sums[g, :, part] = value
            wire[g, :, part] = value.astype(BF16)

        if send is None:
            pl.loop(0, N_ETP)(columns_of)
            return
        for k in range(N_ETP):
            columns_of((y + N_ETP + reduce_a.order[k]) % N_ETP)
            send(k)

    def weight_grad(which):
        source = (rows, rows, grads)[which]

        @pl.loop(0, N_ETP)
        def _(k):
            part = pl.ds(pl.multiple_of(k * COLS, COLS), COLS)
            left = turned_scaled[:FF, :] if which == 2 else turned[pl.ds(which * FPAD, FF), :]
            made[which, :, part] = dot(left, source[:, :, part].reshape(N_DP * ROWS, COLS)).astype(BF16)

        c = pltpu.make_async_copy(made.at[which], (grad_gate, grad_up, grad_down)[which].at[0], local.at[5 + which])
        c.start()
        loads.append(c)

    pre[...] = jnp.zeros_like(pre)
    raw[...] = jnp.zeros_like(raw)
    for c in loads[2:]:
        c.wait()
    add_x(x, y)
    add_d(x, y)
    run(1, 2)
    ring_w.round(1)

    @pl.loop(0, 2)
    def _(k):
        add_x(x + 3 + 2 * k, y)
        add_d(x, y + 3 + 2 * k)

    run(3)
    add_sides(0)
    run(4)
    ring_w.round(2)
    add_x(x + 2, y)
    add_d(x, y + 2)
    run(5)
    ring_w.round(3)
    add_sides(-1)
    run(6)
    ring_w.round(4)
    add_sides(1)
    run(7)
    for j in range(1, N_DP):
        g = (x + N_DP - j) % N_DP
        copy_to(tables.at[g], tables.at[g], g_send.at[j], g_recv.at[j], (x, e, y)).wait_recv()
    gather_x.finish_near()
    gather_d.finish_near()
    add_sides(2)
    ring_w.finish(Ring.NEAR + Ring.FAR)
    add_tokens(0, 4)
    add_far((0, 1))
    add_far((2, 3))

    def send_opposite(k):
        reduce_a.opposite(k)
        if k == 0:
            reduce_b.opposite(0)

    backward(3, send_opposite)
    backward(2)
    reduce_b.opposite(1)
    reduce_b.near(0)
    reduce_a.near(0, (0,))
    reduce_a.near(1, (0,))
    backward(1)
    reduce_b.opposite(2)
    reduce_a.near(0, (1,))
    reduce_a.near(1, (1,))
    reduce_b.near(1)
    reduce_a.near(2)
    backward(0)
    reduce_b.opposite(3)
    reduce_b.near(2)
    for j in range(1, N_DP):
        to = (x + j) % N_DP
        c = copy_to(terms.at[to], landed_x.at[j], t_send.at[j], t_recv.at[j], (to, e, y))
        c.start()
        sent.append(c)
    turned[...] = deltas[...].T
    turned_scaled[...] = scaled[...].T
    reduce_a.second_opposite()
    reduce_b.second_opposite()
    total = terms[x]
    for j in range(1, N_DP):
        copy_to(landed_x.at[j], landed_x.at[j], t_send.at[j], t_recv.at[j], (x, e, y)).wait_recv()
        total = total + landed_x[j]
    landed_y[0] = total
    for j in range(1, N_ETP):
        c = copy_to(landed_y.at[0], landed_y.at[j], t_send.at[3 + j], t_recv.at[3 + j], (x, e, (y + j) % N_ETP))
        c.start()
        sent.append(c)
    reduce_a.second_near(0)
    reduce_b.second_near(0)
    reduce_a.near(3)
    reduce_b.near(3)
    weight_grad(0)
    reduce_a.second_near(1)
    reduce_b.second_near(1)
    for j in range(1, N_ETP):
        copy_to(landed_y.at[j], landed_y.at[j], t_send.at[3 + j], t_recv.at[3 + j], (x, e, y)).wait_recv()
        total = total + landed_y[j]
    spare = sum(t_dot(extra_row(which), part) for which, part in enumerate(parts(total)))
    r, k = iota((half, PADDED // 2), 0), iota((half, PADDED // 2), 1)
    spread = jnp.where(((k >> 4) * CAP + (k & 15) == r) & ((k & 15) < CAP), 1.0, 0.0).astype(BF16)
    core = e % 2
    for h, reduce in ((1, reduce_b), (0, reduce_a)):
        padded = t_dot(spread, reduce.finish().astype(BF16))
        own = pl.ds(h * (EXPERTS // 2), EXPERTS // 2)
        extra = spare[h * (PADDED // 2) : (h + 1) * (PADDED // 2)]
        ready[own, :, :LANES] = (padded[:, :LANES] + extra).astype(BF16).reshape(EXPERTS // 2, PAD, LANES)
        ready[own, :, LANES:] = padded[:, LANES:].astype(BF16).reshape(EXPERTS // 2, PAD, COLS - LANES)
        for k in range(3, -1, -1):
            away = ((0, 1, 7, 2), (6, 3, 5, 4))[h][k]
            for flip in range(2):
                to_core = core if flip == 0 else 1 - core
                source = ready.at[8 * h + 2 * k + to_core]
                if away == 0 and flip == 0:
                    back[e] = source[...]
                    continue
                to = ((e // 2 + away) % 8) * 2 + to_core
                c = copy_to(source, back.at[e], r_send.at[away, flip], r_recv.at[away, flip], (x, to, y))
                c.start()
                sent.append(c)
    weight_grad(1)
    weight_grad(2)
    for away in range(8):
        for flip in range(2):
            if away > 0 or flip > 0:
                frm = ((e // 2 + 8 - away) % 8) * 2 + (core if flip == 0 else 1 - core)
                copy_to(
                    back.at[frm], back.at[frm], r_send.at[away, flip], r_recv.at[away, flip], (x, e, y)
                ).wait_recv()
    block = back[...].reshape(PADDED, COLS)
    input_grad[...] = t_dot(table, block).astype(BF16)
    lanes = block[:, :LANES]
    mine = jnp.where(iota((PADDED, LANES), 1) == (iota((PADDED, LANES), 0) & 15), 1.0, 0.0)
    value = sum(dot(same_row(which), lanes) for which in range(3))
    value = jnp.sum(value * mine, axis=1, keepdims=True) * table.astype(F32)
    pairs = jnp.concatenate([jnp.sum(chosen[k] * value, axis=0, keepdims=True) for k in range(TOP)], axis=0)
    share = TOK // N_ETP
    take = jnp.where(iota((TOK, share), 0) == iota((TOK, share), 1) + y * share, 1.0, 0.0).astype(BF16)
    gate_grad[...] = sum(dot(part, take) for part in parts(pairs))
    for c in loads[5:]:
        c.wait()
    for c in sent + gather_x.sent + gather_d.sent + reduce_a.sent + reduce_b.sent:
        c.wait_send()
    for ring in (ring_x, ring_d, ring_w):
        for c in ring.sent:
            c.wait_send()


def copy_out(*refs):
    count = (len(refs) - 2) // 3
    sources, targets, held = refs[:count], refs[count : 2 * count], refs[2 * count : 3 * count]
    into, out = refs[3 * count :]
    steps = []
    for source, target, place in zip(sources, targets, held):
        if len(source.shape) < 3:
            steps.append((source, place, target))
            continue
        for low, size in ((0, 176), (176, 160)):
            view = (0, pl.ds(low, size), slice(None))
            steps.append((source.at[view], place.at[view], target.at[view]))
    steps = steps[::-1]
    first = [pltpu.make_async_copy(source, place, into.at[k]) for k, (source, place, _) in enumerate(steps)]
    second = [pltpu.make_async_copy(place, target, out.at[k]) for k, (_, place, target) in enumerate(steps)]
    for c in first:
        c.start()
    for one, two in zip(first, second):
        one.wait()
        two.start()
    for c in second:
        c.wait()


def per_device(tokens, out_grad, gates, expert_ids, w_gate, w_up, w_down):
    dma = pltpu.SemaphoreType.DMA
    vmem = pl.BlockSpec(memory_space=pltpu.VMEM)
    hbm = pl.BlockSpec(memory_space=pl.ANY)
    count = tokens.shape[0]
    half, quarter = ROWS // 2, ROWS // 4
    landing = [
        pltpu.VMEM((2, 4, quarter, COLS), BF16),
        pltpu.VMEM((2, 4, half, COLS), BF16),
        pltpu.VMEM((2, quarter, COLS), BF16),
        pltpu.VMEM((2, half, COLS), BF16),
    ]
    all_rows = N_DP * ROWS
    weight = jax.ShapeDtypeStruct(w_gate.shape, BF16)
    results = pl.pallas_call(
        kernel,
        out_shape=(
            jax.ShapeDtypeStruct((count, COLS), BF16),
            jax.ShapeDtypeStruct((TOP, count // N_ETP), F32),
            weight,
            weight,
            weight,
        ),
        in_specs=[hbm, hbm, vmem, vmem, hbm, hbm, hbm],
        out_specs=(vmem, vmem, hbm, hbm, hbm),
        scratch_shapes=[
            pltpu.VMEM((EXPERTS * TOK, 2 * PART), BF16),
            pltpu.VMEM((EXPERTS, PAD, LANES), BF16),
            pltpu.VMEM((EXPERTS, PAD, LANES), BF16),
            pltpu.VMEM((N_DP, ROWS, D), BF16),
            pltpu.VMEM((N_DP, ROWS, D), BF16),
            pltpu.VMEM((N_DP, ROWS, LANES), BF16),
            pltpu.VMEM((N_DP, EXPERTS * TOK, 2 * WHOLE), BF16),
            pltpu.VMEM((2 * FPAD, D), BF16),
            pltpu.VMEM((FPAD, D), BF16),
            pltpu.VMEM((N_DP, ROWS, 2 * FPAD), F32),
            pltpu.VMEM((N_DP, ROWS, FPAD), F32),
            pltpu.VMEM((all_rows, 2 * FPAD), BF16),
            pltpu.VMEM((all_rows, FPAD), BF16),
            pltpu.VMEM((2 * FPAD, all_rows), BF16),
            pltpu.VMEM((FPAD, all_rows), BF16),
            pltpu.VMEM((N_DP, ROWS, D), F32),
            pltpu.VMEM((N_DP, ROWS, D), BF16),
            pltpu.VMEM((3, FF, D), BF16),
            pltpu.VMEM((N_DP, EXPERTS, LANES), F32),
            pltpu.VMEM((N_DP, EXPERTS, LANES), F32),
            pltpu.VMEM((N_ETP, EXPERTS, LANES), F32),
            *landing,
            *landing,
            pltpu.VMEM((EXPERTS, PAD, COLS), BF16),
            pltpu.VMEM((EXPERTS, PAD, COLS), BF16),
            dma((EXPERTS,)),
            dma((EXPERTS,)),
            *[dma((PlaneGather.COUNT,))] * 4,
            dma((N_DP,)),
            dma((N_DP,)),
            *[dma((2, N_DP))] * 2,
            dma((12, 2, 5)),
            *[dma((PlaneReduce.COUNT,))] * 4,
            dma((8,)),
            dma((8,)),
            dma((8, 2)),
            dma((8, 2)),
            dma((10,)),
        ],
        compiler_params=pltpu.CompilerParams(collective_id=0, has_side_effects=True, vmem_limit_bytes=58 << 20),
        name="backward",
    )(tokens, out_grad, gates.T, expert_ids.T, w_gate, w_up, w_down)
    input_grad, gate_grad, *weight_grads = pl.pallas_call(
        copy_out,
        out_shape=tuple(jax.ShapeDtypeStruct(r.shape, r.dtype) for r in results),
        in_specs=[hbm] * 5,
        out_specs=(hbm,) * 5,
        scratch_shapes=[*[pltpu.VMEM(r.shape, r.dtype) for r in results], dma((8,)), dma((8,))],
        compiler_params=pltpu.CompilerParams(vmem_limit_bytes=58 << 20),
        name="outputs",
    )(*results)
    return input_grad, gate_grad.T, *weight_grads


def solution(mesh):
    in_specs = (
        P(("dp", "expert"), None),
        P(("dp", "expert"), None),
        P(("dp", "expert"), None),
        P(("dp", "expert"), None),
        P("expert", ("dp", "etp"), None),
        P("expert", ("dp", "etp"), None),
        P("expert", ("dp", "etp"), None),
    )
    out_specs = (
        P(("dp", "expert"), "etp"),
        P(("dp", "expert", "etp"), None),
        P("expert", ("dp", "etp"), None),
        P("expert", ("dp", "etp"), None),
        P("expert", ("dp", "etp"), None),
    )
    return jax.shard_map(
        per_device, mesh=mesh, in_specs=in_specs, out_specs=out_specs, check_vma=False
    )
```

```python
import jax
import jax.numpy as jnp
from jax import lax
from jax.experimental import pallas as pl
from jax.experimental.pallas import tpu as pltpu
from jax.sharding import PartitionSpec as P

EXPERTS = 16
TOP = 4
CAP = 12
PAD = 16
N_DP = 4
N_ETP = 4
ROWS = EXPERTS * CAP
PADDED = EXPERTS * PAD
D = 3072
FF = 336
FPAD = 384
COLS = D // N_ETP
WHOLE = 512
SLOTTED = D - WHOLE
PART = SLOTTED // N_ETP
TOK = 32
LANES = 128
MESH = pl.DeviceIdType.MESH
F32 = jnp.float32
BF16 = jnp.bfloat16


def iota(shape, dim):
    return lax.broadcasted_iota(jnp.int32, shape, dim)


def compact_matrix(rows):
    r, k = iota((rows, PADDED), 0), iota((rows, PADDED), 1)
    return jnp.where(((k >> 4) * CAP + (k & 15) == r) & ((k & 15) < CAP), 1.0, 0.0).astype(BF16)


def place_of(block):
    away = ((block >> 1) + 8 - (lax.axis_index("expert") >> 1)) & 7
    return jnp.where(away > 4, 2 * (8 - away), jnp.maximum(2 * away - 1, 0)) * 2 + (block & 1)


def placed_matrix():
    r, k = iota((ROWS, PADDED), 0), iota((ROWS, PADDED), 1)
    return jnp.where((place_of(k >> 4) * CAP + (k & 15) == r) & ((k & 15) < CAP), 1.0, 0.0).astype(BF16)


def same_row(which):
    k, m = iota((PADDED, PADDED), 0), iota((PADDED, PADDED), 1)
    return jnp.where(m == (k >> 4) * PAD + CAP + which, 1.0, 0.0).astype(BF16)


def extra_row(which):
    b, k = iota((EXPERTS, PADDED), 0), iota((EXPERTS, PADDED), 1)
    return jnp.where(k == b * PAD + CAP + which, 1.0, 0.0).astype(BF16)


def lane_spread():
    c, k = iota((LANES, PADDED), 0), iota((LANES, PADDED), 1)
    return jnp.where((k & 15) == c, 1.0, 0.0).astype(BF16)


def block_of_row(placed=True):
    r, b = iota((ROWS, EXPERTS), 0), iota((ROWS, EXPERTS), 1)
    if not placed:
        b = place_of(b)
    return jnp.where((r >= b * CAP) & (r < b * CAP + CAP), 1.0, 0.0).astype(BF16)


def slot_of_row():
    return dot_t(compact_matrix(ROWS), lane_spread())


def parts(value):
    out = []
    for _ in range(3):
        part = value.astype(BF16)
        value = value - part.astype(F32)
        out.append(part)
    return out


def dot(a, b):
    return jnp.dot(a, b, preferred_element_type=F32)


def dot_t(a, b):
    return lax.dot_general(a, b, (((1,), (1,)), ((), ())), preferred_element_type=F32)


def t_dot(a, b):
    return lax.dot_general(a, b, (((0,), (0,)), ((), ())), preferred_element_type=F32)


def position():
    return lax.axis_index("dp"), lax.axis_index("expert"), lax.axis_index("etp")


def copy_to(src, dst, send_sem, recv_sem, device):
    return pltpu.make_async_remote_copy(
        src_ref=src, dst_ref=dst, send_sem=send_sem, recv_sem=recv_sem, device_id=device, device_id_type=MESH
    )


def piece(ref, i, j):
    return ref.at[i, :, pl.ds(pl.multiple_of(j * COLS, COLS), COLS)]


class PlaneGather:
    COUNT = 26

    def __init__(self, ref, start, width, dp_first, send_sems, recv_sems):
        x, e, y = position()
        self.ref, self.dp_first, self.send_sems, self.recv_sems = ref, dp_first, send_sems, recv_sems
        self.start, self.width = start, width
        self.e = e
        self.a, self.b = (x, y) if dp_first else (y, x)
        self.sent = []

    def at(self, i, j, half=None):
        i, j = i % 4, j % 4
        if not self.dp_first:
            i, j = j, i
        columns = pl.ds(pl.multiple_of(j * PART + self.start, LANES), self.width)
        if half is None:
            return self.ref.at[i, :, columns]
        return self.ref.at[i, pl.ds(half * (ROWS // 2), ROWS // 2), columns]

    def device(self, i, j):
        i, j = i % 4, j % 4
        return (i, self.e, j) if self.dp_first else (j, self.e, i)

    def copy(self, view, index, device):
        return copy_to(view, view, self.send_sems.at[index], self.recv_sems.at[index], device)

    def send(self, view, index, device):
        c = self.copy(view, index, device)
        c.start()
        self.sent.append(c)

    def wait(self, view, index):
        self.copy(view, index, self.device(self.a, self.b)).wait_recv()

    def own(self, half):
        a, b = self.a, self.b
        view = self.at(a, b, half)
        self.send(view, 22 * half, self.device(a + 1, b))
        self.send(view, 1 + 22 * half, self.device(a - 1, b))
        self.send(view, 4 + 20 * half, self.device(a, b + 1))
        self.send(view, 5 + 20 * half, self.device(a, b - 1))

    def forward_own(self):
        a, b = self.a, self.b
        self.wait(self.at(a, b - 1, 0), 4)
        self.send(self.at(a, b - 1, 0), 14, self.device(a, b + 1))
        self.wait(self.at(a, b + 1, 1), 25)
        self.send(self.at(a, b + 1, 1), 15, self.device(a, b - 1))
        self.wait(self.at(a, b - 1, 1), 24)
        self.wait(self.at(a, b + 1, 0), 5)

    def both_second(self, i, slot, half=None):
        view = self.at(i, self.b, half)
        self.send(view, 4 + 2 * slot, self.device(self.a, self.b + 1))
        self.send(view, 5 + 2 * slot, self.device(self.a, self.b - 1))

    def forward_second(self, i, slot):
        self.wait(self.at(i, self.b - 1), 4 + 2 * slot)
        self.send(self.at(i, self.b - 1, 0), 14 + 2 * slot, self.device(self.a, self.b + 1))
        self.wait(self.at(i, self.b + 1), 5 + 2 * slot)
        self.send(self.at(i, self.b + 1, 1), 15 + 2 * slot, self.device(self.a, self.b - 1))

    def steps(self):
        a, b = self.a, self.b

        def lower():
            self.wait(self.at(a - 1, b, 0), 0)
            self.send(self.at(a - 1, b, 0), 2, self.device(a + 1, b))
            self.wait(self.at(a - 1, b, 1), 22)
            self.both_second(a - 1, 1)

        def upper():
            self.wait(self.at(a + 1, b, 1), 23)
            self.send(self.at(a + 1, b, 1), 3, self.device(a - 1, b))
            self.wait(self.at(a + 1, b, 0), 1)
            self.both_second(a + 1, 2)

        def opposite():
            self.wait(self.at(a + 2, b, 0), 2)
            self.both_second(a + 2, 3, 0)
            self.wait(self.at(a + 2, b, 1), 3)
            self.both_second(a + 2, 4, 1)

        def opposite_second():
            self.wait(self.at(a + 2, b - 1, 0), 10)
            self.send(self.at(a + 2, b - 1, 0), 20, self.device(a, b + 1))
            self.wait(self.at(a + 2, b + 1, 1), 13)
            self.send(self.at(a + 2, b + 1, 1), 21, self.device(a, b - 1))

        return [
            None,
            lower,
            upper,
            self.forward_own,
            opposite,
            lambda: self.forward_second(a - 1, 1),
            lambda: self.forward_second(a + 1, 2),
            opposite_second,
        ]

    def finish_near(self):
        a, b = self.a, self.b
        self.wait(self.at(a + 2, b + 1, 0), 11)
        self.wait(self.at(a + 2, b - 1, 1), 12)

    def finish_far(self, slot):
        i = self.a + (0, -1, 1, 2)[slot]
        self.wait(self.at(i, self.b + 2, 0), 14 + 2 * slot)
        self.wait(self.at(i, self.b + 2, 1), 15 + 2 * slot)


class PlaneReduce:
    HALF = ROWS // 2
    QUARTER = ROWS // 4
    COUNT = 20

    def __init__(self, ref, out, low, dp_first, order, opp, full, opp2, full2, send_sems, recv_sems):
        x, e, y = position()
        self.ref, self.out, self.low, self.dp_first, self.order = ref, out, low, dp_first, order
        self.opp, self.full, self.opp2, self.full2 = opp, full, opp2, full2
        self.send_sems, self.recv_sems = send_sems, recv_sems
        self.e = e
        self.a, self.b = (x, y) if dp_first else (y, x)
        self.sent = []

    def device(self, i, j):
        i, j = i % 4, j % 4
        return (i, self.e, j) if self.dp_first else (j, self.e, i)

    def at(self, i, j, start, size, ref=None):
        i, j = i % 4, j % 4
        ref = self.out if ref is None else ref
        view = piece(ref, i, j) if self.dp_first else piece(ref, j, i)
        return view.at[pl.ds(self.low + start, size), :]

    def send(self, src, dst, index, device):
        c = copy_to(src, dst, self.send_sems.at[index], self.recv_sems.at[index], device)
        c.start()
        self.sent.append(c)

    def wait(self, dst, index):
        copy_to(dst, dst, self.send_sems.at[index], self.recv_sems.at[index], self.device(self.a, self.b)).wait_recv()

    def opposite(self, k):
        a, b, q = self.a, self.b, self.QUARTER
        j = b + self.order[k]
        self.send(self.at(a + 2, j, 0, q), self.opp.at[0, k], 4 * k, self.device(a + 1, b))
        self.send(self.at(a + 2, j, q, q), self.opp.at[1, k], 4 * k + 1, self.device(a - 1, b))

    def near(self, k, sides=(0, 1)):
        a, b, q, h = self.a, self.b, self.QUARTER, self.HALF
        j = b + self.order[k]
        for side in sides:
            to = a + 1 if side == 0 else a - 1
            self.wait(self.opp.at[side, k], 4 * k + side)
            own = self.at(to, j, side * q, q, self.ref)[...]
            self.at(to, j, side * q, q)[...] = (own + self.opp[side, k].astype(F32)).astype(BF16)
            self.send(self.at(to, j, 0, h), self.full.at[side, k], 4 * k + 2 + side, self.device(to, b))

    def total(self, relative):
        k = self.order.index(relative)
        for side in range(2):
            self.wait(self.full.at[side, k], 4 * k + 2 + side)
        own = self.at(self.a, self.b + relative, 0, self.HALF, self.ref)[...]
        return own + self.full[0, k].astype(F32) + self.full[1, k].astype(F32)

    def second_opposite(self):
        a, b, q, h = self.a, self.b, self.QUARTER, self.HALF
        self.at(a, b + 2, 0, h)[...] = self.total(2).astype(BF16)
        self.send(self.at(a, b + 2, 0, q), self.opp2.at[0], 16, self.device(a, b + 1))
        self.send(self.at(a, b + 2, q, q), self.opp2.at[1], 17, self.device(a, b - 1))

    def second_near(self, side):
        a, b, q, h = self.a, self.b, self.QUARTER, self.HALF
        step = 1 if side == 0 else -1
        value = self.total(step)
        self.wait(self.opp2.at[side], 16 + side)
        extra = self.opp2[side].astype(F32)
        if side == 0:
            value = jnp.concatenate([value[:q] + extra, value[q:]], axis=0)
        else:
            value = jnp.concatenate([value[:q], value[q:] + extra], axis=0)
        self.at(a, b + step, 0, h)[...] = value.astype(BF16)
        self.send(self.at(a, b + step, 0, h), self.full2.at[side], 18 + side, self.device(a, b + step))

    def finish(self):
        value = self.total(0)
        for side in range(2):
            self.wait(self.full2.at[side], 18 + side)
        return value + self.full2[0].astype(F32) + self.full2[1].astype(F32)


class Ring:
    def __init__(self, block, z_send, z_recv, core_send, core_recv):
        self.x, self.e, self.y = position()
        self.block = block
        self.z_send, self.z_recv, self.core_send, self.core_recv = z_send, z_recv, core_send, core_recv
        self.other = self.e + 1 - 2 * (self.e % 2)
        self.sent = []

    def copy(self, src, dst, send, recv, device):
        c = copy_to(src, dst, send, recv, device)
        c.start()
        self.sent.append(c)

    def view(self, e, side, distance):
        away = 2 * distance
        return self.block((e + (EXPERTS - away if side == 0 else away)) % EXPERTS, side if distance == 4 else None)

    def onward(self, side, distance):
        e = self.e
        view = self.view(e, side, distance)
        if distance > 0:
            copy_to(
                view, view, self.z_send.at[side, distance], self.z_recv.at[side, distance], (self.x, e, self.y)
            ).wait_recv()
        if distance < 4:
            to = (e + (2 if side == 0 else EXPERTS - 2)) % EXPERTS
            next_view = self.view(to, side, distance + 1)
            self.copy(
                next_view, next_view,
                self.z_send.at[side, distance + 1], self.z_recv.at[side, distance + 1], (self.x, to, self.y),
            )
        if distance > 0 or side == 0:
            self.copy(
                view, view, self.core_send.at[side, distance], self.core_recv.at[side, distance],
                (self.x, self.other, self.y),
            )

    def round(self, distance):
        for side in range(2):
            self.onward(side, distance)

    NEAR = ((0, 0), (0, 1), (1, 1), (1, 2))
    FAR = ((0, 2), (0, 3), (1, 3), (0, 4), (1, 4))

    def finish(self, which):
        for side, distance in which:
            view = self.view(self.other, side, distance)
            copy_to(
                view, view, self.core_send.at[side, distance], self.core_recv.at[side, distance],
                (self.x, self.e, self.y),
            ).wait_recv()


def kernel(
    tokens, out_grad, gates, expert_ids, w_gate, w_up, w_down,
    input_grad, gate_grad, grad_gate, grad_up, grad_down,
    near, table_out, table_in, rows, grads, tables, whole, w_in, w_out, pre, raw, deltas, scaled, turned, turned_scaled,
    sums, wire, made, terms, landed_x, landed_y,
    opp_a, full_a, opp2_a, full2_a, opp_b, full_b, opp2_b, full2_b, back, ready,
    slot_send, slot_recv, x_send, x_recv, d_send, d_recv, g_send, g_recv,
    dp_send, dp_recv, z_sems,
    send_a, recv_a, send_b, recv_b, t_send, t_recv, r_send, r_recv, local,
):
    x, e, y = position()
    peers = [(x, (e + j) % EXPERTS, y) for j in range(1, EXPERTS)]
    peers += [((x + j) % N_DP, e, y) for j in range(1, N_DP)]
    peers += [(x, e, (y + j) % N_ETP) for j in range(1, N_ETP)]
    barrier = pltpu.get_barrier_semaphore()
    for device in peers:
        pl.semaphore_signal(barrier, inc=1, device_id=device, device_id_type=MESH)
    columns = pl.ds(pl.multiple_of(y * PART, LANES), PART)
    late = pl.ds(SLOTTED, WHOLE)

    def token_rows(place, half=None):
        if half is None:
            return pl.ds(pl.multiple_of(place * TOK, TOK), TOK)
        return pl.ds(pl.multiple_of(place * TOK + half * (TOK // 2), TOK // 2), TOK // 2)

    def whole_block(place, half=None):
        return whole.at[:, token_rows(place), :] if half is None else whole.at[pl.ds(2 * half, 2), token_rows(place), :]

    def whole_landing(i, which):
        return whole.at[i, token_rows(e), pl.ds(which * WHOLE, WHOLE)]

    ring_x = Ring(lambda p, half=None: near.at[token_rows(p, half), pl.ds(0, PART)], *[z_sems.at[k] for k in range(4)])
    ring_d = Ring(lambda p, half=None: near.at[token_rows(p, half), pl.ds(PART, PART)], *[z_sems.at[k] for k in range(4, 8)])
    ring_w = Ring(whole_block, *[z_sems.at[k] for k in range(8, 12)])

    loads = [
        pltpu.make_async_copy(tokens.at[:, columns], ring_x.block(e), local.at[0]),
        pltpu.make_async_copy(out_grad.at[:, columns], ring_d.block(e), local.at[1]),
        pltpu.make_async_copy(w_gate.at[0], w_in.at[pl.ds(0, FF), :], local.at[2]),
        pltpu.make_async_copy(w_up.at[0], w_in.at[pl.ds(FPAD, FF), :], local.at[3]),
        pltpu.make_async_copy(w_down.at[0], w_out.at[pl.ds(0, FF), :], local.at[4]),
    ]
    own_whole = [
        pltpu.make_async_copy(s.at[:, late], whole_landing(x, which), local.at[8 + which])
        for which, s in enumerate((tokens, out_grad))
    ]
    for c in loads[:2] + own_whole + loads[2:]:
        c.start()
    expert, place = iota((PADDED, TOK), 0) >> 4, iota((PADDED, TOK), 0) & 15
    ids, weight = expert_ids[...], gates[...].astype(F32)
    chosen = [jnp.where(ids[k : k + 1, :] == expert, 1.0, 0.0) for k in range(TOP)]
    member = chosen[0] + chosen[1] + chosen[2] + chosen[3]
    before = jnp.where(iota((TOK, TOK), 0) < iota((TOK, TOK), 1), 1.0, 0.0).astype(BF16)
    earlier = dot(member.astype(BF16), before)
    table = jnp.where((earlier == place.astype(F32)) & (place < CAP), member, 0.0)
    gate_slots = sum(chosen[k] * weight[k : k + 1, :] for k in range(TOP)) * table
    gate_slots = jnp.sum(gate_slots, axis=1, keepdims=True)
    table = table.astype(BF16)
    widen = jnp.where(iota((TOK, LANES), 0) == iota((TOK, LANES), 1), 1.0, 0.0).astype(BF16)
    sent = []

    wide = jnp.where(iota((PADDED, LANES), 1) == TOK, gate_slots, dot(table, widen))
    table_out[...] = wide.astype(BF16).reshape(EXPERTS, PAD, LANES)
    loads[0].wait()
    loads[1].wait()
    pl.semaphore_wait(barrier, len(peers))

    ring_x.round(0)
    ring_d.round(0)
    for j in range(1, EXPERTS):
        to = (e + j) % EXPERTS
        c = copy_to(table_out.at[to], table_in.at[e], slot_send.at[j], slot_recv.at[j], (x, to, y))
        c.start()
        sent.append(c)
    for j in range(1, N_DP):
        for which, source in enumerate((tokens, out_grad)):
            c = copy_to(
                source.at[:, late], whole_landing(x, which),
                dp_send.at[which, j], dp_recv.at[which, j], ((x + j) % N_DP, e, y),
            )
            c.start()
            sent.append(c)
    table_in[e] = table_out[e]
    for ref, low in ((w_in, FF), (w_in, FPAD + FF), (w_out, FF)):
        ref[pl.ds(low, FPAD - FF), :] = jnp.zeros((FPAD - FF, D), BF16)

    gather_x = PlaneGather(rows, 0, PART, True, x_send, x_recv)
    gather_d = PlaneGather(grads, 0, PART, False, d_send, d_recv)
    steps_x, steps_d = gather_x.steps(), gather_d.steps()

    def pick(g):
        repeat = jnp.where(iota((LANES, EXPERTS * TOK), 0) == (iota((LANES, EXPERTS * TOK), 1) & 31), 1.0, 0.0)
        within = jnp.where(iota((EXPERTS, EXPERTS * TOK), 0) == (iota((EXPERTS, EXPERTS * TOK), 1) >> 5), 1.0, 0.0)
        return (dot(tables[g], repeat.astype(BF16)) * dot(block_of_row(False), within.astype(BF16))).astype(BF16)

    def run(*which):
        for k in which:
            steps_x[k]()
            steps_d[k]()

    half = ROWS // 2

    def own_half(ref, start, h):
        r, m = iota((half, EXPERTS // 2 * TOK), 0), iota((half, EXPERTS // 2 * TOK), 1)
        within = (r >= (m >> 5) * CAP) & (r < (m >> 5) * CAP + CAP)
        lane, m = iota((LANES, EXPERTS // 2 * TOK), 0), iota((LANES, EXPERTS // 2 * TOK), 1)
        repeat = jnp.where(lane == (m & 31), 1.0, 0.0).astype(BF16)
        own = pl.ds(h * half, half)
        picker = jnp.where(within, dot(tables[x, own, :], repeat), 0.0).astype(BF16)
        taken = []
        for away in ((0, 1, 7, 2), (6, 3, 5, 4))[h]:
            low = pl.multiple_of((((e // 2) + away) % 8) * (2 * TOK), 2 * TOK)
            taken.append(near[pl.ds(low, 2 * TOK), start : start + PART])
        ref[x, own, columns] = dot(picker, jnp.concatenate(taken, axis=0)).astype(BF16)

    for k in range(1, 3):
        ring_x.round(k)
        ring_d.round(k)
    for j in range(1, EXPERTS):
        view = table_in.at[(e + EXPERTS - j) % EXPERTS]
        copy_to(view, view, slot_send.at[j], slot_recv.at[j], (x, e, y)).wait_recv()
    tables[x] = dot(placed_matrix(), table_in[...].reshape(PADDED, LANES)).astype(BF16)
    for j in range(1, N_DP):
        c = copy_to(tables.at[x], tables.at[x], g_send.at[j], g_recv.at[j], ((x + j) % N_DP, e, y))
        c.start()
        sent.append(c)
    ring_x.finish(Ring.NEAR)
    own_half(rows, 0, 0)
    gather_x.own(0)
    ring_x.round(3)
    ring_d.round(3)
    ring_d.finish(Ring.NEAR)
    own_half(grads, PART, 0)
    gather_d.own(0)
    ring_x.round(4)
    ring_d.round(4)
    ring_x.finish(Ring.FAR)
    own_half(rows, 0, 1)
    gather_x.own(1)
    ring_d.finish(Ring.FAR)
    own_half(grads, PART, 1)
    gather_d.own(1)
    for c in own_whole:
        c.wait()
    for j in range(1, N_DP):
        for which in range(2):
            view = whole_landing((x + N_DP - j) % N_DP, which)
            copy_to(view, view, dp_send.at[which, j], dp_recv.at[which, j], (x, e, y)).wait_recv()
    ring_w.round(0)

    reduce_a = PlaneReduce(
        sums, wire, 0, True, (2, 1, -1, 0), opp_a, full_a, opp2_a, full2_a, send_a, recv_a
    )
    reduce_b = PlaneReduce(
        sums, wire, ROWS // 2, False, (2, 1, -1, 0), opp_b, full_b, opp2_b, full2_b, send_b, recv_b
    )
    group = [(x + j) % N_DP for j in (0, 3, 1, 2)]

    def add_x(i, j):
        part = pl.ds(pl.multiple_of((j % N_ETP) * PART, LANES), PART)
        pre[i % N_DP] += dot_t(rows[i % N_DP, :, part], w_in[:, part])

    def add_d(i, j):
        part = pl.ds(pl.multiple_of((j % N_ETP) * PART, LANES), PART)
        raw[i % N_DP] += dot_t(grads[i % N_DP, :, part], w_out[:, part])

    def add_sides(move):
        @pl.loop(0, 2)
        def _(k):
            add_x(x + N_DP + move, y + 3 + 2 * k)
            add_d(x + 3 + 2 * k, y + N_ETP + move)

    def add_far(slot):
        gather_x.finish_far(slot)
        gather_d.finish_far(slot)
        move = (0, 3, 1, 2)[slot]
        add_x(x + move, y + 2)
        add_d(x + 2, y + move)

    def add_tokens(low, high):
        @pl.loop(low, high)
        def _(k):
            g = (x + k) % N_DP
            picked = dot(pick(g), whole[g]).astype(BF16)
            rows[g, :, SLOTTED:] = picked[:, :WHOLE]
            grads[g, :, SLOTTED:] = picked[:, WHOLE:]
            pre[g] += dot_t(picked[:, :WHOLE], w_in[:, SLOTTED:])
            raw[g] += dot_t(picked[:, WHOLE:], w_out[:, SLOTTED:])

    def backward(slot, send=None):
        g = group[slot]
        a, u, r = pre[g, :, :FPAD], pre[g, :, FPAD:], raw[g]
        which = slot_of_row()
        scale = tables[g, :, TOK : TOK + 1].astype(F32)
        sigmoid = jax.nn.sigmoid(a)
        activated = a * sigmoid
        product = activated * u
        q = jnp.sum(product * r, axis=1, keepdims=True) * which
        terms[g] = sum(t_dot(block_of_row(), part) for part in parts(q))
        own = pl.ds(pl.multiple_of(g * ROWS, ROWS), ROWS)
        scaled[own, :] = (scale * product).astype(BF16)
        hidden = scale * r
        deltas[own, :FPAD] = (hidden * u * sigmoid * (1.0 + a * (1.0 - sigmoid))).astype(BF16)
        deltas[own, FPAD:] = (hidden * activated).astype(BF16)

        def columns_of(k):
            part = pl.ds(pl.multiple_of(k * COLS, COLS), COLS)
            value = dot(deltas[own, :], w_in[:, part])
            sums[g, :, part] = value
            wire[g, :, part] = value.astype(BF16)

        if send is None:
            pl.loop(0, N_ETP)(columns_of)
            return
        for k in range(N_ETP):
            columns_of((y + N_ETP + reduce_a.order[k]) % N_ETP)
            send(k)

    def weight_grad(which):
        source = (rows, rows, grads)[which]

        @pl.loop(0, N_ETP)
        def _(k):
            part = pl.ds(pl.multiple_of(k * COLS, COLS), COLS)
            left = turned_scaled[:FF, :] if which == 2 else turned[pl.ds(which * FPAD, FF), :]
            made[which, :, part] = dot(left, source[:, :, part].reshape(N_DP * ROWS, COLS)).astype(BF16)

        c = pltpu.make_async_copy(made.at[which], (grad_gate, grad_up, grad_down)[which].at[0], local.at[5 + which])
        c.start()
        loads.append(c)

    pre[...] = jnp.zeros_like(pre)
    raw[...] = jnp.zeros_like(raw)
    for c in loads[2:]:
        c.wait()
    add_x(x, y)
    add_d(x, y)
    run(1, 2)
    ring_w.round(1)

    @pl.loop(0, 2)
    def _(k):
        add_x(x + 3 + 2 * k, y)
        add_d(x, y + 3 + 2 * k)

    run(3)
    add_sides(0)
    run(4)
    ring_w.round(2)
    add_x(x + 2, y)
    add_d(x, y + 2)
    run(5)
    ring_w.round(3)
    add_sides(-1)
    run(6)
    ring_w.round(4)
    add_sides(1)
    run(7)
    for j in range(1, N_DP):
        g = (x + N_DP - j) % N_DP
        copy_to(tables.at[g], tables.at[g], g_send.at[j], g_recv.at[j], (x, e, y)).wait_recv()
    gather_x.finish_near()
    gather_d.finish_near()
    add_sides(2)
    ring_w.finish(Ring.NEAR + Ring.FAR)
    add_tokens(0, 4)
    for slot in range(4):
        add_far(slot)

    def send_opposite(k):
        reduce_a.opposite(k)
        if k == 0:
            reduce_b.opposite(0)

    backward(3, send_opposite)
    backward(2)
    reduce_b.opposite(1)
    reduce_b.near(0)
    reduce_a.near(0, (0,))
    reduce_a.near(1, (0,))
    backward(1)
    reduce_b.opposite(2)
    reduce_a.near(0, (1,))
    reduce_a.near(1, (1,))
    reduce_b.near(1)
    reduce_a.near(2)
    backward(0)
    reduce_b.opposite(3)
    reduce_b.near(2)
    for j in range(1, N_DP):
        to = (x + j) % N_DP
        c = copy_to(terms.at[to], landed_x.at[j], t_send.at[j], t_recv.at[j], (to, e, y))
        c.start()
        sent.append(c)
    turned[...] = deltas[...].T
    turned_scaled[...] = scaled[...].T
    reduce_a.second_opposite()
    reduce_b.second_opposite()
    total = terms[x]
    for j in range(1, N_DP):
        copy_to(landed_x.at[j], landed_x.at[j], t_send.at[j], t_recv.at[j], (x, e, y)).wait_recv()
        total = total + landed_x[j]
    landed_y[0] = total
    for j in range(1, N_ETP):
        c = copy_to(landed_y.at[0], landed_y.at[j], t_send.at[3 + j], t_recv.at[3 + j], (x, e, (y + j) % N_ETP))
        c.start()
        sent.append(c)
    reduce_a.second_near(0)
    reduce_b.second_near(0)
    reduce_a.near(3)
    reduce_b.near(3)
    weight_grad(0)
    reduce_a.second_near(1)
    reduce_b.second_near(1)
    for j in range(1, N_ETP):
        copy_to(landed_y.at[j], landed_y.at[j], t_send.at[3 + j], t_recv.at[3 + j], (x, e, y)).wait_recv()
        total = total + landed_y[j]
    spare = sum(t_dot(extra_row(which), part) for which, part in enumerate(parts(total)))
    r, k = iota((half, PADDED // 2), 0), iota((half, PADDED // 2), 1)
    spread = jnp.where(((k >> 4) * CAP + (k & 15) == r) & ((k & 15) < CAP), 1.0, 0.0).astype(BF16)
    core = e % 2
    for h, reduce in ((1, reduce_b), (0, reduce_a)):
        padded = t_dot(spread, reduce.finish().astype(BF16))
        own = pl.ds(h * (EXPERTS // 2), EXPERTS // 2)
        extra = spare[h * (PADDED // 2) : (h + 1) * (PADDED // 2)]
        ready[own, :, :LANES] = (padded[:, :LANES] + extra).astype(BF16).reshape(EXPERTS // 2, PAD, LANES)
        ready[own, :, LANES:] = padded[:, LANES:].astype(BF16).reshape(EXPERTS // 2, PAD, COLS - LANES)
        for k in range(3, -1, -1):
            away = ((0, 1, 7, 2), (6, 3, 5, 4))[h][k]
            for flip in range(2):
                to_core = core if flip == 0 else 1 - core
                source = ready.at[8 * h + 2 * k + to_core]
                if away == 0 and flip == 0:
                    back[e] = source[...]
                    continue
                to = ((e // 2 + away) % 8) * 2 + to_core
                c = copy_to(source, back.at[e], r_send.at[away, flip], r_recv.at[away, flip], (x, to, y))
                c.start()
                sent.append(c)
    weight_grad(1)
    weight_grad(2)
    for away in range(8):
        for flip in range(2):
            if away > 0 or flip > 0:
                frm = ((e // 2 + 8 - away) % 8) * 2 + (core if flip == 0 else 1 - core)
                copy_to(
                    back.at[frm], back.at[frm], r_send.at[away, flip], r_recv.at[away, flip], (x, e, y)
                ).wait_recv()
    block = back[...].reshape(PADDED, COLS)
    input_grad[...] = t_dot(table, block).astype(BF16)
    lanes = block[:, :LANES]
    mine = jnp.where(iota((PADDED, LANES), 1) == (iota((PADDED, LANES), 0) & 15), 1.0, 0.0)
    value = sum(dot(same_row(which), lanes) for which in range(3))
    value = jnp.sum(value * mine, axis=1, keepdims=True) * table.astype(F32)
    pairs = jnp.concatenate([jnp.sum(chosen[k] * value, axis=0, keepdims=True) for k in range(TOP)], axis=0)
    share = TOK // N_ETP
    take = jnp.where(iota((TOK, share), 0) == iota((TOK, share), 1) + y * share, 1.0, 0.0).astype(BF16)
    gate_grad[...] = sum(dot(part, take) for part in parts(pairs))
    for c in loads[5:]:
        c.wait()
    for c in sent + gather_x.sent + gather_d.sent + reduce_a.sent + reduce_b.sent:
        c.wait_send()
    for ring in (ring_x, ring_d, ring_w):
        for c in ring.sent:
            c.wait_send()


def copy_out(*refs):
    count = (len(refs) - 2) // 3
    sources, targets, held = refs[:count], refs[count : 2 * count], refs[2 * count : 3 * count]
    into, out = refs[3 * count :]
    steps = []
    for source, target, place in zip(sources, targets, held):
        if len(source.shape) < 3:
            steps.append((source, place, target))
            continue
        for low, size in ((0, 96), (96, 80), (176, 80), (256, 80)):
            view = (0, pl.ds(low, size), slice(None))
            steps.append((source.at[view], place.at[view], target.at[view]))
    steps = steps[::-1]
    first = [pltpu.make_async_copy(source, place, into.at[k]) for k, (source, place, _) in enumerate(steps)]
    second = [pltpu.make_async_copy(place, target, out.at[k]) for k, (_, place, target) in enumerate(steps)]
    for c in first:
        c.start()
    for one, two in zip(first, second):
        one.wait()
        two.start()
    for c in second:
        c.wait()


def per_device(tokens, out_grad, gates, expert_ids, w_gate, w_up, w_down):
    dma = pltpu.SemaphoreType.DMA
    vmem = pl.BlockSpec(memory_space=pltpu.VMEM)
    hbm = pl.BlockSpec(memory_space=pl.ANY)
    count = tokens.shape[0]
    half, quarter = ROWS // 2, ROWS // 4
    landing = [
        pltpu.VMEM((2, 4, quarter, COLS), BF16),
        pltpu.VMEM((2, 4, half, COLS), BF16),
        pltpu.VMEM((2, quarter, COLS), BF16),
        pltpu.VMEM((2, half, COLS), BF16),
    ]
    all_rows = N_DP * ROWS
    weight = jax.ShapeDtypeStruct(w_gate.shape, BF16)
    results = pl.pallas_call(
        kernel,
        out_shape=(
            jax.ShapeDtypeStruct((count, COLS), BF16),
            jax.ShapeDtypeStruct((TOP, count // N_ETP), F32),
            weight,
            weight,
            weight,
        ),
        in_specs=[hbm, hbm, vmem, vmem, hbm, hbm, hbm],
        out_specs=(vmem, vmem, hbm, hbm, hbm),
        scratch_shapes=[
            pltpu.VMEM((EXPERTS * TOK, 2 * PART), BF16),
            pltpu.VMEM((EXPERTS, PAD, LANES), BF16),
            pltpu.VMEM((EXPERTS, PAD, LANES), BF16),
            pltpu.VMEM((N_DP, ROWS, D), BF16),
            pltpu.VMEM((N_DP, ROWS, D), BF16),
            pltpu.VMEM((N_DP, ROWS, LANES), BF16),
            pltpu.VMEM((N_DP, EXPERTS * TOK, 2 * WHOLE), BF16),
            pltpu.VMEM((2 * FPAD, D), BF16),
            pltpu.VMEM((FPAD, D), BF16),
            pltpu.VMEM((N_DP, ROWS, 2 * FPAD), F32),
            pltpu.VMEM((N_DP, ROWS, FPAD), F32),
            pltpu.VMEM((all_rows, 2 * FPAD), BF16),
            pltpu.VMEM((all_rows, FPAD), BF16),
            pltpu.VMEM((2 * FPAD, all_rows), BF16),
            pltpu.VMEM((FPAD, all_rows), BF16),
            pltpu.VMEM((N_DP, ROWS, D), F32),
            pltpu.VMEM((N_DP, ROWS, D), BF16),
            pltpu.VMEM((3, FF, D), BF16),
            pltpu.VMEM((N_DP, EXPERTS, LANES), F32),
            pltpu.VMEM((N_DP, EXPERTS, LANES), F32),
            pltpu.VMEM((N_ETP, EXPERTS, LANES), F32),
            *landing,
            *landing,
            pltpu.VMEM((EXPERTS, PAD, COLS), BF16),
            pltpu.VMEM((EXPERTS, PAD, COLS), BF16),
            dma((EXPERTS,)),
            dma((EXPERTS,)),
            *[dma((PlaneGather.COUNT,))] * 4,
            dma((N_DP,)),
            dma((N_DP,)),
            *[dma((2, N_DP))] * 2,
            dma((12, 2, 5)),
            *[dma((PlaneReduce.COUNT,))] * 4,
            dma((8,)),
            dma((8,)),
            dma((8, 2)),
            dma((8, 2)),
            dma((10,)),
        ],
        compiler_params=pltpu.CompilerParams(collective_id=0, has_side_effects=True, vmem_limit_bytes=58 << 20),
        name="backward",
    )(tokens, out_grad, gates.T, expert_ids.T, w_gate, w_up, w_down)
    input_grad, gate_grad, *weight_grads = pl.pallas_call(
        copy_out,
        out_shape=tuple(jax.ShapeDtypeStruct(r.shape, r.dtype) for r in results),
        in_specs=[hbm] * 5,
        out_specs=(hbm,) * 5,
        scratch_shapes=[*[pltpu.VMEM(r.shape, r.dtype) for r in results], dma((16,)), dma((16,))],
        compiler_params=pltpu.CompilerParams(vmem_limit_bytes=58 << 20),
        name="outputs",
    )(*results)
    return input_grad, gate_grad.T, *weight_grads


def solution(mesh):
    in_specs = (
        P(("dp", "expert"), None),
        P(("dp", "expert"), None),
        P(("dp", "expert"), None),
        P(("dp", "expert"), None),
        P("expert", ("dp", "etp"), None),
        P("expert", ("dp", "etp"), None),
        P("expert", ("dp", "etp"), None),
    )
    out_specs = (
        P(("dp", "expert"), "etp"),
        P(("dp", "expert", "etp"), None),
        P("expert", ("dp", "etp"), None),
        P("expert", ("dp", "etp"), None),
        P("expert", ("dp", "etp"), None),
    )
    return jax.shard_map(
        per_device, mesh=mesh, in_specs=in_specs, out_specs=out_specs, check_vma=False
    )
```
